32 devices in a mesh: wide: 16 (over z, x, core), narrow: 2 (over y).
Axes of the slice: x: 2, y: 2, z: 4, core: 2. Of those that a mesh axis runs over, the one named last changes fastest.
Arguments:
- patches: bfloat16 [128, 324, 512], P(('wide', 'narrow')), may hold values from -6 to 6
- cotangent: bfloat16 [128, 324, 512], P(('wide', 'narrow')), may hold values from -6 to 6
- size_class: int32 [128], P(('wide', 'narrow')), may hold values from 0 to 2
- w_in: bfloat16 [2, 1572864], P(None, ('wide', 'narrow')), may hold values from -0.25 to 0.25
- w_out: bfloat16 [2, 786432], P(None, ('wide', 'narrow')), may hold values from -0.15625 to 0.15625
- spatial: bfloat16 [2, 105312], P(None, ('wide', 'narrow')), as said below
- vectors: bfloat16 [2, 7680], P(None, ('wide', 'narrow')), as said below
Outputs:
- outputs: float32 [128, 324, 512], P(('wide', 'narrow'))
- patch_grad: float32 [128, 324, 512], P(('wide', 'narrow'))
- grad_w_in: float32 [2, 1572864], P(None, ('wide', 'narrow'))
- grad_w_out: float32 [2, 786432], P(None, ('wide', 'narrow'))
- grad_spatial: float32 [2, 105312], P(None, ('wide', 'narrow'))
- grad_vectors: float32 [2, 7680], P(None, ('wide', 'narrow'))
The draws below stay inside these ranges and needn't reach their ends.
Inputs may be any that keep to these rules, and one draw needn't show every extreme that they name: `spatial`: entries past the 324 x 324 matrix and 324 bias are never read. Entries past the six vectors are never read.
All inputs are finite; a program needn't handle non-finite values.
Results may differ from the reference program's by a relative error of at most 0.009.
Values may be sent and summed in bfloat16 or wider, within the bound.
No kernel may reach another device: no remote copies, remote signals or barrier semaphores. Data moves between devices by JAX's collectives and lax.ppermute only.
A program may use at most 192 MiB of HBM per device.

```python
import math
import jax
import jax.numpy as jnp
from jax import lax

D = 512
H = 3072
P_SIZE = 324
LAYERS = 2
G = 1536
IMAGES = 128
SFLAT = 105312
VFLAT = 7680


def draw_spatial(key, part):
    key = jax.random.fold_in(key, 7)
    where = lax.broadcasted_iota(jnp.int32, (LAYERS, SFLAT), 1)
    base = jnp.clip(jax.random.normal(key, (LAYERS, SFLAT), jnp.float32), -4.0, 4.0)
    matrix = base * (1.0 / math.sqrt(P_SIZE))
    bias = 1.0 + 0.5 * jnp.clip(base, -1.0, 1.0)
    values = jnp.where(where < P_SIZE * P_SIZE, matrix, jnp.where(where < P_SIZE * P_SIZE + P_SIZE, bias, 0.0))
    return values.astype(jnp.bfloat16)


def draw_vectors(key, part):
    key = jax.random.fold_in(key, 11)
    where = lax.broadcasted_iota(jnp.int32, (LAYERS, VFLAT), 1)
    base = jnp.clip(jax.random.normal(key, (LAYERS, VFLAT), jnp.float32), -3.0, 3.0)
    first_gain = where < D
    second_gain = (where >= 2 * D + H) & (where < 2 * D + H + G)
    gains = 1.0 + 0.25 * base
    shifts = 0.5 * base
    values = jnp.where(first_gain | second_gain, gains, shifts)
    values = jnp.where(where < 3 * D + H + 2 * G, values, 0.0)
    return values.astype(jnp.bfloat16)


def place_ends(entries, stream_key, smallest, largest):
    shape = entries.shape
    spot = [jax.random.randint(jax.random.fold_in(stream_key, axis), (), 0, shape[axis]) for axis in range(len(shape))]
    entries = entries.at[tuple(spot)].set(smallest)
    longest = shape.index(max(shape))
    spot[longest] = (spot[longest] + 1) % shape[longest]
    return entries.at[tuple(spot)].set(largest)


def shard_levels(own_key, extent, cuts, low, largest):
    level = 1.0
    for dim, parts in cuts:
        steps = jax.random.uniform(jax.random.fold_in(jax.random.fold_in(own_key, 6), dim), (parts,), jnp.float32, low / len(cuts), largest / len(cuts))
        level = level * jnp.repeat(jnp.exp(steps), extent[dim] // parts).reshape((-1,) + (1,) * (len(extent) - 1 - dim))
    return level


def noise(stream_key, shape, scale, bound, split=(), kind=jnp.bfloat16):
    factor_of = shard_levels(stream_key, shape, split, -0.22, 0.18) if split else 1.0
    values = jax.random.normal(stream_key, shape, jnp.float32) * scale * factor_of
    return jnp.minimum(jnp.maximum(values, -bound), bound).astype(kind)


def setup_inputs(seed: int = 0) -> dict:
    splits = jax.random.split(jax.random.key(seed), 8)
    return {
        "patches": noise(splits[0], (IMAGES, P_SIZE, D), 1.0, 6.0, ((0, 32),)),
        "cotangent": noise(splits[1], (IMAGES, P_SIZE, D), 1.0, 6.0, ((0, 32),)),
        "size_class": place_ends(jax.random.randint(splits[2], (IMAGES,), 0, 3), jax.random.fold_in(splits[2], 1), 0, 2).astype(jnp.int32),
        "w_in": noise(splits[3], (LAYERS, D * H), D ** -0.5, 0.25, ((1, 32),)),
        "w_out": noise(splits[4], (LAYERS, G * D), G ** -0.5, 0.15625, ((1, 32),)),
        "spatial": draw_spatial(jax.random.fold_in(splits[7], 71), 0),
        "vectors": draw_vectors(jax.random.fold_in(splits[7], 71), 0),
    }


EPS = 1e-05
HIGH = lax.Precision.HIGHEST

@jax.custom_vjp
def low(v):
    return lax.optimization_barrier(v.astype(jnp.bfloat16)).astype(jnp.float32)

@jax.custom_vjp
def low_back(v):
    return v

def low_keep(v):
    return (low(v), None)

def low_pass(kept, grad):
    return (grad,)

def back_keep(v):
    return (v, None)

def back_low(kept, grad):
    return (low(grad),)
low.defvjp(low_keep, low_pass)
low_back.defvjp(back_keep, back_low)

def norm_rows(value, gain, shift):
    mean = lax.optimization_barrier(jnp.mean(value, axis=-1, keepdims=True))
    centred = value - mean
    spread = lax.optimization_barrier(jnp.mean(centred * centred, axis=-1, keepdims=True))
    return centred * lax.rsqrt(spread + EPS) * gain + shift

def layer_forward(resid, gmask, w_in_m, w_out_m, sp_flat, vec):
    ln1_gain = vec[0:D]
    ln1_shift = vec[D:2 * D]
    in_bias = vec[2 * D:2 * D + H]
    ln2_gain = vec[2 * D + H:2 * D + H + G]
    ln2_shift = vec[2 * D + H + G:2 * D + H + 2 * G]
    out_bias = vec[2 * D + H + 2 * G:3 * D + H + 2 * G]
    sp_mat = sp_flat[0:P_SIZE * P_SIZE].reshape(P_SIZE, P_SIZE)
    sp_bias = sp_flat[P_SIZE * P_SIZE:P_SIZE * P_SIZE + P_SIZE]
    normed = low(norm_rows(resid, ln1_gain, ln1_shift))
    pre = low_back(jnp.einsum('bpd,dh->bph', normed, w_in_m, precision=HIGH) + in_bias)
    act = jax.nn.gelu(pre, approximate=True)
    upper = act[..., :G]
    lower = act[..., G:]
    mixed_in = low(norm_rows(lower, ln2_gain, ln2_shift)) * gmask
    mixed = jnp.einsum('ij,bjc->bic', sp_mat, mixed_in, precision=HIGH)
    gate = low_back(gmask * (mixed + sp_bias[None, :, None]))
    gated = low(upper * gate)
    branch = low_back(jnp.einsum('bpc,cd->bpd', gated, w_out_m, precision=HIGH) + out_bias)
    return gmask * (resid + branch)

def group_forward(params, pair):
    w_in_f, w_out_f, spatial_f, vectors_f = params
    resid, gmask = pair
    for layer in range(LAYERS):
        resid = layer_forward(resid, gmask, w_in_f[layer].reshape(D, H), w_out_f[layer].reshape(G, D), spatial_f[layer], vectors_f[layer])
    return resid

def reference(patches, cotangent, size_class, w_in, w_out, spatial, vectors):
    counts = jnp.where(size_class == 0, 100, jnp.where(size_class == 1, 196, 324)).astype(jnp.int32)
    places = jnp.arange(P_SIZE, dtype=jnp.int32)
    mask = (places[None, :] < counts[:, None]).astype(jnp.float32)[:, :, None]
    params = (w_in.astype(jnp.float32), w_out.astype(jnp.float32), spatial.astype(jnp.float32), vectors.astype(jnp.float32))
    checked = jax.checkpoint(group_forward)
    groups = IMAGES // 4

    def forward(params_in, inputs):
        shaped = inputs.reshape(groups, 4, P_SIZE, D)
        masks = mask.reshape(groups, 4, P_SIZE, 1)
        result = lax.map(lambda pair: checked(params_in, pair), (shaped, masks))
        return result.reshape(IMAGES, P_SIZE, D)
    outputs, pull = jax.vjp(forward, params, patches.astype(jnp.float32))
    grads, patch_grad = pull(cotangent.astype(jnp.float32))
    return (outputs, patch_grad, grads[0], grads[1], grads[2], grads[3])
```

```python
import functools
import jax
import jax.numpy as jnp
from jax import lax
from jax.experimental import pallas as pl
from jax.experimental.pallas import tpu as pltpu
from jax.sharding import PartitionSpec as P

D = 512
H = 3072
P_SIZE = 324
LAYERS = 2
G = 1536
EPS = 1e-05
CW = 512
NG = G // CW
NH = H // CW
RMAX = 336
SIZES = ((112, 100), (208, 196), (336, 324))
F32 = jnp.float32
BF16 = jnp.bfloat16
O_LN1G, O_LN1S, O_INB = 0, D, 2 * D
O_LN2G, O_LN2S, O_OUTB = 2 * D + H, 2 * D + H + G, 2 * D + H + 2 * G
VUSED = 3 * D + H + 2 * G
VROWS = VUSED // 128
VPAD = (VROWS + 15) // 16 * 16
GELU_C = 0.7978845608028654
GELU_A = 0.044715
AXES = ("wide", "narrow")
VLIM = 60 * 2**20
PART_FIELDS = {"a": (0, 1, 6), "d": (2, 3, 7), "b": (4, 5, 8, 9)}
PART_DIMS = {"a": ("y", "x", "z"), "d": ("x", "y", "z"), "b": ("z", "y", "x")}
PARTS = ("a", "d", "b")


class Layout:
    def __init__(self, mesh_shape, sp_shard, vec_shard):
        wide, narrow = mesh_shape
        self.size = {"core": 2, "x": 2, "z": wide // 4, "y": narrow}
        self.count = wide * narrow
        self.rows = D // self.count
        self.sp_shard, self.vec_shard = sp_shard, vec_shard
        self.sp_rows = (sp_shard + 2 * P_SIZE - 2) // P_SIZE
        self.vec_rows = (vec_shard + 2 * 128 - 2) // 128
        self.native = self.rows % 16 == 0
        self.small = (self.sp_rows + self.vec_rows + 7) // 8 * 8

    def part_rows(self, part):
        return sum(self.small if f == 9 else self.rows for f in PART_FIELDS[part])

    def offsets(self, part):
        spots, at = [], 0
        for f in PART_FIELDS[part]:
            spots.append((f, at))
            at += self.small if f == 9 else self.rows
        return spots

    def index(self, at):
        return ((at["z"] * 2 + at["x"]) * 2 + at["core"]) * self.size["y"] + at["y"]

    def coords(self, i):
        y, wide = i % self.size["y"], i // self.size["y"]
        return {"core": wide % 2, "x": wide // 2 % 2, "z": wide // 4, "y": y}

    def shift(self, value, axis, step=1):
        pairs = []
        for i in range(self.count):
            at = self.coords(i)
            at[axis] = (at[axis] + step) % self.size[axis]
            pairs.append((i, self.index(at)))
        return lax.ppermute(value, AXES, pairs)


def dot(a, b):
    return lax.dot_general(a, b, (((1,), (0,)), ((), ())), preferred_element_type=F32)


def dot_nt(a, b):
    return lax.dot_general(a, b, (((1,), (1,)), ((), ())), preferred_element_type=F32)


def gelu_both(z, need_grad):
    z2 = z * z
    t = jnp.tanh(z * (GELU_C + (GELU_C * GELU_A) * z2))
    w = 0.5 * t + 0.5
    h = z * w
    if not need_grad:
        return h, None
    return h, w + (h - h * w) * (2.0 * GELU_C + (6.0 * GELU_C * GELU_A) * z2)


def rows_sum8(x):
    rows, cols = x.shape
    return jnp.sum(x.reshape(rows // 8, 8, cols), axis=0)


def picker(lay, rows, cols, first, per, length, width):
    r = lax.broadcasted_iota(jnp.int32, (rows, cols), 0)
    c = lax.broadcasted_iota(jnp.int32, (rows, cols), 1)
    i, t = c // lay.small, c % lay.small - first
    hit = (t >= 0) & (t < per) & (r == (i * length) // width + t)
    return jnp.where(hit, 1.0, 0.0).astype(BF16)


def unpack_small(lay, frames_ref, vec_ref, sc_refs, st_refs):
    count = lay.count * lay.small
    ms = picker(lay, RMAX, count, 0, lay.sp_rows, lay.sp_shard, P_SIZE)
    mv = picker(lay, VPAD, count, lay.sp_rows, lay.vec_rows, lay.vec_shard, 128)
    sp = dot(ms, frames_ref[:, 0:384])
    vec = dot(mv, frames_ref[:, 0:128])
    for r in range(VROWS):
        vec_ref[:, r * 128 : (r + 1) * 128] = vec[r : r + 1, :]
    sp_t = jnp.transpose(sp)
    for (rows, n), sc, st in zip(SIZES, sc_refs, st_refs):
        i = lax.broadcasted_iota(jnp.int32, (rows, rows), 0)
        j = lax.broadcasted_iota(jnp.int32, (rows, rows), 1)
        inside = (i < n) & (j < n)
        beta = sp_t[0:rows, P_SIZE : P_SIZE + 1]
        block = jnp.where(inside, sp[0:rows, 0:rows], 0.0)
        sc[...] = jnp.where((j == n) & (i < n), beta, block).astype(BF16)
        if st is not None:
            st[...] = jnp.where(inside, sp_t[0:rows, 0:rows], 0.0).astype(BF16)


def each_block(lay, part, me):
    dims = PART_DIMS[part]
    for core in range(2):
        for p in range(lay.size[dims[0]]):
            for q in range(lay.size[dims[1]]):
                for s in range(lay.size[dims[2]]):
                    yield core, (p, q, s), dict(zip(dims, (p, q, s)), core=core)


def owner(lay, me, rel, sign):
    at = {}
    for axis, k in rel.items():
        n = lay.size[axis]
        at[axis] = lax.rem(me[axis] + (k if sign > 0 else (n - k) % n), n)
    return lay.index(at)


def assemble(lay, me, piece_refs, win_ref, wout_ref, frames_ref):
    for part in PARTS:
        mine, theirs = piece_refs[part]
        for core, place, rel in each_block(lay, part, me):
            i = owner(lay, me, rel, -1)
            src = theirs if core else mine
            for f, at in lay.offsets(part):
                if f < 6:
                    win_ref[f, pl.ds(pl.multiple_of(i * 16, 16), 16), :] = src[place + (slice(at, at + 16),)]
                elif f < 9:
                    start = pl.multiple_of(i * 48 + 16 * (f - 6), 16)
                    wout_ref[pl.ds(start, 16), :] = src[place + (slice(at, at + 16),)]
                else:
                    frames_ref[pl.ds(pl.multiple_of(i * 16, 16), 16), :] = src[place + (slice(at, at + 16),)]


def forward_part(rows, n, r_ref, vec_ref, win_ref, wout_ref, sc_ref, sv, need_grad, need_out):
    valid = lax.broadcasted_iota(jnp.int32, (rows, 1), 0) < n
    r, k, xh, a = first_norm(rows, valid, r_ref, vec_ref, sv)
    tot = jnp.zeros((rows, 1), F32)
    for j in list(range(NG, NH)) + list(range(NG)):
        z = dot(a, win_ref[j]) + vec_ref[:, O_INB + j * CW : O_INB + (j + 1) * CW]
        h, hp = gelu_both(z, need_grad)
        if j >= NG:
            if need_grad:
                sv["hv"][j - NG, 0:rows, :] = hp
            sv["v"][j - NG, 0:rows, :] = h
            tot = tot + jnp.sum(h, axis=1, keepdims=True)
        else:
            if need_grad:
                sv["sh"][j, 0:rows, :] = hp
            sv["u"][j, 0:rows, :] = h
    mu2 = tot * (1.0 / G)
    ssq = jnp.zeros((rows, 1), F32)
    for j in range(NG):
        vc = sv["v"][j, 0:rows, :] - mu2
        ssq = ssq + jnp.sum(vc * vc, axis=1, keepdims=True)
    k2 = lax.rsqrt(ssq * (1.0 / G) + EPS)
    tail = rows - 16
    trow = lax.broadcasted_iota(jnp.int32, (16, 1), 0) + tail
    for j in range(NG):
        lo = j * CW
        xh2 = (sv["v"][j, 0:rows, :] - mu2) * k2
        if need_grad:
            sv["v"][j, 0:rows, :] = xh2
        q = xh2 * vec_ref[:, O_LN2G + lo : O_LN2G + lo + CW] + vec_ref[:, O_LN2S + lo : O_LN2S + lo + CW]
        sv["q"][j, 0:rows, :] = q.astype(BF16)
        qt = q[tail:rows, :]
        qt = jnp.where(trow < n, qt, jnp.where(trow == n, 1.0, 0.0))
        sv["q"][j, tail:rows, :] = qt.astype(BF16)
    o = None
    for j in range(NG):
        s = dot(sc_ref[...], sv["q"][j, 0:rows, :])
        e = (sv["u"][j, 0:rows, :] * s).astype(BF16)
        if need_grad:
            sv["sh"][j, 0:rows, :] = sv["sh"][j, 0:rows, :] * s
            sv["e"][j, 0:rows, :] = e
        if need_out:
            part = dot(e, wout_ref[j * CW : (j + 1) * CW, :])
            o = part if o is None else o + part
    if need_out:
        o = jnp.where(valid, r + (o + vec_ref[:, O_OUTB : O_OUTB + D]), 0.0)
    return valid, (k, xh, a), k2, o


def first_norm(rows, valid, r_ref, vec_ref, sv):
    if rows > P_SIZE:
        sv["r"][0:P_SIZE, :] = r_ref[0].astype(F32)
        r = sv["r"][0:rows, :]
    else:
        r = r_ref[0, 0:rows, :].astype(F32)
    r = jnp.where(valid, r, 0.0)
    mu = jnp.mean(r, axis=1, keepdims=True)
    c = r - mu
    k = lax.rsqrt(jnp.mean(c * c, axis=1, keepdims=True) + EPS)
    xh = c * k
    a = (xh * vec_ref[:, O_LN1G : O_LN1G + D] + vec_ref[:, O_LN1S : O_LN1S + D]).astype(BF16)
    return r, k, xh, a


def backward_part(rows, n, valid, norm, k2, dn_ref, vec_ref, win_ref, wout_ref, st_ref, sv, acc):
    k, xh, a = norm
    sv["xh1"][0:rows, :] = xh
    sv["at"][0:D, 0:rows] = jnp.transpose(a)
    if rows > P_SIZE:
        sv["r"][0:P_SIZE, :] = dn_ref[0].astype(F32)
        dn = sv["r"][0:rows, :]
    else:
        dn = dn_ref[0, 0:rows, :].astype(F32)
    dn = jnp.where(valid, dn, 0.0)
    do = dn.astype(BF16)
    dot_t = jnp.transpose(do)
    gvec = acc["vec"]
    gvec[:, O_OUTB : O_OUTB + D] += rows_sum8(do.astype(F32))
    for j in range(NG):
        acc["wout"][j] += dot(dot_t, sv["e"][j, 0:rows, :])
        de = dot_nt(do, wout_ref[j * CW : (j + 1) * CW, :])
        sv["dz"][j, 0:rows, :] = (de * sv["sh"][j, 0:rows, :]).astype(BF16)
        sv["ds"][j, 0:rows, :] = (de * sv["u"][j, 0:rows, :]).astype(BF16)
    gs = None
    for j in range(NG):
        part = dot_nt(sv["ds"][j, 0:rows, :], sv["q"][j, 0:rows, :])
        gs = part if gs is None else gs + part
    acc["sp"][SIZES.index((rows, n))][...] += gs
    m1 = jnp.zeros((rows, 1), F32)
    m2 = jnp.zeros((rows, 1), F32)
    for j in range(NG):
        lo = j * CW
        dq = dot(st_ref[...], sv["ds"][j, 0:rows, :])
        sv["dq"][j, 0:rows, :] = dq
        gain = vec_ref[:, O_LN2G + lo : O_LN2G + lo + CW]
        w = dq * sv["v"][j, 0:rows, :]
        gvec[:, O_LN2G + lo : O_LN2G + lo + CW] += rows_sum8(w)
        gvec[:, O_LN2S + lo : O_LN2S + lo + CW] += rows_sum8(dq)
        m1 = m1 + jnp.sum(dq * gain, axis=1, keepdims=True)
        m2 = m2 + jnp.sum(w * gain, axis=1, keepdims=True)
    m1 = m1 * (1.0 / G)
    m2 = m2 * (1.0 / G)
    for j in range(NG):
        lo = j * CW
        gain = vec_ref[:, O_LN2G + lo : O_LN2G + lo + CW]
        dv = k2 * (sv["dq"][j, 0:rows, :] * gain - m1 - sv["v"][j, 0:rows, :] * m2)
        sv["dz"][NG + j, 0:rows, :] = (dv * sv["hv"][j, 0:rows, :]).astype(BF16)
    da = None
    for j in range(NH):
        dz = sv["dz"][j, 0:rows, :]
        acc["win"][j] += dot(sv["at"][0:D, 0:rows], dz)
        gvec[:, O_INB + j * CW : O_INB + (j + 1) * CW] += rows_sum8(dz.astype(F32))
        part = dot_nt(dz, win_ref[j])
        da = part if da is None else da + part
    xh = sv["xh1"][0:rows, :]
    gain = vec_ref[:, O_LN1G : O_LN1G + D]
    w = da * xh
    gvec[:, O_LN1G : O_LN1G + D] += rows_sum8(w)
    gvec[:, O_LN1S : O_LN1S + D] += rows_sum8(da)
    t = da * gain
    mt = jnp.mean(t, axis=1, keepdims=True)
    mx = jnp.mean(w * gain, axis=1, keepdims=True)
    return dn + k * (t - mt - xh * mx)


def put_rows(ref, value, rows):
    if rows > P_SIZE:
        ref[0] = value[0:P_SIZE, :].astype(ref.dtype)
    else:
        ref[0, 0:rows, :] = value.astype(ref.dtype)
        ref[0, rows:P_SIZE, :] = jnp.zeros((P_SIZE - rows, D), ref.dtype)


def by_class(cls, fn):
    for index, (rows, n) in enumerate(SIZES):
        pl.when(cls == index)(functools.partial(fn, index, rows, n))


def gather_grads(lay, acc, sp_scratch, wout_ref, frames_ref):
    for j in range(NG):
        wout_ref[j * CW : (j + 1) * CW, :] = jnp.transpose(acc["wout"][j]).astype(BF16)
    sp_scratch[...] = jnp.zeros(sp_scratch.shape, F32)
    for (rows, n), ref in zip(SIZES, acc["sp"]):
        jj = lax.broadcasted_iota(jnp.int32, (rows, rows), 1)
        val = ref[...]
        sp_scratch[0:rows, 0:rows] += jnp.where(jj < n, val, 0.0)
        sp_scratch[0:rows, P_SIZE : P_SIZE + 1] += val[:, n : n + 1]
    whole = sp_scratch[...]
    row = lax.broadcasted_iota(jnp.int32, (RMAX, RMAX), 0)
    col = lax.broadcasted_iota(jnp.int32, (RMAX, RMAX), 1)
    ext = jnp.where(row == P_SIZE, jnp.transpose(whole), jnp.where(row < P_SIZE, whole, 0.0))
    ext = jnp.where(col < P_SIZE, ext, 0.0).astype(BF16)
    sums = jnp.sum(acc["vec"][...], axis=0, keepdims=True)
    vec = jnp.concatenate([sums[:, r * 128 : (r + 1) * 128] for r in range(VROWS)] + [jnp.zeros((VPAD - VROWS, 128), F32)], axis=0)
    count = lay.count * lay.small
    ms = picker(lay, RMAX, count, 0, lay.sp_rows, lay.sp_shard, P_SIZE)
    mv = picker(lay, VPAD, count, lay.sp_rows, lay.vec_rows, lay.vec_shard, 128)
    tn = (((0,), (0,)), ((), ()))
    frames_ref[...] = jnp.zeros(frames_ref.shape, BF16)
    frames_ref[:, 0:RMAX] = lax.dot_general(ms, ext, tn, preferred_element_type=F32).astype(BF16)
    part = lax.dot_general(mv, vec.astype(BF16), tn, preferred_element_type=F32)
    frames_ref[:, 0:128] += part.astype(BF16)


def scatter_grads(lay, me, acc, wout_ref, frames_ref, out_refs):
    for part in PARTS:
        out = out_refs[part]
        for core, place, rel in each_block(lay, part, me):
            i = owner(lay, me, rel, 1)
            for f, at in lay.offsets(part):
                spot = (core,) + place + (slice(at, at + 16),)
                if f < 6:
                    out[spot] = acc["win"][f, pl.ds(pl.multiple_of(i * 16, 16), 16), :].astype(BF16)
                elif f < 9:
                    out[spot] = wout_ref[pl.ds(pl.multiple_of(i * 48 + 16 * (f - 6), 16), 16), :]
                else:
                    out[spot] = frames_ref[pl.ds(pl.multiple_of(i * 16, 16), 16), :]


def read_me(info_ref, images):
    return {axis: info_ref[images + k] for k, axis in enumerate(("core", "x", "z", "y"))}


class Names:
    def __init__(self, refs):
        self.refs = list(refs)

    def take(self, names):
        got = dict(zip(names, self.refs))
        self.refs = self.refs[len(names) :]
        return got


def load_weights(lay, info_ref, images, given, w):
    if lay.native:
        pieces = {p: (given[p + "0"], given[p + "1"]) for p in PARTS}
        assemble(lay, read_me(info_ref, images), pieces, w["win"], w["wout"], w["frames"])


WEIGHTS = ("win", "wout", "frames")
SAVED = ("u", "sh", "v", "hv", "q", "e")


def kernel_body(lay, images, mode, info_ref, *refs):
    names = Names(refs)
    given = names.take(weight_names(lay))
    r_ref = names.take(["r"])["r"]
    saved_in = names.take(SAVED + ("k2",)) if mode == "back" else {}
    dn_ref = names.take(["dn"])["dn"] if mode != "fore" else None
    out_ref = names.take(["out"])["out"] if mode != "back" else None
    saved_out = names.take(SAVED + ("k2",)) if mode == "fore" else {}
    gr_ref = names.take(["gr"])["gr"] if mode != "fore" else None
    grad_refs = names.take(grad_names(lay)) if mode != "fore" else {}
    w = names.take(WEIGHTS) if lay.native else given
    base = names.take(["sc0", "sc1", "sc2", "r", "vec"])
    scs = [base["sc%d" % k] for k in range(3)]
    sv = {"r": base["r"]}
    sts, acc, sp_scratch = (None,) * 3, {}, None
    if mode != "fore":
        more = names.take(["st0", "st1", "st2", "ds", "dz", "dq", "xh1", "at", "awin", "awout", "as0", "as1", "as2", "avec", "spall"])
        sts = [more["st%d" % k] for k in range(3)]
        sv.update({k: more[k] for k in ("ds", "dz", "dq", "xh1", "at")})
        acc = {"win": more["awin"], "wout": more["awout"], "sp": [more["as%d" % k] for k in range(3)], "vec": more["avec"]}
        sp_scratch = more["spall"]
    if mode == "both":
        sv.update(names.take(SAVED))
    saved = saved_in or saved_out
    sv.update({k: saved[k].at[0] for k in saved if k != "k2"})
    b = pl.program_id(0)

    @pl.when(b == 0)
    def _():
        load_weights(lay, info_ref, images, given, w)
        unpack_small(lay, w["frames"], base["vec"], scs, sts)
        sv["r"][P_SIZE:RMAX, :] = jnp.zeros((RMAX - P_SIZE, D), F32)
        if mode != "fore":
            for ref in [acc["win"], acc["wout"], acc["vec"]] + acc["sp"]:
                ref[...] = jnp.zeros(ref.shape, F32)

    def one(index, rows, n):
        if mode == "back":
            valid = lax.broadcasted_iota(jnp.int32, (rows, 1), 0) < n
            _, k, xh, a = first_norm(rows, valid, r_ref, base["vec"], sv)
            norm, k2 = (k, xh, a), saved["k2"][0, 0:rows, 0:1]
        else:
            valid, norm, k2, o = forward_part(rows, n, r_ref, base["vec"], w["win"], w["wout"], scs[index], sv, True, True)
            put_rows(out_ref, o, rows)
            if mode == "fore":
                saved["k2"][0, 0:rows, :] = jnp.broadcast_to(k2, (rows, 128))
        if mode != "fore":
            grad = backward_part(rows, n, valid, norm, k2, dn_ref, base["vec"], w["win"], w["wout"], sts[index], sv, acc)
            put_rows(gr_ref, grad, rows)

    by_class(info_ref[b], one)

    if mode != "fore":

        @pl.when(b == pl.num_programs(0) - 1)
        def _():
            if lay.native:
                gather_grads(lay, acc, sp_scratch, w["wout"], w["frames"])
                scatter_grads(lay, read_me(info_ref, images), acc, w["wout"], w["frames"], grad_refs)
            else:
                gather_grads(lay, acc, sp_scratch, grad_refs["gwout"], grad_refs["gframes"])
                grad_refs["gwin"][...] = acc["win"][...].astype(BF16)


def weight_names(lay):
    return [p + c for p in PARTS for c in "01"] if lay.native else list(WEIGHTS)


def grad_names(lay):
    return list(PARTS) if lay.native else ["gwin", "gwout", "gframes"]


def image_spec():
    return pl.BlockSpec((1, P_SIZE, D), lambda b, c: (b, 0, 0))


def saved_shapes(images):
    kinds = {"u": F32, "sh": F32, "v": F32, "hv": F32, "q": BF16, "e": BF16}
    shapes = [jax.ShapeDtypeStruct((images, NG, RMAX, CW), kinds[k]) for k in SAVED]
    return shapes + [jax.ShapeDtypeStruct((images, RMAX, 128), F32)]


def saved_specs():
    spec = pl.BlockSpec((1, NG, RMAX, CW), lambda b, c: (b, 0, 0, 0))
    return [spec] * len(SAVED) + [pl.BlockSpec((1, RMAX, 128), lambda b, c: (b, 0, 0))]


def run_kernel(lay, mode, info, weights, r, saved=None, dn=None):
    images = r.shape[0]
    image = jax.ShapeDtypeStruct((images, P_SIZE, D), F32)
    whole = pl.BlockSpec(memory_space=pltpu.VMEM)
    operands = list(weights) + [r]
    in_specs = [whole] * len(weights) + [image_spec()]
    outs, out_specs = [], []
    if mode == "back":
        operands += list(saved)
        in_specs += saved_specs()
    if mode != "fore":
        operands.append(dn)
        in_specs.append(image_spec())
    if mode != "back":
        outs.append(image)
        out_specs.append(image_spec())
    if mode == "fore":
        outs += saved_shapes(images)
        out_specs += saved_specs()
    scratch = []
    if mode != "fore":
        outs.append(image)
        out_specs.append(image_spec())
        if lay.native:
            grads = [(2,) + tuple(lay.size[a] for a in PART_DIMS[p]) + (lay.part_rows(p), CW) for p in PARTS]
        else:
            grads = [(NH, D, CW), (G, D), (lay.count * lay.small, CW)]
        outs += [jax.ShapeDtypeStruct(s, BF16) for s in grads]
        out_specs += [whole] * len(grads)
    if lay.native:
        scratch += [pltpu.VMEM((NH, D, CW), BF16), pltpu.VMEM((G, D), BF16), pltpu.VMEM((lay.count * lay.small, CW), BF16)]
    big = lambda m, dt: pltpu.VMEM((m, RMAX, CW), dt)
    scratch += [pltpu.VMEM((rows, rows), BF16) for rows, _ in SIZES] + [pltpu.VMEM((RMAX, D), F32), pltpu.VMEM((1, VUSED), F32)]
    if mode != "fore":
        scratch += [pltpu.VMEM((rows, rows), BF16) for rows, _ in SIZES]
        scratch += [big(NG, BF16), big(NH, BF16), big(NG, F32), pltpu.VMEM((RMAX, D), F32), pltpu.VMEM((D, RMAX), BF16)]
        scratch += [pltpu.VMEM((NH, D, CW), F32), pltpu.VMEM((NG, D, CW), F32)]
        scratch += [pltpu.VMEM((rows, rows), F32) for rows, _ in SIZES]
        scratch += [pltpu.VMEM((8, VUSED), F32), pltpu.VMEM((RMAX, RMAX), F32)]
    if mode == "both":
        scratch += [big(NG, F32)] * 4 + [big(NG, BF16)] * 2
    return pl.pallas_call(
        functools.partial(kernel_body, lay, images, mode),
        grid_spec=pltpu.PrefetchScalarGridSpec(
            num_scalar_prefetch=1, grid=(images,), in_specs=in_specs, out_specs=out_specs, scratch_shapes=scratch
        ),
        out_shape=outs,
        compiler_params=pltpu.CompilerParams(vmem_limit_bytes=VLIM),
        name="layer_" + mode,
    )(info, *operands)


def pack_layer(lay, w_in, w_out, spatial, vectors, me):
    index = lay.index(me)
    win = w_in.reshape(lay.rows, NH, CW)
    wout = w_out.reshape(NG, lay.rows, D)
    sp_at = lax.rem(index * lay.sp_shard, P_SIZE)
    vec_at = lax.rem(index * lay.vec_shard, 128)
    sp = lax.dynamic_update_slice(jnp.zeros((lay.sp_rows * P_SIZE,), BF16), spatial, (sp_at,)).reshape(lay.sp_rows, P_SIZE)
    vec = lax.dynamic_update_slice(jnp.zeros((lay.vec_rows * 128,), BF16), vectors, (vec_at,)).reshape(lay.vec_rows, 128)
    sp = jnp.pad(sp, ((0, 0), (0, CW - P_SIZE)))
    vec = jnp.pad(vec, ((0, lay.small - lay.sp_rows - lay.vec_rows), (0, CW - 128)))
    fields = [win[:, j] for j in range(NH)] + [wout[k] for k in range(NG)] + [jnp.concatenate([sp, vec])]
    return {p: jnp.concatenate([fields[f] for f in PART_FIELDS[p]]) for p in PARTS}


def ring_gather(lay, value, axis):
    pieces = [value]
    for _ in range(lay.size[axis] - 1):
        pieces.append(lay.shift(pieces[-1], axis))
    return jnp.stack(pieces)


def gather_layer(lay, packed, me):
    got = {}
    for p in PARTS:
        value = packed[p]
        for axis in reversed(PART_DIMS[p]):
            value = ring_gather(lay, value, axis)
        got[p] = (value, lay.shift(value, "core"))
    if lay.native:
        return [a for p in PARTS for a in got[p]]
    win, wout, frames = [None] * NH, [None] * NG, None
    for p in PARTS:
        dims = ("core",) + PART_DIMS[p]
        value = jnp.stack(got[p])
        for k, axis in enumerate(dims):
            n = lay.size[axis]
            value = jnp.take(value, lax.rem(me[axis] - jnp.arange(n) + n, n), axis=k)
        order = [dims.index(a) for a in ("z", "x", "core", "y")]
        value = value.transpose(order + [4, 5]).reshape(lay.count, lay.part_rows(p), CW)
        for f, at in lay.offsets(p):
            if f < 6:
                win[f] = value[:, at : at + lay.rows].reshape(D, CW)
            elif f < 9:
                wout[f - 6] = value[:, at : at + lay.rows]
            else:
                frames = value[:, at : at + lay.small].reshape(lay.count * lay.small, CW)
    return [jnp.stack(win), jnp.stack(wout, axis=1).reshape(G, D), frames]


def ring_scatter(lay, value, axis):
    n = lay.size[axis]
    total = value[n - 1]
    for k in range(n - 2, -1, -1):
        total = lay.shift(total.astype(BF16), axis).astype(F32) + value[k].astype(F32)
    return total


def scatter_layer(lay, grads, me):
    if not lay.native:
        gwin, gwout, gframes = grads
        gwin = gwin.reshape(NH, lay.count, lay.rows, CW)
        gwout = gwout.reshape(lay.count, NG, lay.rows, D)
        gframes = gframes.reshape(lay.count, lay.small, CW)
        fields = [gwin[j] for j in range(NH)] + [gwout[:, k] for k in range(NG)] + [gframes]
        grads = []
        for p in PARTS:
            dims = ("core",) + PART_DIMS[p]
            value = jnp.concatenate([fields[f] for f in PART_FIELDS[p]], axis=1)
            value = value.reshape(lay.size["z"], 2, 2, lay.size["y"], lay.part_rows(p), CW)
            value = value.transpose([("z", "x", "core", "y").index(a) for a in dims] + [4, 5])
            for k, axis in enumerate(dims):
                n = lay.size[axis]
                value = jnp.take(value, lax.rem(me[axis] + jnp.arange(n), n), axis=k)
            grads.append(value)
    result = {}
    for p, value in zip(PARTS, grads):
        for axis in ("core",) + PART_DIMS[p]:
            value = ring_scatter(lay, value, axis)
            if axis != PART_DIMS[p][-1]:
                value = value.astype(BF16)
        result[p] = value
    return result


def unpack_grads(lay, mine, me, sp_len, vec_len):
    fields = {f: mine[p][at : at + (lay.small if f == 9 else lay.rows)] for p in PARTS for f, at in lay.offsets(p)}
    index = lay.index(me)
    gwin = jnp.stack([fields[j] for j in range(NH)], axis=1).reshape(-1)
    gwout = jnp.concatenate([fields[6 + k] for k in range(NG)]).reshape(-1)
    sp = fields[9][0 : lay.sp_rows, 0:P_SIZE].reshape(-1)
    sp = lax.dynamic_slice(sp, (lax.rem(index * lay.sp_shard, P_SIZE),), (lay.sp_shard,))
    vec = fields[9][lay.sp_rows : lay.sp_rows + lay.vec_rows, 0:128].reshape(-1)
    vec = lax.dynamic_slice(vec, (lax.rem(index * lay.vec_shard, 128),), (lay.vec_shard,))
    return gwin, gwout, sp, vec


def per_device(mesh_shape, patches, cotangent, size_class, w_in, w_out, spatial, vectors):
    lay = Layout(mesh_shape, spatial.shape[1], vectors.shape[1])
    wide, narrow = lax.axis_index("wide"), lax.axis_index("narrow")
    me = {"core": lax.rem(wide, 2), "x": lax.rem(wide // 2, 2), "z": wide // 4, "y": narrow}
    info = jnp.concatenate([size_class, jnp.stack([me[a] for a in ("core", "x", "z", "y")]).astype(jnp.int32)])
    weights = []
    for layer in range(LAYERS):
        packed = pack_layer(lay, w_in[layer], w_out[layer], spatial[layer], vectors[layer], me)
        weights.append(gather_layer(lay, packed, me))
    hidden, *saved = run_kernel(lay, "fore", info, weights[0], patches)
    outputs, grad, *grads1 = run_kernel(lay, "both", info, weights[1], hidden, dn=cotangent)
    sums1 = scatter_layer(lay, grads1, me)
    patch_grad, *grads0 = run_kernel(lay, "back", info, weights[0], patches, saved=saved, dn=grad)
    sums0 = scatter_layer(lay, grads0, me)
    flat = [unpack_grads(lay, s, me, spatial.shape[1], vectors.shape[1]) for s in (sums0, sums1)]
    result = [jnp.stack([flat[layer][k] for layer in range(LAYERS)]) for k in range(4)]
    return (outputs, patch_grad, *result)


def solution(mesh):
    shape = (mesh.shape["wide"], mesh.shape["narrow"])
    rows = P(AXES, None, None)
    flat = P(None, AXES)
    return jax.shard_map(
        functools.partial(per_device, shape),
        mesh=mesh,
        in_specs=(rows, rows, P(AXES), flat, flat, flat, flat),
        out_specs=(rows, rows, flat, flat, flat, flat),
        check_vma=False,
    )
```

```python
import functools
import jax
import jax.numpy as jnp
import numpy as np
from jax import lax
from jax.experimental import pallas as pl
from jax.experimental.pallas import tpu as pltpu
from jax.sharding import PartitionSpec as P

D = 512
H = 3072
P_SIZE = 324
LAYERS = 2
G = 1536
EPS = 1e-05
CW = 512
NG = G // CW
NH = H // CW
RMAX = 336
COUNTS = (100, 196, 324)
F32 = jnp.float32
BF16 = jnp.bfloat16
O_LN1G, O_LN1S, O_INB = 0, D, 2 * D
O_LN2G, O_LN2S, O_OUTB = 2 * D + H, 2 * D + H + G, 2 * D + H + 2 * G
VUSED = 3 * D + H + 2 * G
VROWS = VUSED // 128
VPAD = (VROWS + 15) // 16 * 16
GELU_C = 0.7978845608028654
GELU_A = 0.044715
AXES = ("wide", "narrow")
VLIM = 60 * 2**20
PART_FIELDS = {"a": (0, 1, 6), "d": (2, 3, 7), "b": (4, 5, 8, 9)}
PART_DIMS = {"a": ("y", "x", "z"), "d": ("x", "y", "z"), "b": ("z", "y", "x")}
PARTS = ("a", "d", "b")
PIECES = ("t00", "t01", "t10", "t11", "b00", "b01", "b10", "b11")


class Layout:
    def __init__(self, mesh_shape, sp_shard, vec_shard):
        wide, narrow = mesh_shape
        self.size = {"core": 2, "x": 2, "z": wide // 4, "y": narrow}
        self.count = wide * narrow
        self.rows = D // self.count
        self.sp_shard, self.vec_shard = sp_shard, vec_shard
        self.sp_rows = (sp_shard + 2 * P_SIZE - 2) // P_SIZE
        self.vec_rows = (vec_shard + 2 * 128 - 2) // 128
        self.native = self.rows == 16 and narrow == 2 and wide == 16
        self.small = (self.sp_rows + self.vec_rows + 7) // 8 * 8

    def part_rows(self, part):
        return sum(self.small if f == 9 else self.rows for f in PART_FIELDS[part])

    def offsets(self, part):
        spots, at = [], 0
        for f in PART_FIELDS[part]:
            spots.append((f, at))
            at += self.small if f == 9 else self.rows
        return spots

    def index(self, at):
        return ((at["z"] * 2 + at["x"]) * 2 + at["core"]) * self.size["y"] + at["y"]

    def coords(self, i):
        y, wide = i % self.size["y"], i // self.size["y"]
        return {"core": wide % 2, "x": wide // 2 % 2, "z": wide // 4, "y": y}

    def shift(self, value, axis, step=1):
        pairs = []
        for i in range(self.count):
            at = self.coords(i)
            at[axis] = (at[axis] + step) % self.size[axis]
            pairs.append((i, self.index(at)))
        return lax.ppermute(value, AXES, pairs)

    def exchange(self, value, *flips):
        pairs = []
        for i in range(self.count):
            at = self.coords(i)
            for axis, bit in flips[at["core"] % len(flips)].items():
                at[axis] ^= bit
            pairs.append((i, self.index(at)))
        return lax.ppermute(value, AXES, pairs)


CORE, NEAR, FAR = {"core": 1}, {"z": 1}, {"z": 2}
FIRST, SECOND = ({"x": 1}, {"y": 1}), ({"y": 1}, {"x": 1})


def dot(a, b):
    return lax.dot_general(a, b, (((1,), (0,)), ((), ())), preferred_element_type=F32)


def dot_nt(a, b):
    return lax.dot_general(a, b, (((1,), (1,)), ((), ())), preferred_element_type=F32)


def gelu_both(z):
    z2 = z * z
    t = jnp.tanh(z * (GELU_C + (GELU_C * GELU_A) * z2))
    w = 0.5 * t + 0.5
    h = z * w
    return h, w + (h - h * w) * (2.0 * GELU_C + (6.0 * GELU_C * GELU_A) * z2)


def rows_sum8(x):
    rows, cols = x.shape
    return jnp.sum(x.reshape(rows // 8, 8, cols), axis=0)


def picker(lay, rows, cols, first, per, length, width):
    r = lax.broadcasted_iota(jnp.int32, (rows, cols), 0)
    c = lax.broadcasted_iota(jnp.int32, (rows, cols), 1)
    i, t = c // lay.small, c % lay.small - first
    hit = (t >= 0) & (t < per) & (r == (i * length) // width + t)
    return jnp.where(hit, 1.0, 0.0).astype(BF16)


def unpack_small(lay, frames_ref, vec_ref, sc_ref, st_ref):
    count = lay.count * lay.small
    ms = picker(lay, RMAX, count, 0, lay.sp_rows, lay.sp_shard, P_SIZE)
    mv = picker(lay, VPAD, count, lay.sp_rows, lay.vec_rows, lay.vec_shard, 128)
    sp = dot(ms, frames_ref[:, 0:384])
    vec = dot(mv, frames_ref[:, 0:128])
    for r in range(VROWS):
        vec_ref[:, r * 128 : (r + 1) * 128] = vec[r : r + 1, :]
    row = lax.broadcasted_iota(jnp.int32, (RMAX, RMAX), 0)
    col = lax.broadcasted_iota(jnp.int32, (RMAX, RMAX), 1)
    inside = (row < P_SIZE) & (col < P_SIZE)
    sp = sp[:, 0:RMAX]
    sp_t = jnp.transpose(sp)
    sc_ref[...] = jnp.where(inside, sp, jnp.where((col == P_SIZE) & (row < P_SIZE), sp_t, 0.0)).astype(BF16)
    if st_ref is not None:
        st_ref[...] = jnp.where(inside, sp_t, 0.0).astype(BF16)


def role_blocks(lay, me, sign):
    for who in range(2):
        role = me["core"] ^ who
        for second in range(2):
            for first, k1, k2, core in np.ndindex(2, 2, 2, 2):
                swap = role * (first ^ second)
                at = {"z": me["z"] ^ (k1 + 2 * k2), "core": role ^ core, "x": me["x"] ^ first ^ swap, "y": me["y"] ^ second ^ swap}
                yield who, second, (first, k1, k2, core), role, lay.index(at)


def both_blocks(lay, me, sign):
    for who in range(2):
        role = me["core"] ^ who
        for k1 in range(2):
            for second, k2, first in np.ndindex(2, 2, 2):
                swap = role * (first ^ second)
                at = {"z": me["z"] ^ (k1 + 2 * k2), "core": role, "x": me["x"] ^ first ^ swap, "y": me["y"] ^ second ^ swap}
                yield who, k1, (second, k2, first), lay.index(at)


def sixteen(start):
    return pl.ds(pl.multiple_of(start, 16), 16)


def assemble(lay, me, given, win_ref, wout_ref, frames_ref):
    for who, second, place, role, i in role_blocks(lay, me, -1):
        src = given["t%d%d" % (who, second)]
        for t in range(2):
            win_ref[2 * role + t, sixteen(i * 16), :] = src[place + (slice(16 * t, 16 * t + 16),)]
        wout_ref[sixteen(i * 48 + 16 * role), :] = src[place + (slice(32, 48),)]
    for who, z, place, i in both_blocks(lay, me, -1):
        src = given["b%d%d" % (who, z)]
        for t in range(2):
            win_ref[4 + t, sixteen(i * 16), :] = src[place + (slice(16 * t, 16 * t + 16),)]
        wout_ref[sixteen(i * 48 + 32), :] = src[place + (slice(32, 48),)]
        frames_ref[sixteen(i * 16), :] = src[place + (slice(48, 64),)]


def forward_part(rows, valid, r_ref, vec_ref, win_ref, wout_ref, sc_ref, sv, save):
    h, hp = sv["h"], sv["hp"]
    r, k, xh, a = first_norm(rows, valid, r_ref, vec_ref)
    tot = jnp.zeros((rows, 1), F32)
    for j in list(range(NG, NH)) + list(range(NG)):
        z = dot(a, win_ref[j]) + vec_ref[:, O_INB + j * CW : O_INB + (j + 1) * CW]
        h[j], hpj = gelu_both(z)
        if save and j >= NG:
            sv["hv"][j - NG] = hpj.astype(BF16)
        else:
            hp[j] = hpj
        if j >= NG:
            tot = tot + jnp.sum(h[j], axis=1, keepdims=True)
    mu2 = tot * (1.0 / G)
    ssq = jnp.zeros((rows, 1), F32)
    for j in range(NG):
        vc = h[NG + j] - mu2
        ssq = ssq + jnp.sum(vc * vc, axis=1, keepdims=True)
    k2 = lax.rsqrt(ssq * (1.0 / G) + EPS)
    one = jnp.where(lax.broadcasted_iota(jnp.int32, (rows, 1), 0) == P_SIZE, 1.0, 0.0)
    for j in range(NG):
        lo = j * CW
        xh2 = (h[NG + j] - mu2) * k2
        sv["v"][j] = xh2.astype(sv["v"].dtype)
        q = xh2 * vec_ref[:, O_LN2G + lo : O_LN2G + lo + CW] + vec_ref[:, O_LN2S + lo : O_LN2S + lo + CW]
        sv["q"][j] = jnp.where(valid, q, one).astype(BF16)
    o = None
    for j in range(NG):
        s = dot(sc_ref[...], sv["q"][j])
        u = h[j]
        e = (u * s).astype(BF16)
        sv["sh"][j] = (hp[j] * s).astype(sv["sh"].dtype)
        sv["e"][j] = e
        if save:
            sv["u"][j] = u.astype(BF16)
        part = dot(e, wout_ref[j * CW : (j + 1) * CW, :])
        o = part if o is None else o + part
    o = jnp.where(valid, r + (o + vec_ref[:, O_OUTB : O_OUTB + D]), 0.0)
    return (k, xh, a), k2, o


def first_norm(rows, valid, r_ref, vec_ref):
    r = jnp.where(valid, r_ref[0, 0:rows, :].astype(F32), 0.0)
    mu = jnp.mean(r, axis=1, keepdims=True)
    c = r - mu
    k = lax.rsqrt(jnp.mean(c * c, axis=1, keepdims=True) + EPS)
    xh = c * k
    a = (xh * vec_ref[:, O_LN1G : O_LN1G + D] + vec_ref[:, O_LN1S : O_LN1S + D]).astype(BF16)
    return r, k, xh, a


def backward_part(rows, valid, norm, k2, dn_ref, vec_ref, win_ref, wout_ref, st_ref, sv, acc):
    k, xh, a = norm
    sv["xh1"][0:rows, :] = xh
    sv["at"][0:D, 0:rows] = jnp.transpose(a)
    dn = jnp.where(valid, dn_ref[0, 0:rows, :].astype(F32), 0.0)
    do = dn.astype(BF16)
    dot_t = jnp.transpose(do)
    gvec = acc["vec"]
    gvec[:, O_OUTB : O_OUTB + D] += rows_sum8(do.astype(F32))
    for j in range(NG):
        acc["wout"][j] += dot(dot_t, sv["e"][j, 0:rows, :])
        de = dot_nt(do, wout_ref[j * CW : (j + 1) * CW, :])
        sv["dz"][j, 0:rows, :] = (de * sv["sh"][j].astype(F32)).astype(BF16)
        sv["ds"][j, 0:rows, :] = (de * sv["u"][j].astype(F32)).astype(BF16)
    gs = None
    for j in range(NG):
        part = dot_nt(sv["ds"][j, 0:rows, :], sv["q"][j, 0:rows, :])
        gs = part if gs is None else gs + part
    acc["sp"][...] += gs
    m1 = jnp.zeros((rows, 1), F32)
    m2 = jnp.zeros((rows, 1), F32)
    for j in range(NG):
        lo = j * CW
        dq = jnp.where(valid, dot(st_ref[...], sv["ds"][j, 0:rows, :]), 0.0)
        sv["dq"][j, 0:rows, :] = dq
        gain = vec_ref[:, O_LN2G + lo : O_LN2G + lo + CW]
        w = dq * sv["v"][j].astype(F32)
        gvec[:, O_LN2G + lo : O_LN2G + lo + CW] += rows_sum8(w)
        gvec[:, O_LN2S + lo : O_LN2S + lo + CW] += rows_sum8(dq)
        m1 = m1 + jnp.sum(dq * gain, axis=1, keepdims=True)
        m2 = m2 + jnp.sum(w * gain, axis=1, keepdims=True)
    m1 = m1 * (1.0 / G)
    m2 = m2 * (1.0 / G)
    for j in range(NG):
        lo = j * CW
        gain = vec_ref[:, O_LN2G + lo : O_LN2G + lo + CW]
        dv = k2 * (sv["dq"][j, 0:rows, :] * gain - m1 - sv["v"][j].astype(F32) * m2)
        sv["dz"][NG + j, 0:rows, :] = (dv * sv["hv"][j].astype(F32)).astype(BF16)
    da = None
    for j in range(NH):
        dz = sv["dz"][j, 0:rows, :]
        acc["win"][j] += dot(sv["at"][0:D, 0:rows], dz)
        gvec[:, O_INB + j * CW : O_INB + (j + 1) * CW] += rows_sum8(dz.astype(F32))
        part = dot_nt(dz, win_ref[j])
        da = part if da is None else da + part
    xh = sv["xh1"][0:rows, :]
    gain = vec_ref[:, O_LN1G : O_LN1G + D]
    w = da * xh
    gvec[:, O_LN1G : O_LN1G + D] += rows_sum8(w)
    gvec[:, O_LN1S : O_LN1S + D] += rows_sum8(da)
    t = da * gain
    mt = jnp.mean(t, axis=1, keepdims=True)
    mx = jnp.mean(w * gain, axis=1, keepdims=True)
    return dn + k * (t - mt - xh * mx)


def gather_grads(lay, acc, wout_ref, frames_ref):
    for j in range(NG):
        wout_ref[j * CW : (j + 1) * CW, :] = jnp.transpose(acc["wout"][j]).astype(BF16)
    whole = acc["sp"][...]
    row = lax.broadcasted_iota(jnp.int32, (RMAX, RMAX), 0)
    col = lax.broadcasted_iota(jnp.int32, (RMAX, RMAX), 1)
    ext = jnp.where(row == P_SIZE, jnp.transpose(whole), jnp.where(row < P_SIZE, whole, 0.0))
    ext = jnp.where(col < P_SIZE, ext, 0.0).astype(BF16)
    sums = jnp.sum(acc["vec"][...], axis=0, keepdims=True)
    vec = jnp.concatenate([sums[:, r * 128 : (r + 1) * 128] for r in range(VROWS)] + [jnp.zeros((VPAD - VROWS, 128), F32)], axis=0)
    count = lay.count * lay.small
    ms = picker(lay, RMAX, count, 0, lay.sp_rows, lay.sp_shard, P_SIZE)
    mv = picker(lay, VPAD, count, lay.sp_rows, lay.vec_rows, lay.vec_shard, 128)
    tn = (((0,), (0,)), ((), ()))
    frames_ref[...] = jnp.zeros(frames_ref.shape, BF16)
    frames_ref[:, 0:RMAX] = lax.dot_general(ms, ext, tn, preferred_element_type=F32).astype(BF16)
    part = lax.dot_general(mv, vec.astype(BF16), tn, preferred_element_type=F32)
    frames_ref[:, 0:128] += part.astype(BF16)


def scatter_grads(lay, me, acc, wout_ref, frames_ref, out):
    for who, second, place, role, i in role_blocks(lay, me, 1):
        dst = out["t%d%d" % (who, second)]
        for t in range(2):
            dst[place + (slice(16 * t, 16 * t + 16),)] = acc["win"][2 * role + t, sixteen(i * 16), :].astype(BF16)
        dst[place + (slice(32, 48),)] = wout_ref[sixteen(i * 48 + 16 * role), :]
    for who, z, place, i in both_blocks(lay, me, 1):
        dst, spot = out["b%d%d" % (who, z)], place
        for t in range(2):
            dst[spot + (slice(16 * t, 16 * t + 16),)] = acc["win"][4 + t, sixteen(i * 16), :].astype(BF16)
        dst[spot + (slice(32, 48),)] = wout_ref[sixteen(i * 48 + 32), :]
        dst[spot + (slice(48, 64),)] = frames_ref[sixteen(i * 16), :]


def read_me(info_ref, images):
    return {axis: info_ref[images + k] for k, axis in enumerate(("core", "x", "z", "y"))}


class Names:
    def __init__(self, refs):
        self.refs = list(refs)

    def take(self, names):
        got = dict(zip(names, self.refs))
        self.refs = self.refs[len(names) :]
        return got


WEIGHTS = ("win", "wout", "frames")
SAVED = ("u", "sh", "v", "hv", "q", "e")


def kernel_body(lay, images, mode, scratch_names, info_ref, *refs):
    names = Names(refs)
    given = names.take(weight_names(lay))
    r_ref = names.take(["r"])["r"]
    saved = names.take(SAVED + ("k2",)) if mode == "back" else {}
    dn_ref = names.take(["dn"])["dn"] if mode != "fore" else None
    out_ref = names.take(["out"])["out"] if mode != "back" else None
    if mode == "fore":
        saved = names.take(SAVED + ("k2",))
    gr_ref = names.take(["gr"])["gr"] if mode != "fore" else None
    grad_refs = names.take(grad_names(lay)) if mode != "fore" else {}
    sv = names.take(scratch_names)
    w = sv if lay.native else given
    sv.update({k: saved[k].at[0] for k in saved})
    if mode == "both":
        sv.update(u=sv["h"], sh=sv["hp"], v=sv["h"].at[NG:NH], hv=sv["hp"].at[NG:NH])
    acc = {k: sv.get("a" + k) for k in ("win", "wout", "sp", "vec")}
    b = pl.program_id(0)

    @pl.when(b == 0)
    def _():
        if lay.native:
            assemble(lay, read_me(info_ref, images), given, w["win"], w["wout"], w["frames"])
        unpack_small(lay, w["frames"], sv["vec"], sv["sc"], sv.get("st"))
        if mode != "fore":
            for ref in acc.values():
                ref[...] = jnp.zeros(ref.shape, F32)

    cls = info_ref[b]
    n = jnp.where(cls == 0, COUNTS[0], jnp.where(cls == 1, COUNTS[1], COUNTS[2]))
    valid = lax.broadcasted_iota(jnp.int32, (RMAX, 1), 0) < n
    if mode == "back":
        _, k, xh, a = first_norm(RMAX, valid, r_ref, sv["vec"])
        norm, k2 = (k, xh, a), sv["k2"][:, 0:1]
    else:
        norm, k2, o = forward_part(RMAX, valid, r_ref, sv["vec"], w["win"], w["wout"], sv["sc"], sv, mode == "fore")
        out_ref[0] = o
        if mode == "fore":
            sv["k2"][...] = jnp.broadcast_to(k2, (RMAX, 128))
    if mode != "fore":
        gr_ref[0] = backward_part(RMAX, valid, norm, k2, dn_ref, sv["vec"], w["win"], w["wout"], sv["st"], sv, acc)

        @pl.when(b == pl.num_programs(0) - 1)
        def _():
            if lay.native:
                gather_grads(lay, acc, w["wout"], w["frames"])
                scatter_grads(lay, read_me(info_ref, images), acc, w["wout"], w["frames"], grad_refs)
            else:
                gather_grads(lay, acc, grad_refs["gwout"], grad_refs["gframes"])
                grad_refs["gwin"][...] = acc["win"][...].astype(BF16)


def scratch_for(lay, mode):
    big = lambda m, dt: pltpu.VMEM((m, RMAX, CW), dt)
    wide = lambda dt: pltpu.VMEM((RMAX, D), dt)
    made = {}
    if lay.native:
        made.update(win=pltpu.VMEM((NH, D, CW), BF16), wout=pltpu.VMEM((G, D), BF16), frames=pltpu.VMEM((lay.count * lay.small, CW), BF16))
    made.update(vec=pltpu.VMEM((1, VUSED), F32), sc=pltpu.VMEM((RMAX, RMAX), BF16))
    if mode != "back":
        made.update(h=big(NH, F32), hp=big(NH, F32))
    if mode == "both":
        made.update(q=big(NG, BF16), e=big(NG, BF16))
    if mode != "fore":
        made.update(st=pltpu.VMEM((RMAX, RMAX), BF16), ds=big(NG, BF16), dz=big(NH, BF16), dq=big(NG, F32), xh1=wide(F32))
        made.update(at=pltpu.VMEM((D, RMAX), BF16), awin=pltpu.VMEM((NH, D, CW), F32), awout=pltpu.VMEM((NG, D, CW), F32))
        made.update(asp=pltpu.VMEM((RMAX, RMAX), F32), avec=pltpu.VMEM((8, VUSED), F32))
    return made


def weight_names(lay):
    if not lay.native:
        return list(WEIGHTS)
    return list(PIECES)


def grad_names(lay):
    return list(PIECES) if lay.native else ["gwin", "gwout", "gframes"]


def image_spec():
    return pl.BlockSpec((1, RMAX, D), lambda b, c: (b, 0, 0))


def saved_shapes(images):
    shapes = [jax.ShapeDtypeStruct((images, NG, RMAX, CW), BF16) for _ in SAVED]
    return shapes + [jax.ShapeDtypeStruct((images, RMAX, 128), F32)]


def saved_specs():
    spec = pl.BlockSpec((1, NG, RMAX, CW), lambda b, c: (b, 0, 0, 0))
    return [spec] * len(SAVED) + [pl.BlockSpec((1, RMAX, 128), lambda b, c: (b, 0, 0))]


def run_kernel(lay, mode, info, weights, r, saved=None, dn=None):
    images = r.shape[0]
    image = jax.ShapeDtypeStruct((images, RMAX, D), F32)
    whole = pl.BlockSpec(memory_space=pltpu.VMEM)
    operands = list(weights) + [r]
    in_specs = [whole] * len(weights) + [image_spec()]
    outs, out_specs = [], []
    if mode == "back":
        operands += list(saved)
        in_specs += saved_specs()
    if mode != "fore":
        operands.append(dn)
        in_specs.append(image_spec())
    if mode != "back":
        outs.append(image)
        out_specs.append(image_spec())
    if mode == "fore":
        outs += saved_shapes(images)
        out_specs += saved_specs()
    if mode != "fore":
        outs.append(image)
        out_specs.append(image_spec())
        if lay.native:
            grads = [(2, 2, 2, 2, lay.part_rows("a"), CW)] * 4 + [(2, 2, 2, lay.part_rows("b"), CW)] * 4
        else:
            grads = [(NH, D, CW), (G, D), (lay.count * lay.small, CW)]
        outs += [jax.ShapeDtypeStruct(s, BF16) for s in grads]
        out_specs += [whole] * len(grads)
    scratch = scratch_for(lay, mode)
    return pl.pallas_call(
        functools.partial(kernel_body, lay, images, mode, list(scratch)),
        grid_spec=pltpu.PrefetchScalarGridSpec(
            num_scalar_prefetch=1, grid=(images,), in_specs=in_specs, out_specs=out_specs, scratch_shapes=list(scratch.values())
        ),
        out_shape=outs,
        compiler_params=pltpu.CompilerParams(vmem_limit_bytes=VLIM),
        name="layer_" + mode,
    )(info, *operands)


def pack_layer(lay, w_in, w_out, spatial, vectors, me):
    index = lay.index(me)
    win = w_in.reshape(lay.rows, NH, CW)
    wout = w_out.reshape(NG, lay.rows, D)
    sp_at = lax.rem(index * lay.sp_shard, P_SIZE)
    vec_at = lax.rem(index * lay.vec_shard, 128)
    sp = lax.dynamic_update_slice(jnp.zeros((lay.sp_rows * P_SIZE,), BF16), spatial, (sp_at,)).reshape(lay.sp_rows, P_SIZE)
    vec = lax.dynamic_update_slice(jnp.zeros((lay.vec_rows * 128,), BF16), vectors, (vec_at,)).reshape(lay.vec_rows, 128)
    sp = jnp.pad(sp, ((0, 0), (0, CW - P_SIZE)))
    vec = jnp.pad(vec, ((0, lay.small - lay.sp_rows - lay.vec_rows), (0, CW - 128)))
    fields = [win[:, j] for j in range(NH)] + [wout[k] for k in range(NG)] + [jnp.concatenate([sp, vec])]
    return {p: jnp.concatenate([fields[f] for f in PART_FIELDS[p]]) for p in PARTS}


def ring_gather(lay, value, axis):
    pieces = [value]
    for _ in range(lay.size[axis] - 1):
        pieces.append(lay.shift(pieces[-1], axis))
    return pieces


def hold(*values):
    return lax.optimization_barrier(values)


def move(lay, *items):
    values = hold(*[value for value, _ in items])
    return hold(*[lay.exchange(value, *flips) for value, (_, flips) in zip(values, items)])


def gather_start(lay, packed, me):
    even = me["core"] == 0
    keep = jnp.where(even, packed["a"], packed["d"])
    give = jnp.where(even, packed["d"], packed["a"])
    return jnp.stack([keep, lay.exchange(give, CORE)]), packed["b"]


GATHER_T = ((FAR,), (NEAR,), FIRST, SECOND)
GATHER_B = (FIRST, (FAR,), SECOND, (NEAR,))


def gather_plain(lay, packed, me):
    win, wout, frames = [None] * NH, [None] * NG, None
    for p in PARTS:
        dims = ("core",) + PART_DIMS[p]
        value = packed[p]
        for axis in reversed(dims):
            value = jnp.stack(ring_gather(lay, value, axis))
        for k, axis in enumerate(dims):
            n = lay.size[axis]
            value = jnp.take(value, lax.rem(me[axis] - jnp.arange(n) + n, n), axis=k)
        order = [dims.index(a) for a in ("z", "x", "core", "y")]
        value = value.transpose(order + [4, 5]).reshape(lay.count, lay.part_rows(p), CW)
        for f, at in lay.offsets(p):
            if f < 6:
                win[f] = value[:, at : at + lay.rows].reshape(D, CW)
            elif f < 9:
                wout[f - 6] = value[:, at : at + lay.rows]
            else:
                frames = value[:, at : at + lay.small].reshape(lay.count * lay.small, CW)
    return [jnp.stack(win), jnp.stack(wout, axis=1).reshape(G, D), frames]


def ring_scatter(lay, value, axis):
    n = lay.size[axis]
    total = value[n - 1].astype(F32)
    for k in range(n - 2, -1, -1):
        total = lay.shift(total.astype(BF16), axis).astype(F32) + value[k].astype(F32)
    return total


def low(v):
    return v.astype(BF16)


def add(mine, got):
    return mine.astype(F32) + got.astype(F32)


def scatter_core(lay, grads):
    t00, t01, t10, t11, b00, b01, b10, b11 = grads
    t11, b11 = move(lay, (t11, (CORE,)), (b11, (CORE,)))
    far, bfar = hold(low(add(t01, t11)), low(add(b01, b11)))
    t10, b10, far, bfar = hold(t10, b10, far, bfar)
    return far, bfar, (t00, lay.exchange(t10, CORE)), (b00, lay.exchange(b10, CORE))


SCATTER_T = (SECOND, FIRST, (NEAR,), (FAR,))
SCATTER_B = ((NEAR,), SECOND, (FAR,), FIRST)


def scatter_end(me, top, other, b):
    even = me["core"] == 0
    return {"a": jnp.where(even, top[0], other), "d": jnp.where(even, other, top[0]), "b": b}


def native_path(lay, me, info, packed, patches, cotangent):
    stack = lambda v, got: jnp.stack([v, got])
    (t0, b0), (t1, b1) = [gather_start(lay, p, me) for p in packed]
    x, y = move(lay, (t0, GATHER_T[0]), (b0, GATHER_B[0]))
    t0, b0 = stack(t0, x), stack(b0, y)
    for k in (1, 2):
        x, y, u, v = move(lay, (t0, GATHER_T[k]), (b0, GATHER_B[k]), (t1, GATHER_T[k - 1]), (b1, GATHER_B[k - 1]))
        t0, b0, t1, b1 = stack(t0, x), stack(b0, y), stack(t1, u), stack(b1, v)
    t0, b0, t1, b1 = hold(t0, b0, t1, b1)
    t0c, b0c = lay.exchange(t0, CORE), lay.exchange(b0, CORE)
    x, y, u, v = [lay.exchange(g, *f) for g, f in ((t0, SECOND), (b0, (NEAR,)), (t1, FIRST), (b1, SECOND))]
    x, y, u, v = hold(x, y, u, v)
    weights0 = [t0, x, t0c, lay.exchange(x, CORE), b0, y, b0c, lay.exchange(y, CORE)]
    t1, b1 = stack(t1, u), stack(b1, v)
    *weights0, t1, b1 = hold(*weights0, t1, b1)
    x, y, t1c, b1c = [lay.exchange(v, *f) for v, f in ((t1, SECOND), (b1, (NEAR,)), (t1, (CORE,)), (b1, (CORE,)))]
    hidden, *saved = run_kernel(lay, "fore", info, weights0, patches)
    x, y, t1c, b1c, hidden = hold(x, y, t1c, b1c, hidden)
    weights1 = [t1, x, t1c, lay.exchange(x, CORE), b1, y, b1c, lay.exchange(y, CORE)]
    outputs, grad, *grads1 = run_kernel(lay, "both", info, weights1, hidden, dn=cotangent)

    far1, bfar1, near1, bnear1 = scatter_core(lay, grads1)
    far1, bfar1, grad = hold(far1, bfar1, grad)
    x, y = lay.exchange(far1, *SECOND), lay.exchange(bfar1, NEAR)
    patch_grad, *grads0 = run_kernel(lay, "back", info, weights0, patches, saved=saved, dn=grad)
    x, y, patch_grad, outputs, *grads0 = hold(x, y, patch_grad, outputs, *grads0)
    top1, b1 = add(add(*near1), x), add(add(*bnear1), y)
    far0, bfar0, near0, bnear0 = scatter_core(lay, grads0)
    u, v = move(lay, (low(top1[1]), SCATTER_T[1]), (low(b1[1]), SCATTER_B[1]))
    top1, b1 = add(top1[0], u), add(b1[0], v)
    far0, bfar0, outputs, patch_grad = hold(far0, bfar0, outputs, patch_grad)
    x, y = lay.exchange(far0, *SECOND), lay.exchange(bfar0, NEAR)
    x, y, outputs, patch_grad = hold(x, y, tilt(outputs), tilt(patch_grad))
    top0, b0 = add(add(*near0), x), add(add(*bnear0), y)
    x, y, u, v = move(lay, *[(low(s[1]), f) for s, f in ((top0, SCATTER_T[1]), (b0, SCATTER_B[1]), (top1, SCATTER_T[2]), (b1, SCATTER_B[2]))])
    top0, b0, top1, b1 = add(top0[0], x), add(b0[0], y), add(top1[0], u), add(b1[0], v)
    x, y, u, v = move(lay, *[(low(s[1]), f) for s, f in ((top0, SCATTER_T[2]), (b0, SCATTER_B[2]), (top1, SCATTER_T[3]), (b1, SCATTER_B[3]))])
    top0, b0, top1, b1 = add(top0[0], x), add(b0[0], y), add(top1[0], u), add(b1[0], v)
    x, y, last1 = move(lay, (low(top0[1]), SCATTER_T[3]), (low(b0[1]), SCATTER_B[3]), (top1[1], (CORE,)))
    top0, b0 = add(top0[0], x), add(b0[0], y)
    last0 = lay.exchange(top0[1], CORE)
    outputs, patch_grad = outputs.transpose(1, 0, 2), patch_grad.transpose(1, 0, 2)
    return outputs, patch_grad, scatter_end(me, top0, last0, b0), scatter_end(me, top1, last1, b1)


def tilt(v):
    return v[:, :P_SIZE].transpose(1, 0, 2)


def plain_path(lay, me, info, packed, patches, cotangent):
    weights0, weights1 = [gather_plain(lay, p, me) for p in packed]
    hidden, *saved = run_kernel(lay, "fore", info, weights0, patches)
    outputs, grad, *grads1 = run_kernel(lay, "both", info, weights1, hidden, dn=cotangent)
    patch_grad, *grads0 = run_kernel(lay, "back", info, weights0, patches, saved=saved, dn=grad)
    outputs, patch_grad = outputs[:, :P_SIZE], patch_grad[:, :P_SIZE]
    return outputs, patch_grad, scatter_plain(lay, grads0, me), scatter_plain(lay, grads1, me)


def scatter_plain(lay, grads, me):
    gwin, gwout, gframes = grads
    gwin = gwin.reshape(NH, lay.count, lay.rows, CW)
    gwout = gwout.reshape(lay.count, NG, lay.rows, D)
    gframes = gframes.reshape(lay.count, lay.small, CW)
    fields = [gwin[j] for j in range(NH)] + [gwout[:, k] for k in range(NG)] + [gframes]
    result = {}
    for p in PARTS:
        dims = ("core",) + PART_DIMS[p]
        value = jnp.concatenate([fields[f] for f in PART_FIELDS[p]], axis=1)
        value = value.reshape(lay.size["z"], 2, 2, lay.size["y"], lay.part_rows(p), CW)
        value = value.transpose([("z", "x", "core", "y").index(a) for a in dims] + [4, 5])
        for k, axis in enumerate(dims):
            n = lay.size[axis]
            value = jnp.take(value, lax.rem(me[axis] + jnp.arange(n), n), axis=k)
        for axis in dims:
            value = ring_scatter(lay, value, axis)
        result[p] = value
    return result


def unpack_grads(lay, mine, me, sp_len, vec_len):
    fields = {f: mine[p][at : at + (lay.small if f == 9 else lay.rows)] for p in PARTS for f, at in lay.offsets(p)}
    index = lay.index(me)
    gwin = jnp.stack([fields[j] for j in range(NH)], axis=1).reshape(-1)
    gwout = jnp.concatenate([fields[6 + k] for k in range(NG)]).reshape(-1)
    sp = fields[9][0 : lay.sp_rows, 0:P_SIZE].reshape(-1)
    sp = lax.dynamic_slice(sp, (lax.rem(index * lay.sp_shard, P_SIZE),), (lay.sp_shard,))
    vec = fields[9][lay.sp_rows : lay.sp_rows + lay.vec_rows, 0:128].reshape(-1)
    vec = lax.dynamic_slice(vec, (lax.rem(index * lay.vec_shard, 128),), (lay.vec_shard,))
    return gwin, gwout, sp, vec


def per_device(mesh_shape, patches, cotangent, size_class, w_in, w_out, spatial, vectors):
    lay = Layout(mesh_shape, spatial.shape[1], vectors.shape[1])
    wide, narrow = lax.axis_index("wide"), lax.axis_index("narrow")
    me = {"core": lax.rem(wide, 2), "x": lax.rem(wide // 2, 2), "z": wide // 4, "y": narrow}
    info = jnp.concatenate([size_class, jnp.stack([me[a] for a in ("core", "x", "z", "y")]).astype(jnp.int32)])
    packed = [pack_layer(lay, w_in[l], w_out[l], spatial[l], vectors[l], me) for l in range(LAYERS)]
    spare = ((0, 0), (0, RMAX - P_SIZE), (0, 0))
    patches, cotangent = jnp.pad(patches, spare), jnp.pad(cotangent, spare)
    path = native_path if lay.native else plain_path
    outputs, patch_grad, *sums = path(lay, me, info, packed, patches, cotangent)
    flat = [unpack_grads(lay, s, me, spatial.shape[1], vectors.shape[1]) for s in sums]
    result = [jnp.stack([flat[layer][k] for layer in range(LAYERS)]) for k in range(4)]
    return (outputs, patch_grad, *result)


def solution(mesh):
    shape = (mesh.shape["wide"], mesh.shape["narrow"])
    rows = P(AXES, None, None)
    flat = P(None, AXES)
    return jax.shard_map(
        functools.partial(per_device, shape),
        mesh=mesh,
        in_specs=(rows, rows, P(AXES), flat, flat, flat, flat),
        out_specs=(rows, rows, flat, flat, flat, flat),
        check_vma=False,
    )
```

```python
import functools
import jax
import jax.numpy as jnp
import numpy as np
from jax import lax
from jax.experimental import pallas as pl
from jax.experimental.pallas import tpu as pltpu
from jax.sharding import PartitionSpec as P

D = 512
H = 3072
P_SIZE = 324
LAYERS = 2
G = 1536
EPS = 1e-05
CW = 512
NG = G // CW
NH = H // CW
RMAX = 336
COUNTS = (100, 196, 324)
F32 = jnp.float32
BF16 = jnp.bfloat16
O_LN1G, O_LN1S, O_INB = 0, D, 2 * D
O_LN2G, O_LN2S, O_OUTB = 2 * D + H, 2 * D + H + G, 2 * D + H + 2 * G
VUSED = 3 * D + H + 2 * G
VROWS = VUSED // 128
VPAD = (VROWS + 15) // 16 * 16
GELU_C = 0.7978845608028654
GELU_A = 0.044715
AXES = ("wide", "narrow")
VLIM = {"plain": 60 * 2**20, "fore": 46 * 2**20, "both": 48 * 2**20, "back": 48 * 2**20}
PART_FIELDS = {"a": (0, 1, 6), "d": (2, 3, 7), "b": (4, 5, 8, 9)}
PART_DIMS = {"a": ("y", "x", "z"), "d": ("x", "y", "z"), "b": ("z", "y", "x")}
PARTS = ("a", "d", "b")
PIECES = ("t00", "t01", "t10", "t11", "b00", "b01", "b10", "b11")


class Layout:
    def __init__(self, mesh_shape, sp_shard, vec_shard):
        wide, narrow = mesh_shape
        self.size = {"core": 2, "x": 2, "z": wide // 4, "y": narrow}
        self.count = wide * narrow
        self.rows = D // self.count
        self.sp_shard, self.vec_shard = sp_shard, vec_shard
        self.sp_rows = (sp_shard + 2 * P_SIZE - 2) // P_SIZE
        self.vec_rows = (vec_shard + 2 * 128 - 2) // 128
        self.native = self.rows == 16 and narrow == 2 and wide == 16
        self.small = (self.sp_rows + self.vec_rows + 7) // 8 * 8

    def part_rows(self, part):
        return sum(self.small if f == 9 else self.rows for f in PART_FIELDS[part])

    def offsets(self, part):
        spots, at = [], 0
        for f in PART_FIELDS[part]:
            spots.append((f, at))
            at += self.small if f == 9 else self.rows
        return spots

    def index(self, at):
        return ((at["z"] * 2 + at["x"]) * 2 + at["core"]) * self.size["y"] + at["y"]

    def coords(self, i):
        y, wide = i % self.size["y"], i // self.size["y"]
        return {"core": wide % 2, "x": wide // 2 % 2, "z": wide // 4, "y": y}

    def shift(self, value, axis, step=1):
        pairs = []
        for i in range(self.count):
            at = self.coords(i)
            at[axis] = (at[axis] + step) % self.size[axis]
            pairs.append((i, self.index(at)))
        return lax.ppermute(value, AXES, pairs)

    def exchange(self, value, *flips):
        pairs = []
        for i in range(self.count):
            at = self.coords(i)
            for axis, bit in flips[at["core"] % len(flips)].items():
                at[axis] ^= bit
            pairs.append((i, self.index(at)))
        return lax.ppermute(value, AXES, pairs)


CORE, NEAR, FAR = {"core": 1}, {"z": 1}, {"z": 2}
FIRST, SECOND = ({"x": 1}, {"y": 1}), ({"y": 1}, {"x": 1})


def dot(a, b):
    return lax.dot_general(a, b, (((1,), (0,)), ((), ())), preferred_element_type=F32)


def dot_nt(a, b):
    return lax.dot_general(a, b, (((1,), (1,)), ((), ())), preferred_element_type=F32)


def gelu_both(z):
    z2 = z * z
    t = jnp.tanh(z * (GELU_C + (GELU_C * GELU_A) * z2))
    w = 0.5 * t + 0.5
    h = z * w
    return h, w + (h - h * w) * (2.0 * GELU_C + (6.0 * GELU_C * GELU_A) * z2)


def rows_sum8(x):
    rows, cols = x.shape
    return jnp.sum(x.reshape(rows // 8, 8, cols), axis=0)


def picker(lay, rows, cols, first, per, length, width):
    r = lax.broadcasted_iota(jnp.int32, (rows, cols), 0)
    c = lax.broadcasted_iota(jnp.int32, (rows, cols), 1)
    i, t = c // lay.small, c % lay.small - first
    hit = (t >= 0) & (t < per) & (r == (i * length) // width + t)
    return jnp.where(hit, 1.0, 0.0).astype(BF16)


def unpack_small(lay, frames_ref, vec_ref, sc_ref, st_ref):
    count = lay.count * lay.small
    ms = picker(lay, RMAX, count, 0, lay.sp_rows, lay.sp_shard, P_SIZE)
    mv = picker(lay, VPAD, count, lay.sp_rows, lay.vec_rows, lay.vec_shard, 128)
    sp = dot(ms, frames_ref[:, 0:384])
    vec = dot(mv, frames_ref[:, 0:128])
    for r in range(VROWS):
        vec_ref[:, r * 128 : (r + 1) * 128] = vec[r : r + 1, :]
    row = lax.broadcasted_iota(jnp.int32, (RMAX, RMAX), 0)
    col = lax.broadcasted_iota(jnp.int32, (RMAX, RMAX), 1)
    inside = (row < P_SIZE) & (col < P_SIZE)
    sp = sp[:, 0:RMAX]
    sp_t = jnp.transpose(sp)
    sc_ref[...] = jnp.where(inside, sp, jnp.where((col == P_SIZE) & (row < P_SIZE), sp_t, 0.0)).astype(BF16)
    if st_ref is not None:
        st_ref[...] = jnp.where(inside, sp_t, 0.0).astype(BF16)


def role_blocks(lay, me, sign):
    for who in range(2):
        role = me["core"] ^ who
        for second in range(2):
            for first, k1, k2, core in np.ndindex(2, 2, 2, 2):
                swap = role * (first ^ second)
                at = {"z": me["z"] ^ (k1 + 2 * k2), "core": role ^ core, "x": me["x"] ^ first ^ swap, "y": me["y"] ^ second ^ swap}
                yield who, second, (first, k1, k2, core), role, lay.index(at)


def both_blocks(lay, me, sign):
    for who in range(2):
        role = me["core"] ^ who
        for k1 in range(2):
            for second, k2, first in np.ndindex(2, 2, 2):
                swap = role * (first ^ second)
                at = {"z": me["z"] ^ (k1 + 2 * k2), "core": role, "x": me["x"] ^ first ^ swap, "y": me["y"] ^ second ^ swap}
                yield who, k1, (second, k2, first), lay.index(at)


def sixteen(start):
    return pl.ds(pl.multiple_of(start, 16), 16)


def assemble(lay, me, given, win_ref, wout_ref, frames_ref):
    for who, second, place, role, i in role_blocks(lay, me, -1):
        src = given["t%d%d" % (who, second)]
        for t in range(2):
            win_ref[2 * role + t, sixteen(i * 16), :] = src[place + (slice(16 * t, 16 * t + 16),)]
        wout_ref[sixteen(i * 48 + 16 * role), :] = src[place + (slice(32, 48),)]
    for who, z, place, i in both_blocks(lay, me, -1):
        src = given["b%d%d" % (who, z)]
        for t in range(2):
            win_ref[4 + t, sixteen(i * 16), :] = src[place + (slice(16 * t, 16 * t + 16),)]
        wout_ref[sixteen(i * 48 + 32), :] = src[place + (slice(32, 48),)]
        frames_ref[sixteen(i * 16), :] = src[place + (slice(48, 64),)]


def forward_part(rows, valid, r_ref, vec_ref, win_ref, wout_ref, sc_ref, sv, save):
    h, hp = sv["h"], sv["hp"]
    r, k, xh, a = first_norm(rows, valid, r_ref, vec_ref)
    tot = jnp.zeros((rows, 1), F32)
    for j in list(range(NG, NH)) + list(range(NG)):
        z = dot(a, win_ref[j]) + vec_ref[:, O_INB + j * CW : O_INB + (j + 1) * CW]
        h[j], hpj = gelu_both(z)
        hp[j] = hpj
        if j >= NG:
            tot = tot + jnp.sum(h[j], axis=1, keepdims=True)
    mu2 = tot * (1.0 / G)
    ssq = jnp.zeros((rows, 1), F32)
    for j in range(NG):
        vc = h[NG + j] - mu2
        ssq = ssq + jnp.sum(vc * vc, axis=1, keepdims=True)
    k2 = lax.rsqrt(ssq * (1.0 / G) + EPS)
    one = jnp.where(lax.broadcasted_iota(jnp.int32, (rows, 1), 0) == P_SIZE, 1.0, 0.0)
    for j in range(NG):
        lo = j * CW
        xh2 = (h[NG + j] - mu2) * k2
        sv["v"][j] = xh2.astype(sv["v"].dtype)
        sv["hv"][j] = (hp[NG + j] * k2).astype(sv["hv"].dtype)
        q = xh2 * vec_ref[:, O_LN2G + lo : O_LN2G + lo + CW] + vec_ref[:, O_LN2S + lo : O_LN2S + lo + CW]
        sv["q"][j] = jnp.where(valid, q, one).astype(BF16)
    o = None
    for j in range(NG):
        s = dot(sc_ref[...], sv["q"][j])
        u = h[j]
        e = (u * s).astype(BF16)
        sv["sh"][j] = (hp[j] * s).astype(sv["sh"].dtype)
        sv["e"][j] = e
        if save:
            sv["u"][j] = u.astype(BF16)
        part = dot(e, wout_ref[j * CW : (j + 1) * CW, :])
        o = part if o is None else o + part
    o = jnp.where(valid, r + (o + vec_ref[:, O_OUTB : O_OUTB + D]), 0.0)
    return (k, xh, a), o


def first_norm(rows, valid, r_ref, vec_ref):
    r = jnp.where(valid, r_ref[0, 0:rows, :].astype(F32), 0.0)
    mu = jnp.mean(r, axis=1, keepdims=True)
    c = r - mu
    k = lax.rsqrt(jnp.mean(c * c, axis=1, keepdims=True) + EPS)
    xh = c * k
    a = (xh * vec_ref[:, O_LN1G : O_LN1G + D] + vec_ref[:, O_LN1S : O_LN1S + D]).astype(BF16)
    return r, k, xh, a


def backward_part(rows, valid, norm, dn_ref, vec_ref, win_ref, wout_ref, st_ref, sv, acc):
    k, xh, a = norm
    sv["xh1"][0:rows, :] = xh
    sv["at"][0:D, 0:rows] = jnp.transpose(a)
    dn = jnp.where(valid, dn_ref[0, 0:rows, :].astype(F32), 0.0)
    do = dn.astype(BF16)
    dot_t = jnp.transpose(do)
    gvec = acc["vec"]
    gvec[:, O_OUTB : O_OUTB + D] += rows_sum8(do.astype(F32))
    for j in range(NG):
        acc["wout"][j] += dot(dot_t, sv["e"][j, 0:rows, :])
        de = dot_nt(do, wout_ref[j * CW : (j + 1) * CW, :])
        sv["dz"][j, 0:rows, :] = (de * sv["sh"][j].astype(F32)).astype(BF16)
        sv["ds"][j, 0:rows, :] = (de * sv["u"][j].astype(F32)).astype(BF16)
    gs = None
    for j in range(NG):
        part = dot_nt(sv["ds"][j, 0:rows, :], sv["q"][j, 0:rows, :])
        gs = part if gs is None else gs + part
    acc["sp"][...] += gs
    m1 = jnp.zeros((rows, 1), F32)
    m2 = jnp.zeros((rows, 1), F32)
    for j in range(NG):
        lo = j * CW
        dq = jnp.where(valid, dot(st_ref[...], sv["ds"][j, 0:rows, :]), 0.0)
        sv["dq"][j, 0:rows, :] = dq
        gain = vec_ref[:, O_LN2G + lo : O_LN2G + lo + CW]
        w = dq * sv["v"][j].astype(F32)
        gvec[:, O_LN2G + lo : O_LN2G + lo + CW] += rows_sum8(w)
        gvec[:, O_LN2S + lo : O_LN2S + lo + CW] += rows_sum8(dq)
        m1 = m1 + jnp.sum(dq * gain, axis=1, keepdims=True)
        m2 = m2 + jnp.sum(w * gain, axis=1, keepdims=True)
    m1 = m1 * (1.0 / G)
    m2 = m2 * (1.0 / G)
    for j in range(NG):
        lo = j * CW
        gain = vec_ref[:, O_LN2G + lo : O_LN2G + lo + CW]
        dv = (sv["dq"][j, 0:rows, :] * gain - m1 - sv["v"][j].astype(F32) * m2)
        sv["dz"][NG + j, 0:rows, :] = (dv * sv["hv"][j].astype(F32)).astype(BF16)
    da = None
    for j in range(NH):
        dz = sv["dz"][j, 0:rows, :]
        acc["win"][j] += dot(sv["at"][0:D, 0:rows], dz)
        gvec[:, O_INB + j * CW : O_INB + (j + 1) * CW] += rows_sum8(dz.astype(F32))
        part = dot_nt(dz, win_ref[j])
        da = part if da is None else da + part
    xh = sv["xh1"][0:rows, :]
    gain = vec_ref[:, O_LN1G : O_LN1G + D]
    w = da * xh
    gvec[:, O_LN1G : O_LN1G + D] += rows_sum8(w)
    gvec[:, O_LN1S : O_LN1S + D] += rows_sum8(da)
    t = da * gain
    mt = jnp.mean(t, axis=1, keepdims=True)
    mx = jnp.mean(w * gain, axis=1, keepdims=True)
    return dn + k * (t - mt - xh * mx)


def gather_grads(lay, acc, wout_ref, frames_ref):
    for j in range(NG):
        wout_ref[j * CW : (j + 1) * CW, :] = jnp.transpose(acc["wout"][j]).astype(BF16)
    whole = acc["sp"][...]
    row = lax.broadcasted_iota(jnp.int32, (RMAX, RMAX), 0)
    col = lax.broadcasted_iota(jnp.int32, (RMAX, RMAX), 1)
    ext = jnp.where(row == P_SIZE, jnp.transpose(whole), jnp.where(row < P_SIZE, whole, 0.0))
    ext = jnp.where(col < P_SIZE, ext, 0.0).astype(BF16)
    sums = jnp.sum(acc["vec"][...], axis=0, keepdims=True)
    vec = jnp.concatenate([sums[:, r * 128 : (r + 1) * 128] for r in range(VROWS)] + [jnp.zeros((VPAD - VROWS, 128), F32)], axis=0)
    count = lay.count * lay.small
    ms = picker(lay, RMAX, count, 0, lay.sp_rows, lay.sp_shard, P_SIZE)
    mv = picker(lay, VPAD, count, lay.sp_rows, lay.vec_rows, lay.vec_shard, 128)
    tn = (((0,), (0,)), ((), ()))
    frames_ref[...] = jnp.zeros(frames_ref.shape, BF16)
    frames_ref[:, 0:RMAX] = lax.dot_general(ms, ext, tn, preferred_element_type=F32).astype(BF16)
    part = lax.dot_general(mv, vec.astype(BF16), tn, preferred_element_type=F32)
    frames_ref[:, 0:128] += part.astype(BF16)


def scatter_grads(lay, me, acc, wout_ref, frames_ref, staged, out, sems):
    def send(k):
        return pltpu.make_async_copy(staged[PIECES[k]], out[PIECES[k]], sems.at[k])

    for who, second, place, role, i in role_blocks(lay, me, 1):
        dst = staged["t%d%d" % (who, second)]
        for t in range(2):
            dst[place + (slice(16 * t, 16 * t + 16),)] = acc["win"][2 * role + t, sixteen(i * 16), :].astype(BF16)
        dst[place + (slice(32, 48),)] = wout_ref[sixteen(i * 48 + 16 * role), :]
        if place == (1, 1, 1, 1):
            send(2 * who + second).start()
    for who, z, place, i in both_blocks(lay, me, 1):
        dst = staged["b%d%d" % (who, z)]
        for t in range(2):
            dst[place + (slice(16 * t, 16 * t + 16),)] = acc["win"][4 + t, sixteen(i * 16), :].astype(BF16)
        dst[place + (slice(32, 48),)] = wout_ref[sixteen(i * 48 + 32), :]
        dst[place + (slice(48, 64),)] = frames_ref[sixteen(i * 16), :]
        if place == (1, 1, 1):
            send(4 + 2 * who + z).start()
    for k in range(len(PIECES)):
        send(k).wait()


def read_me(info_ref, images):
    return {axis: info_ref[images + k] for k, axis in enumerate(("core", "x", "z", "y"))}


class Names:
    def __init__(self, refs):
        self.refs = list(refs)

    def take(self, names):
        got = dict(zip(names, self.refs))
        self.refs = self.refs[len(names) :]
        return got


WEIGHTS = ("win", "wout", "frames")
SAVED = ("u", "sh", "v", "hv", "q", "e")


def kernel_body(lay, images, mode, scratch_names, info_ref, *refs):
    names = Names(refs)
    given = names.take(weight_names(lay))
    r_ref = names.take(["r"])["r"]
    saved = names.take(SAVED) if mode == "back" else {}
    dn_ref = names.take(["dn"])["dn"] if mode != "fore" else None
    out_ref = names.take(["out"])["out"] if mode != "back" else None
    if mode == "fore":
        saved = names.take(SAVED)
    gr_ref = names.take(["gr"])["gr"] if mode != "fore" else None
    grad_refs = names.take(grad_names(lay)) if mode != "fore" else {}
    sv = names.take(scratch_names)
    w = sv if lay.native else given
    sv.update({k: saved[k].at[0] for k in saved})
    if mode == "both":
        sv.update(u=sv["h"], sh=sv["hp"], v=sv["h"].at[NG:NH], hv=sv["hp"].at[NG:NH])
    acc = {k: sv.get("a" + k) for k in ("win", "wout", "sp", "vec")}
    b = pl.program_id(0)

    @pl.when(b == 0)
    def _():
        if lay.native:
            assemble(lay, read_me(info_ref, images), given, w["win"], w["wout"], w["frames"])
        unpack_small(lay, w["frames"], sv["vec"], sv["sc"], sv.get("st"))
        if mode != "fore":
            for ref in acc.values():
                ref[...] = jnp.zeros(ref.shape, F32)

    cls = info_ref[b]
    n = jnp.where(cls == 0, COUNTS[0], jnp.where(cls == 1, COUNTS[1], COUNTS[2]))
    valid = lax.broadcasted_iota(jnp.int32, (RMAX, 1), 0) < n
    if mode == "back":
        _, k, xh, a = first_norm(RMAX, valid, r_ref, sv["vec"])
        norm = (k, xh, a)
    else:
        norm, o = forward_part(RMAX, valid, r_ref, sv["vec"], w["win"], w["wout"], sv["sc"], sv, mode == "fore")
        out_ref[0] = o
    if mode != "fore":
        gr_ref[0] = backward_part(RMAX, valid, norm, dn_ref, sv["vec"], w["win"], w["wout"], sv["st"], sv, acc)

        @pl.when(b == pl.num_programs(0) - 1)
        def _():
            if lay.native:
                gather_grads(lay, acc, w["wout"], w["frames"])
                staged = {p: sv["stage_" + p] for p in PIECES}
                scatter_grads(lay, read_me(info_ref, images), acc, w["wout"], w["frames"], staged, grad_refs, sv["sems"])
            else:
                gather_grads(lay, acc, grad_refs["gwout"], grad_refs["gframes"])
                grad_refs["gwin"][...] = acc["win"][...].astype(BF16)


def piece_shape(lay, piece):
    return ((2, 2, 2, 2) if piece[0] == "t" else (2, 2, 2)) + (lay.part_rows("a" if piece[0] == "t" else "b"), CW)


def scratch_for(lay, mode):
    big = lambda m, dt: pltpu.VMEM((m, RMAX, CW), dt)
    wide = lambda dt: pltpu.VMEM((RMAX, D), dt)
    made = {}
    if lay.native:
        made.update(win=pltpu.VMEM((NH, D, CW), BF16), wout=pltpu.VMEM((G, D), BF16), frames=pltpu.VMEM((lay.count * lay.small, CW), BF16))
    if lay.native and mode != "fore":
        for p in PIECES:
            made["stage_" + p] = pltpu.VMEM(piece_shape(lay, p), BF16)
        made["sems"] = pltpu.SemaphoreType.DMA((len(PIECES),))
    made.update(vec=pltpu.VMEM((1, VUSED), F32), sc=pltpu.VMEM((RMAX, RMAX), BF16))
    if mode != "back":
        made.update(h=big(NH, F32), hp=big(NH, F32))
    if mode == "both":
        made.update(q=big(NG, BF16), e=big(NG, BF16))
    if mode != "fore":
        made.update(st=pltpu.VMEM((RMAX, RMAX), BF16), ds=big(NG, BF16), dz=big(NH, BF16), dq=big(NG, F32), xh1=wide(F32))
        made.update(at=pltpu.VMEM((D, RMAX), BF16), awin=pltpu.VMEM((NH, D, CW), F32), awout=pltpu.VMEM((NG, D, CW), F32))
        made.update(asp=pltpu.VMEM((RMAX, RMAX), F32), avec=pltpu.VMEM((8, VUSED), F32))
    return made


def weight_names(lay):
    if not lay.native:
        return list(WEIGHTS)
    return list(PIECES)


def grad_names(lay):
    return list(PIECES) if lay.native else ["gwin", "gwout", "gframes"]


def image_spec():
    return pl.BlockSpec((1, RMAX, D), lambda b, c: (b, 0, 0))


def saved_shapes(images):
    return [jax.ShapeDtypeStruct((images, NG, RMAX, CW), BF16) for _ in SAVED]


def saved_specs():
    spec = pl.BlockSpec((1, NG, RMAX, CW), lambda b, c: (b, 0, 0, 0))
    return [spec] * len(SAVED)


def run_kernel(lay, mode, info, weights, r, saved=None, dn=None):
    images = r.shape[0]
    image = jax.ShapeDtypeStruct((images, RMAX, D), F32)
    whole = pl.BlockSpec(memory_space=pltpu.VMEM)
    operands = list(weights) + [r]
    in_specs = [whole] * len(weights) + [image_spec()]
    outs, out_specs = [], []
    if mode == "back":
        operands += list(saved)
        in_specs += saved_specs()
    if mode != "fore":
        operands.append(dn)
        in_specs.append(image_spec())
    if mode != "back":
        outs.append(image)
        out_specs.append(image_spec())
    if mode == "fore":
        outs += saved_shapes(images)
        out_specs += saved_specs()
    if mode != "fore":
        outs.append(image)
        out_specs.append(image_spec())
        if lay.native:
            grads = [piece_shape(lay, p) for p in PIECES]
        else:
            grads = [(NH, D, CW), (G, D), (lay.count * lay.small, CW)]
        outs += [jax.ShapeDtypeStruct(s, BF16) for s in grads]
        out_specs += [pl.BlockSpec(memory_space=pl.ANY) if lay.native else whole] * len(grads)
    scratch = scratch_for(lay, mode)
    return pl.pallas_call(
        functools.partial(kernel_body, lay, images, mode, list(scratch)),
        grid_spec=pltpu.PrefetchScalarGridSpec(
            num_scalar_prefetch=1, grid=(images,), in_specs=in_specs, out_specs=out_specs, scratch_shapes=list(scratch.values())
        ),
        out_shape=outs,
        compiler_params=pltpu.CompilerParams(vmem_limit_bytes=VLIM[mode if lay.native else "plain"]),
        name="layer_" + mode,
    )(info, *operands)


def pack_large(lay, w_in, w_out):
    win = w_in.reshape(lay.rows, NH, CW)
    wout = w_out.reshape(NG, lay.rows, D)
    return [win[:, j] for j in range(NH)] + [wout[k] for k in range(NG)]


def pack_small(lay, spatial, vectors, me):
    index = lay.index(me)
    sp_at = lax.rem(index * lay.sp_shard, P_SIZE)
    vec_at = lax.rem(index * lay.vec_shard, 128)
    sp = lax.dynamic_update_slice(jnp.zeros((lay.sp_rows * P_SIZE,), BF16), spatial, (sp_at,)).reshape(lay.sp_rows, P_SIZE)
    vec = lax.dynamic_update_slice(jnp.zeros((lay.vec_rows * 128,), BF16), vectors, (vec_at,)).reshape(lay.vec_rows, 128)
    sp = jnp.pad(sp, ((0, 0), (0, CW - P_SIZE)))
    vec = jnp.pad(vec, ((0, lay.small - lay.sp_rows - lay.vec_rows), (0, CW - 128)))
    return jnp.concatenate([sp, vec])


def part_of(fields, part):
    return jnp.concatenate([fields[f] for f in PART_FIELDS[part]])


def ring_gather(lay, value, axis):
    pieces = [value]
    for _ in range(lay.size[axis] - 1):
        pieces.append(lay.shift(pieces[-1], axis))
    return pieces


def hold(*values):
    return lax.optimization_barrier(values)


def move(lay, *items):
    values = hold(*[value for value, _ in items])
    return hold(*[lay.exchange(value, *flips) for value, (_, flips) in zip(values, items)])


def gather_start(lay, packed, me):
    even = me["core"] == 0
    keep = jnp.where(even, packed["a"], packed["d"])
    give = jnp.where(even, packed["d"], packed["a"])
    return jnp.stack([keep, lay.exchange(give, CORE)])


GATHER_T = ((FAR,), (NEAR,), FIRST, SECOND)
GATHER_B = (FIRST, (FAR,), SECOND, (NEAR,))


def gather_plain(lay, packed, me):
    win, wout, frames = [None] * NH, [None] * NG, None
    for p in PARTS:
        dims = ("core",) + PART_DIMS[p]
        value = packed[p]
        for axis in reversed(dims):
            value = jnp.stack(ring_gather(lay, value, axis))
        for k, axis in enumerate(dims):
            n = lay.size[axis]
            value = jnp.take(value, lax.rem(me[axis] - jnp.arange(n) + n, n), axis=k)
        order = [dims.index(a) for a in ("z", "x", "core", "y")]
        value = value.transpose(order + [4, 5]).reshape(lay.count, lay.part_rows(p), CW)
        for f, at in lay.offsets(p):
            if f < 6:
                win[f] = value[:, at : at + lay.rows].reshape(D, CW)
            elif f < 9:
                wout[f - 6] = value[:, at : at + lay.rows]
            else:
                frames = value[:, at : at + lay.small].reshape(lay.count * lay.small, CW)
    return [jnp.stack(win), jnp.stack(wout, axis=1).reshape(G, D), frames]


def ring_scatter(lay, value, axis):
    n = lay.size[axis]
    total = value[n - 1].astype(F32)
    for k in range(n - 2, -1, -1):
        total = lay.shift(total.astype(BF16), axis).astype(F32) + value[k].astype(F32)
    return total


def low(v):
    return v.astype(BF16)


def add(mine, got):
    return mine.astype(F32) + got.astype(F32)


def scatter_core(lay, grads):
    t00, t01, t10, t11, b00, b01, b10, b11 = grads
    t11, b11 = move(lay, (t11, (CORE,)), (b11, (CORE,)))
    far, bfar = hold(low(add(t01, t11)), low(add(b01, b11)))
    t10, b10, far, bfar = hold(t10, b10, far, bfar)
    return far, bfar, (t00, lay.exchange(t10, CORE)), (b00, lay.exchange(b10, CORE))


SCATTER_T = (SECOND, FIRST, (NEAR,), (FAR,))
SCATTER_B = ((NEAR,), SECOND, (FAR,), FIRST)


def scatter_end(me, top, other, b):
    even = me["core"] == 0
    return {"a": jnp.where(even, top[0], other), "d": jnp.where(even, other, top[0]), "b": b}


def native_path(lay, me, size_class, params, patches, cotangent):
    stack = lambda v, got: jnp.stack([v, got])
    info = size_class
    w_in, w_out, spatial, vectors = params
    large = pack_large(lay, w_in[0], w_out[0])
    t0 = gather_start(lay, {p: part_of(large, p) for p in "ad"}, me)
    t0, spatial, vectors, w_in, w_out = hold(t0, spatial, vectors, w_in, w_out)
    x = lay.exchange(t0, *GATHER_T[0])
    b0 = part_of(large + [pack_small(lay, spatial[0], vectors[0], me)], "b")
    y = lay.exchange(b0, *GATHER_B[0])
    x, y, w_in, w_out, spatial, vectors = hold(x, y, w_in, w_out, spatial, vectors)
    large = pack_large(lay, w_in[1], w_out[1])
    t1 = gather_start(lay, {p: part_of(large, p) for p in "ad"}, me)
    b1 = part_of(large + [pack_small(lay, spatial[1], vectors[1], me)], "b")
    t0, b0, patches, cotangent, info = hold(stack(t0, x), stack(b0, y), patches, cotangent, info)
    for k in (1, 2):
        x, y = lay.exchange(t0, *GATHER_T[k]), lay.exchange(b0, *GATHER_B[k])
        u, v = lay.exchange(t1, *GATHER_T[k - 1]), lay.exchange(b1, *GATHER_B[k - 1])
        if k == 1:
            info, patches, cotangent = describe(me, info), spread(patches), spread(cotangent)
        x, y, u, v, patches, cotangent, info = hold(x, y, u, v, patches, cotangent, info)
        t0, b0, t1, b1 = hold(stack(t0, x), stack(b0, y), stack(t1, u), stack(b1, v))
    t0c, b0c = lay.exchange(t0, CORE), lay.exchange(b0, CORE)
    x, y, u, v = [lay.exchange(g, *f) for g, f in ((t0, SECOND), (b0, (NEAR,)), (t1, FIRST), (b1, SECOND))]
    x, y, u, v = hold(x, y, u, v)
    weights0 = [t0, x, t0c, lay.exchange(x, CORE), b0, y, b0c, lay.exchange(y, CORE)]
    t1, b1 = stack(t1, u), stack(b1, v)
    *weights0, t1, b1 = hold(*weights0, t1, b1)
    x, y, t1c, b1c = [lay.exchange(v, *f) for v, f in ((t1, SECOND), (b1, (NEAR,)), (t1, (CORE,)), (b1, (CORE,)))]
    hidden, *saved = run_kernel(lay, "fore", info, weights0, patches)
    x, y, t1c, b1c, hidden = hold(x, y, t1c, b1c, hidden)
    weights1 = [t1, x, t1c, lay.exchange(x, CORE), b1, y, b1c, lay.exchange(y, CORE)]
    outputs, grad, *grads1 = run_kernel(lay, "both", info, weights1, hidden, dn=cotangent)

    far1, bfar1, near1, bnear1 = scatter_core(lay, grads1)
    far1, bfar1, grad = hold(far1, bfar1, grad)
    x, y = lay.exchange(far1, *SECOND), lay.exchange(bfar1, NEAR)
    patch_grad, *grads0 = run_kernel(lay, "back", info, weights0, patches, saved=saved, dn=grad)
    x, y, patch_grad, outputs, *grads0 = hold(x, y, patch_grad, outputs, *grads0)
    top1, b1 = add(add(*near1), x), add(add(*bnear1), y)
    u, v = lay.exchange(low(top1[1]), *SCATTER_T[1]), lay.exchange(low(b1[1]), *SCATTER_B[1])
    far0, bfar0, near0, bnear0 = scatter_core(lay, grads0)
    far0, bfar0, outputs, patch_grad = hold(far0, bfar0, outputs, patch_grad)
    x, y = lay.exchange(far0, *SECOND), lay.exchange(bfar0, NEAR)
    x, y, u, v, outputs, patch_grad = hold(x, y, u, v, tilt(outputs), tilt(patch_grad))
    top1, b1 = add(top1[0], u), add(b1[0], v)
    top0, b0 = add(add(*near0), x), add(add(*bnear0), y)
    for k in (1, 2):
        sends = [(low(v[1]), f) for v, f in ((top0, SCATTER_T[k]), (b0, SCATTER_B[k]), (top1, SCATTER_T[k + 1]), (b1, SCATTER_B[k + 1]))]
        x, y, u, v = move(lay, *sends)
        top0, b0, top1, b1 = add(top0[0], x), add(b0[0], y), add(top1[0], u), add(b1[0], v)
    last1 = lay.exchange(top1[1], CORE)
    x, y = move(lay, (low(top0[1]), SCATTER_T[3]), (low(b0[1]), SCATTER_B[3]))
    top0, b0 = add(top0[0], x), add(b0[0], y)
    last0 = lay.exchange(top0[1], CORE)
    outputs, patch_grad = outputs.transpose(1, 0, 2), patch_grad.transpose(1, 0, 2)
    return outputs, patch_grad, scatter_end(me, top0, last0, b0), scatter_end(me, top1, last1, b1)


def tilt(v):
    return v[:, :P_SIZE].transpose(1, 0, 2)


def describe(me, size_class):
    return jnp.concatenate([size_class, jnp.stack([me[a] for a in ("core", "x", "z", "y")]).astype(jnp.int32)])


def spread(v):
    return jnp.pad(v, ((0, 0), (0, RMAX - P_SIZE), (0, 0)))


def plain_path(lay, me, size_class, params, patches, cotangent):
    packed = []
    for w_in, w_out, spatial, vectors in zip(*params):
        fields = pack_large(lay, w_in, w_out) + [pack_small(lay, spatial, vectors, me)]
        packed.append({p: part_of(fields, p) for p in PARTS})
    info, patches, cotangent = describe(me, size_class), spread(patches), spread(cotangent)
    weights0, weights1 = [gather_plain(lay, p, me) for p in packed]
    hidden, *saved = run_kernel(lay, "fore", info, weights0, patches)
    outputs, grad, *grads1 = run_kernel(lay, "both", info, weights1, hidden, dn=cotangent)
    patch_grad, *grads0 = run_kernel(lay, "back", info, weights0, patches, saved=saved, dn=grad)
    outputs, patch_grad = outputs[:, :P_SIZE], patch_grad[:, :P_SIZE]
    return outputs, patch_grad, scatter_plain(lay, grads0, me), scatter_plain(lay, grads1, me)


def scatter_plain(lay, grads, me):
    gwin, gwout, gframes = grads
    gwin = gwin.reshape(NH, lay.count, lay.rows, CW)
    gwout = gwout.reshape(lay.count, NG, lay.rows, D)
    gframes = gframes.reshape(lay.count, lay.small, CW)
    fields = [gwin[j] for j in range(NH)] + [gwout[:, k] for k in range(NG)] + [gframes]
    result = {}
    for p in PARTS:
        dims = ("core",) + PART_DIMS[p]
        value = jnp.concatenate([fields[f] for f in PART_FIELDS[p]], axis=1)
        value = value.reshape(lay.size["z"], 2, 2, lay.size["y"], lay.part_rows(p), CW)
        value = value.transpose([("z", "x", "core", "y").index(a) for a in dims] + [4, 5])
        for k, axis in enumerate(dims):
            n = lay.size[axis]
            value = jnp.take(value, lax.rem(me[axis] + jnp.arange(n), n), axis=k)
        for axis in dims:
            value = ring_scatter(lay, value, axis)
        result[p] = value
    return result


def unpack_grads(lay, mine, me, sp_len, vec_len):
    fields = {f: mine[p][at : at + (lay.small if f == 9 else lay.rows)] for p in PARTS for f, at in lay.offsets(p)}
    index = lay.index(me)
    gwin = jnp.stack([fields[j] for j in range(NH)], axis=1).reshape(-1)
    gwout = jnp.concatenate([fields[6 + k] for k in range(NG)]).reshape(-1)
    sp = fields[9][0 : lay.sp_rows, 0:P_SIZE].reshape(-1)
    sp = lax.dynamic_slice(sp, (lax.rem(index * lay.sp_shard, P_SIZE),), (lay.sp_shard,))
    vec = fields[9][lay.sp_rows : lay.sp_rows + lay.vec_rows, 0:128].reshape(-1)
    vec = lax.dynamic_slice(vec, (lax.rem(index * lay.vec_shard, 128),), (lay.vec_shard,))
    return gwin, gwout, sp, vec


def per_device(mesh_shape, patches, cotangent, size_class, w_in, w_out, spatial, vectors):
    lay = Layout(mesh_shape, spatial.shape[1], vectors.shape[1])
    wide, narrow = lax.axis_index("wide"), lax.axis_index("narrow")
    me = {"core": lax.rem(wide, 2), "x": lax.rem(wide // 2, 2), "z": wide // 4, "y": narrow}
    params = w_in, w_out, spatial, vectors
    path = native_path if lay.native else plain_path
    outputs, patch_grad, *sums = path(lay, me, size_class, params, patches, cotangent)
    flat = [unpack_grads(lay, s, me, spatial.shape[1], vectors.shape[1]) for s in sums]
    result = [jnp.stack([flat[layer][k] for layer in range(LAYERS)]) for k in range(4)]
    return (outputs, patch_grad, *result)


def solution(mesh):
    shape = (mesh.shape["wide"], mesh.shape["narrow"])
    rows = P(AXES, None, None)
    flat = P(None, AXES)
    return jax.shard_map(
        functools.partial(per_device, shape),
        mesh=mesh,
        in_specs=(rows, rows, P(AXES), flat, flat, flat, flat),
        out_specs=(rows, rows, flat, flat, flat, flat),
        check_vma=False,
    )
```

```python
import functools
import jax
import jax.numpy as jnp
import numpy as np
from jax import lax
from jax.experimental import pallas as pl
from jax.experimental.pallas import tpu as pltpu
from jax.sharding import PartitionSpec as P

D = 512
H = 3072
P_SIZE = 324
LAYERS = 2
G = 1536
EPS = 1e-05
CW = 512
NG = G // CW
NH = H // CW
RMAX = 336
COUNTS = (100, 196, 324)
F32 = jnp.float32
BF16 = jnp.bfloat16
O_LN1G, O_LN1S, O_INB = 0, D, 2 * D
O_LN2G, O_LN2S, O_OUTB = 2 * D + H, 2 * D + H + G, 2 * D + H + 2 * G
VUSED = 3 * D + H + 2 * G
VROWS = VUSED // 128
VPAD = (VROWS + 15) // 16 * 16
GELU_C = 0.7978845608028654
GELU_A = 0.044715
AXES = ("wide", "narrow")
VLIM = {"plain": 60 * 2**20, "fore": 46 * 2**20, "both": 40 * 2**20, "back": 41 * 2**20}
PART_FIELDS = {"a": (0, 1, 6), "d": (2, 3, 7), "b": (4, 5, 8, 9)}
PART_DIMS = {"a": ("y", "x", "z"), "d": ("x", "y", "z"), "b": ("z", "y", "x")}
PARTS = ("a", "d", "b")
KEPT = ("fore", "both", "back")
PIECES = ("t00", "t01", "t10", "t11", "b00", "b01", "b10", "b11")


class Layout:
    def __init__(self, mesh_shape, sp_shard, vec_shard):
        wide, narrow = mesh_shape
        self.size = {"core": 2, "x": 2, "z": wide // 4, "y": narrow}
        self.count = wide * narrow
        self.rows = D // self.count
        self.sp_shard, self.vec_shard = sp_shard, vec_shard
        self.sp_rows = (sp_shard + 2 * P_SIZE - 2) // P_SIZE
        self.vec_rows = (vec_shard + 2 * 128 - 2) // 128
        self.native = self.rows == 16 and narrow == 2 and wide == 16
        self.small = (self.sp_rows + self.vec_rows + 7) // 8 * 8

    def part_rows(self, part):
        return sum(self.small if f == 9 else self.rows for f in PART_FIELDS[part])

    def offsets(self, part):
        spots, at = [], 0
        for f in PART_FIELDS[part]:
            spots.append((f, at))
            at += self.small if f == 9 else self.rows
        return spots

    def index(self, at):
        return ((at["z"] * 2 + at["x"]) * 2 + at["core"]) * self.size["y"] + at["y"]

    def coords(self, i):
        y, wide = i % self.size["y"], i // self.size["y"]
        return {"core": wide % 2, "x": wide // 2 % 2, "z": wide // 4, "y": y}

    def shift(self, value, axis, step=1):
        pairs = []
        for i in range(self.count):
            at = self.coords(i)
            at[axis] = (at[axis] + step) % self.size[axis]
            pairs.append((i, self.index(at)))
        return lax.ppermute(value, AXES, pairs)

    def exchange(self, value, *flips):
        pairs = []
        for i in range(self.count):
            at = self.coords(i)
            for axis, bit in flips[at["core"] % len(flips)].items():
                at[axis] ^= bit
            pairs.append((i, self.index(at)))
        return lax.ppermute(value, AXES, pairs)


CORE, NEAR, FAR = {"core": 1}, {"z": 1}, {"z": 2}
FIRST, SECOND = ({"x": 1}, {"y": 1}), ({"y": 1}, {"x": 1})


def dot(a, b):
    return lax.dot_general(a, b, (((1,), (0,)), ((), ())), preferred_element_type=F32)


def dot_nt(a, b):
    return lax.dot_general(a, b, (((1,), (1,)), ((), ())), preferred_element_type=F32)


def gelu_both(z):
    z2 = z * z
    t = jnp.tanh(z * (GELU_C + (GELU_C * GELU_A) * z2))
    w = 0.5 * t + 0.5
    h = z * w
    return h, w + (h - h * w) * (2.0 * GELU_C + (6.0 * GELU_C * GELU_A) * z2)


def rows_sum8(x):
    rows, cols = x.shape
    return jnp.sum(x.reshape(rows // 8, 8, cols), axis=0)


def picker(lay, rows, cols, first, per, length, width):
    r = lax.broadcasted_iota(jnp.int32, (rows, cols), 0)
    c = lax.broadcasted_iota(jnp.int32, (rows, cols), 1)
    i, t = c // lay.small, c % lay.small - first
    hit = (t >= 0) & (t < per) & (r == (i * length) // width + t)
    return jnp.where(hit, 1.0, 0.0).astype(BF16)


def unpack_small(lay, frames_ref, vec_ref, sc_ref, st_ref):
    count = lay.count * lay.small
    ms = picker(lay, RMAX, count, 0, lay.sp_rows, lay.sp_shard, P_SIZE)
    mv = picker(lay, VPAD, count, lay.sp_rows, lay.vec_rows, lay.vec_shard, 128)
    sp = dot(ms, frames_ref[:, 0:384])
    vec = dot(mv, frames_ref[:, 0:128])
    for r in range(VROWS):
        vec_ref[:, r * 128 : (r + 1) * 128] = vec[r : r + 1, :]
    row = lax.broadcasted_iota(jnp.int32, (RMAX, RMAX), 0)
    col = lax.broadcasted_iota(jnp.int32, (RMAX, RMAX), 1)
    inside = (row < P_SIZE) & (col < P_SIZE)
    sp = sp[:, 0:RMAX]
    sp_t = jnp.transpose(sp)
    sc_ref[...] = jnp.where(inside, sp, jnp.where((col == P_SIZE) & (row < P_SIZE), sp_t, 0.0)).astype(BF16)
    if st_ref is not None:
        st_ref[...] = jnp.where(inside, sp_t, 0.0).astype(BF16)


def role_blocks(lay, me, sign):
    for who in range(2):
        role = me["core"] ^ who
        for second in range(2):
            for first, k1, k2, core in np.ndindex(2, 2, 2, 2):
                swap = role * (first ^ second)
                at = {"z": me["z"] ^ (k1 + 2 * k2), "core": role ^ core, "x": me["x"] ^ first ^ swap, "y": me["y"] ^ second ^ swap}
                yield who, second, (first, k1, k2, core), role, lay.index(at)


def both_blocks(lay, me, sign):
    for who in range(2):
        role = me["core"] ^ who
        for k1 in range(2):
            for second, k2, first in np.ndindex(2, 2, 2):
                swap = role * (first ^ second)
                at = {"z": me["z"] ^ (k1 + 2 * k2), "core": role, "x": me["x"] ^ first ^ swap, "y": me["y"] ^ second ^ swap}
                yield who, k1, (second, k2, first), lay.index(at)


def sixteen(start):
    return pl.ds(pl.multiple_of(start, 16), 16)


def assemble(lay, me, given, win_ref, wout_ref, frames_ref):
    for who, second, place, role, i in role_blocks(lay, me, -1):
        src = given["t%d%d" % (who, second)]
        for t in range(2):
            win_ref[2 * role + t, sixteen(i * 16), :] = src[place + (slice(16 * t, 16 * t + 16),)]
        wout_ref[sixteen(i * 48 + 16 * role), :] = src[place + (slice(32, 48),)]
    for who, z, place, i in both_blocks(lay, me, -1):
        src = given["b%d%d" % (who, z)]
        for t in range(2):
            win_ref[4 + t, sixteen(i * 16), :] = src[place + (slice(16 * t, 16 * t + 16),)]
        wout_ref[sixteen(i * 48 + 32), :] = src[place + (slice(32, 48),)]
        frames_ref[sixteen(i * 16), :] = src[place + (slice(48, 64),)]


def forward_part(rows, valid, r_ref, vec_ref, win_ref, wout_ref, sc_ref, sv, save):
    h, hp = sv["h"], sv["hp"]
    r, k, xh, a = first_norm(rows, valid, r_ref, vec_ref)
    tot = jnp.zeros((rows, 1), F32)
    for j in list(range(NG, NH)) + list(range(NG)):
        z = dot(a, win_ref[j]) + vec_ref[:, O_INB + j * CW : O_INB + (j + 1) * CW]
        h[j], hpj = gelu_both(z)
        hp[j] = hpj
        if j >= NG:
            tot = tot + jnp.sum(h[j], axis=1, keepdims=True)
    mu2 = tot * (1.0 / G)
    ssq = jnp.zeros((rows, 1), F32)
    for j in range(NG):
        vc = h[NG + j] - mu2
        ssq = ssq + jnp.sum(vc * vc, axis=1, keepdims=True)
    k2 = lax.rsqrt(ssq * (1.0 / G) + EPS)
    one = jnp.where(lax.broadcasted_iota(jnp.int32, (rows, 1), 0) == P_SIZE, 1.0, 0.0)
    for j in range(NG):
        lo = j * CW
        xh2 = (h[NG + j] - mu2) * k2
        sv["v"][j] = xh2.astype(sv["v"].dtype)
        sv["hv"][j] = (hp[NG + j] * k2).astype(sv["hv"].dtype)
        q = xh2 * vec_ref[:, O_LN2G + lo : O_LN2G + lo + CW] + vec_ref[:, O_LN2S + lo : O_LN2S + lo + CW]
        sv["q"][j] = jnp.where(valid, q, one).astype(BF16)
    o = None
    for j in range(NG):
        s = dot(sc_ref[...], sv["q"][j])
        u = h[j]
        e = (u * s).astype(BF16)
        sv["sh"][j] = (hp[j] * s).astype(sv["sh"].dtype)
        sv["e"][j] = e
        if save:
            sv["u"][j] = u.astype(BF16)
        part = dot(e, wout_ref[j * CW : (j + 1) * CW, :])
        o = part if o is None else o + part
    o = jnp.where(valid, r + (o + vec_ref[:, O_OUTB : O_OUTB + D]), 0.0)
    return (k, xh, a), o


def first_norm(rows, valid, r_ref, vec_ref):
    r = jnp.where(valid, r_ref[0, 0:rows, :].astype(F32), 0.0)
    mu = jnp.mean(r, axis=1, keepdims=True)
    c = r - mu
    k = lax.rsqrt(jnp.mean(c * c, axis=1, keepdims=True) + EPS)
    xh = c * k
    a = (xh * vec_ref[:, O_LN1G : O_LN1G + D] + vec_ref[:, O_LN1S : O_LN1S + D]).astype(BF16)
    return r, k, xh, a


def backward_part(rows, valid, norm, dn_ref, vec_ref, win_ref, wout_ref, st_ref, sv, acc):
    k, xh, a = norm
    sv["xh1"][0:rows, :] = xh
    sv["at"][0:D, 0:rows] = jnp.transpose(a)
    dn = jnp.where(valid, dn_ref[0, 0:rows, :].astype(F32), 0.0)
    do = dn.astype(BF16)
    dot_t = jnp.transpose(do)
    gvec = acc["vec"]
    gvec[:, O_OUTB : O_OUTB + D] += rows_sum8(do.astype(F32))
    for j in range(NG):
        acc["wout"][j] += dot(dot_t, sv["e"][j, 0:rows, :])
        de = dot_nt(do, wout_ref[j * CW : (j + 1) * CW, :])
        sv["dz"][j, 0:rows, :] = (de * sv["sh"][j].astype(F32)).astype(BF16)
        sv["ds"][j, 0:rows, :] = (de * sv["u"][j].astype(F32)).astype(BF16)
    gs = None
    for j in range(NG):
        part = dot_nt(sv["ds"][j, 0:rows, :], sv["q"][j, 0:rows, :])
        gs = part if gs is None else gs + part
    acc["sp"][...] += gs
    m1 = jnp.zeros((rows, 1), F32)
    m2 = jnp.zeros((rows, 1), F32)
    for j in range(NG):
        lo = j * CW
        dq = jnp.where(valid, dot(st_ref[...], sv["ds"][j, 0:rows, :]), 0.0)
        sv["dq"][j, 0:rows, :] = dq
        gain = vec_ref[:, O_LN2G + lo : O_LN2G + lo + CW]
        w = dq * sv["v"][j].astype(F32)
        gvec[:, O_LN2G + lo : O_LN2G + lo + CW] += rows_sum8(w)
        gvec[:, O_LN2S + lo : O_LN2S + lo + CW] += rows_sum8(dq)
        m1 = m1 + jnp.sum(dq * gain, axis=1, keepdims=True)
        m2 = m2 + jnp.sum(w * gain, axis=1, keepdims=True)
    m1 = m1 * (1.0 / G)
    m2 = m2 * (1.0 / G)
    for j in range(NG):
        lo = j * CW
        gain = vec_ref[:, O_LN2G + lo : O_LN2G + lo + CW]
        dv = (sv["dq"][j, 0:rows, :] * gain - m1 - sv["v"][j].astype(F32) * m2)
        sv["dz"][NG + j, 0:rows, :] = (dv * sv["hv"][j].astype(F32)).astype(BF16)
    da = None
    for j in range(NH):
        dz = sv["dz"][j, 0:rows, :]
        acc["win"][j] += dot(sv["at"][0:D, 0:rows], dz)
        gvec[:, O_INB + j * CW : O_INB + (j + 1) * CW] += rows_sum8(dz.astype(F32))
        part = dot_nt(dz, win_ref[j])
        da = part if da is None else da + part
    xh = sv["xh1"][0:rows, :]
    gain = vec_ref[:, O_LN1G : O_LN1G + D]
    w = da * xh
    gvec[:, O_LN1G : O_LN1G + D] += rows_sum8(w)
    gvec[:, O_LN1S : O_LN1S + D] += rows_sum8(da)
    t = da * gain
    mt = jnp.mean(t, axis=1, keepdims=True)
    mx = jnp.mean(w * gain, axis=1, keepdims=True)
    return dn + k * (t - mt - xh * mx)


def gather_grads(lay, acc, wout_ref, frames_ref):
    for j in range(NG):
        wout_ref[j * CW : (j + 1) * CW, :] = jnp.transpose(acc["wout"][j]).astype(BF16)
    whole = acc["sp"][...]
    row = lax.broadcasted_iota(jnp.int32, (RMAX, RMAX), 0)
    col = lax.broadcasted_iota(jnp.int32, (RMAX, RMAX), 1)
    ext = jnp.where(row == P_SIZE, jnp.transpose(whole), jnp.where(row < P_SIZE, whole, 0.0))
    ext = jnp.where(col < P_SIZE, ext, 0.0).astype(BF16)
    sums = jnp.sum(acc["vec"][...], axis=0, keepdims=True)
    vec = jnp.concatenate([sums[:, r * 128 : (r + 1) * 128] for r in range(VROWS)] + [jnp.zeros((VPAD - VROWS, 128), F32)], axis=0)
    count = lay.count * lay.small
    ms = picker(lay, RMAX, count, 0, lay.sp_rows, lay.sp_shard, P_SIZE)
    mv = picker(lay, VPAD, count, lay.sp_rows, lay.vec_rows, lay.vec_shard, 128)
    tn = (((0,), (0,)), ((), ()))
    frames_ref[...] = jnp.zeros(frames_ref.shape, BF16)
    frames_ref[:, 0:RMAX] = lax.dot_general(ms, ext, tn, preferred_element_type=F32).astype(BF16)
    part = lax.dot_general(mv, vec.astype(BF16), tn, preferred_element_type=F32)
    frames_ref[:, 0:128] += part.astype(BF16)


def scatter_grads(lay, me, acc, wout_ref, frames_ref, out):
    for who, second, place, role, i in role_blocks(lay, me, 1):
        dst = out["t%d%d" % (who, second)]
        for t in range(2):
            dst[place + (slice(16 * t, 16 * t + 16),)] = acc["win"][2 * role + t, sixteen(i * 16), :].astype(BF16)
        dst[place + (slice(32, 48),)] = wout_ref[sixteen(i * 48 + 16 * role), :]
    for who, z, place, i in both_blocks(lay, me, 1):
        dst = out["b%d%d" % (who, z)]
        for t in range(2):
            dst[place + (slice(16 * t, 16 * t + 16),)] = acc["win"][4 + t, sixteen(i * 16), :].astype(BF16)
        dst[place + (slice(32, 48),)] = wout_ref[sixteen(i * 48 + 32), :]
        dst[place + (slice(48, 64),)] = frames_ref[sixteen(i * 16), :]


def read_me(info_ref, images):
    return {axis: info_ref[images + k] for k, axis in enumerate(("core", "x", "z", "y"))}


class Names:
    def __init__(self, refs):
        self.refs = list(refs)

    def take(self, names):
        got = dict(zip(names, self.refs))
        self.refs = self.refs[len(names) :]
        return got


WEIGHTS = ("win", "wout", "frames")
SAVED = ("u", "sh", "v", "hv", "q", "e")


def kernel_body(lay, images, mode, scratch_names, info_ref, *refs):
    names = Names(refs)
    given = names.take(weight_names(lay))
    r_ref = names.take(["r"])["r"]
    saved = names.take(SAVED) if mode == "back" else {}
    dn_ref = names.take(["dn"])["dn"] if mode != "fore" else None
    out_ref = names.take(["out"])["out"] if mode != "back" else None
    if mode == "fore":
        saved = names.take(SAVED)
    gr_ref = names.take(["gr"])["gr"] if mode != "fore" else None
    grad_refs = names.take(grad_names(lay)) if mode != "fore" else {}
    sv = names.take(scratch_names)
    w = sv if lay.native else given
    sv.update({k: saved[k].at[0] for k in saved})
    if mode == "both":
        sv.update(u=sv["h"], sh=sv["hp"], v=sv["h"].at[NG:NH], hv=sv["hp"].at[NG:NH])
    acc = {k: sv.get("a" + k) for k in ("win", "wout", "sp", "vec")}
    b = pl.program_id(0)

    @pl.when(b == 0)
    def _():
        if lay.native:
            assemble(lay, read_me(info_ref, images), given, w["win"], w["wout"], w["frames"])
        unpack_small(lay, w["frames"], sv["vec"], sv["sc"], sv.get("st"))
        if mode != "fore":
            for ref in acc.values():
                ref[...] = jnp.zeros(ref.shape, F32)

    cls = info_ref[b]
    n = jnp.where(cls == 0, COUNTS[0], jnp.where(cls == 1, COUNTS[1], COUNTS[2]))
    valid = lax.broadcasted_iota(jnp.int32, (RMAX, 1), 0) < n
    if mode == "back":
        _, k, xh, a = first_norm(RMAX, valid, r_ref, sv["vec"])
        norm = (k, xh, a)
    else:
        norm, o = forward_part(RMAX, valid, r_ref, sv["vec"], w["win"], w["wout"], sv["sc"], sv, mode == "fore")
        out_ref[0] = o
    if mode != "fore":
        gr_ref[0] = backward_part(RMAX, valid, norm, dn_ref, sv["vec"], w["win"], w["wout"], sv["st"], sv, acc)

        @pl.when(b == pl.num_programs(0) - 1)
        def _():
            if lay.native:
                gather_grads(lay, acc, w["wout"], w["frames"])
                scatter_grads(lay, read_me(info_ref, images), acc, w["wout"], w["frames"], grad_refs)
            else:
                gather_grads(lay, acc, grad_refs["gwout"], grad_refs["gframes"])
                grad_refs["gwin"][...] = acc["win"][...].astype(BF16)


def piece_shape(lay, piece):
    return ((2, 2, 2, 2) if piece[0] == "t" else (2, 2, 2)) + (lay.part_rows("a" if piece[0] == "t" else "b"), CW)


def scratch_for(lay, mode):
    big = lambda m, dt: pltpu.VMEM((m, RMAX, CW), dt)
    wide = lambda dt: pltpu.VMEM((RMAX, D), dt)
    made = {}
    if lay.native:
        made.update(win=pltpu.VMEM((NH, D, CW), BF16), wout=pltpu.VMEM((G, D), BF16), frames=pltpu.VMEM((lay.count * lay.small, CW), BF16))
    made.update(vec=pltpu.VMEM((1, VUSED), F32), sc=pltpu.VMEM((RMAX, RMAX), BF16))
    if mode != "back":
        made.update(h=big(NH, F32), hp=big(NH, F32))
    if mode == "both":
        made.update(q=big(NG, BF16), e=big(NG, BF16))
    if mode != "fore":
        made.update(st=pltpu.VMEM((RMAX, RMAX), BF16), ds=big(NG, BF16), dz=big(NH, BF16), dq=big(NG, F32), xh1=wide(F32))
        made.update(at=pltpu.VMEM((D, RMAX), BF16), awin=pltpu.VMEM((NH, D, CW), F32), awout=pltpu.VMEM((NG, D, CW), F32))
        made.update(asp=pltpu.VMEM((RMAX, RMAX), F32), avec=pltpu.VMEM((8, VUSED), F32))
    return made


def weight_names(lay):
    if not lay.native:
        return list(WEIGHTS)
    return list(PIECES)


def grad_names(lay):
    return list(PIECES) if lay.native else ["gwin", "gwout", "gframes"]


def image_spec():
    return pl.BlockSpec((1, RMAX, D), lambda b, c: (b, 0, 0))


def saved_shapes(images):
    return [jax.ShapeDtypeStruct((images, NG, RMAX, CW), BF16) for _ in SAVED]


def saved_specs():
    spec = pl.BlockSpec((1, NG, RMAX, CW), lambda b, c: (b, 0, 0, 0))
    return [spec] * len(SAVED)


def run_kernel(lay, mode, info, weights, r, saved=None, dn=None):
    images = r.shape[0]
    image = jax.ShapeDtypeStruct((images, RMAX, D), F32)
    whole = pl.BlockSpec(memory_space=pltpu.VMEM)
    operands = list(weights) + [r]
    if lay.native and mode in KEPT:
        operands = [pltpu.with_memory_space_constraint(w, pltpu.VMEM) for w in weights] + [r]
    in_specs = [whole] * len(weights) + [image_spec()]
    outs, out_specs = [], []
    if mode == "back":
        operands += list(saved)
        in_specs += saved_specs()
    if mode != "fore":
        operands.append(dn)
        in_specs.append(image_spec())
    if mode != "back":
        outs.append(image)
        out_specs.append(image_spec())
    if mode == "fore":
        outs += saved_shapes(images)
        out_specs += saved_specs()
    if mode != "fore":
        outs.append(image)
        out_specs.append(image_spec())
        if lay.native:
            grads = [piece_shape(lay, p) for p in PIECES]
        else:
            grads = [(NH, D, CW), (G, D), (lay.count * lay.small, CW)]
        outs += [pltpu.VMEM(s, BF16) if lay.native else jax.ShapeDtypeStruct(s, BF16) for s in grads]
        out_specs += [whole] * len(grads)
    scratch = scratch_for(lay, mode)
    return pl.pallas_call(
        functools.partial(kernel_body, lay, images, mode, list(scratch)),
        grid_spec=pltpu.PrefetchScalarGridSpec(
            num_scalar_prefetch=1, grid=(images,), in_specs=in_specs, out_specs=out_specs, scratch_shapes=list(scratch.values())
        ),
        out_shape=outs,
        compiler_params=pltpu.CompilerParams(vmem_limit_bytes=VLIM[mode if lay.native else "plain"]),
        name="layer_" + mode,
    )(info, *operands)


def pack_large(lay, w_in, w_out):
    win = w_in.reshape(lay.rows, NH, CW)
    wout = w_out.reshape(NG, lay.rows, D)
    return [win[:, j] for j in range(NH)] + [wout[k] for k in range(NG)]


def pack_small(lay, spatial, vectors, me):
    index = lay.index(me)
    sp_at = lax.rem(index * lay.sp_shard, P_SIZE)
    vec_at = lax.rem(index * lay.vec_shard, 128)
    sp = lax.dynamic_update_slice(jnp.zeros((lay.sp_rows * P_SIZE,), BF16), spatial, (sp_at,)).reshape(lay.sp_rows, P_SIZE)
    vec = lax.dynamic_update_slice(jnp.zeros((lay.vec_rows * 128,), BF16), vectors, (vec_at,)).reshape(lay.vec_rows, 128)
    sp = jnp.pad(sp, ((0, 0), (0, CW - P_SIZE)))
    vec = jnp.pad(vec, ((0, lay.small - lay.sp_rows - lay.vec_rows), (0, CW - 128)))
    return jnp.concatenate([sp, vec])


def part_of(fields, part):
    return jnp.concatenate([fields[f] for f in PART_FIELDS[part]])


def ring_gather(lay, value, axis):
    pieces = [value]
    for _ in range(lay.size[axis] - 1):
        pieces.append(lay.shift(pieces[-1], axis))
    return pieces


def hold(*values):
    return lax.optimization_barrier(values)


def move(lay, *items):
    values = hold(*[value for value, _ in items])
    return hold(*[lay.exchange(value, *flips) for value, (_, flips) in zip(values, items)])


def gather_start(lay, packed, me):
    even = me["core"] == 0
    keep = jnp.where(even, packed["a"], packed["d"])
    give = jnp.where(even, packed["d"], packed["a"])
    return jnp.stack([keep, lay.exchange(give, CORE)])


GATHER_T = ((FAR,), (NEAR,), FIRST, SECOND)
GATHER_B = (FIRST, (FAR,), SECOND, (NEAR,))


def gather_plain(lay, packed, me):
    win, wout, frames = [None] * NH, [None] * NG, None
    for p in PARTS:
        dims = ("core",) + PART_DIMS[p]
        value = packed[p]
        for axis in reversed(dims):
            value = jnp.stack(ring_gather(lay, value, axis))
        for k, axis in enumerate(dims):
            n = lay.size[axis]
            value = jnp.take(value, lax.rem(me[axis] - jnp.arange(n) + n, n), axis=k)
        order = [dims.index(a) for a in ("z", "x", "core", "y")]
        value = value.transpose(order + [4, 5]).reshape(lay.count, lay.part_rows(p), CW)
        for f, at in lay.offsets(p):
            if f < 6:
                win[f] = value[:, at : at + lay.rows].reshape(D, CW)
            elif f < 9:
                wout[f - 6] = value[:, at : at + lay.rows]
            else:
                frames = value[:, at : at + lay.small].reshape(lay.count * lay.small, CW)
    return [jnp.stack(win), jnp.stack(wout, axis=1).reshape(G, D), frames]


def ring_scatter(lay, value, axis):
    n = lay.size[axis]
    total = value[n - 1].astype(F32)
    for k in range(n - 2, -1, -1):
        total = lay.shift(total.astype(BF16), axis).astype(F32) + value[k].astype(F32)
    return total


def low(v):
    return v.astype(BF16)


def add(mine, got):
    return mine.astype(F32) + got.astype(F32)


def scatter_core(lay, grads):
    t00, t01, t10, t11, b00, b01, b10, b11 = grads
    t11, b11 = move(lay, (t11, (CORE,)), (b11, (CORE,)))
    far, bfar = hold(low(add(t01, t11)), low(add(b01, b11)))
    t10, b10, far, bfar = hold(t10, b10, far, bfar)
    return far, bfar, (t00, lay.exchange(t10, CORE)), (b00, lay.exchange(b10, CORE))


SCATTER_T = (SECOND, FIRST, (NEAR,), (FAR,))
SCATTER_B = ((NEAR,), SECOND, (FAR,), FIRST)


def part_fields(lay, part, rows):
    return {f: rows[at : at + (lay.small if f == 9 else lay.rows)] for f, at in lay.offsets(part)}


def end_fields(lay, me, top, other):
    even = me["core"] == 0
    a, d = jnp.where(even, top[0], other), jnp.where(even, other, top[0])
    return {**part_fields(lay, "a", a), **part_fields(lay, "d", d)}


def join_large(lay, *layers):
    gwin = [jnp.stack([fields[j] for j in range(NH)], axis=1).reshape(-1) for fields in layers]
    gwout = [jnp.concatenate([fields[6 + k] for k in range(NG)]).reshape(-1) for fields in layers]
    return [jnp.stack(gwin), jnp.stack(gwout)]


def native_path(lay, me, size_class, params, patches, cotangent):
    stack = lambda v, got: jnp.stack([v, got])
    info = size_class
    w_in, w_out, spatial, vectors = params
    large = pack_large(lay, w_in[0], w_out[0])
    t0 = gather_start(lay, {p: part_of(large, p) for p in "ad"}, me)
    t0, spatial, vectors, w_in, w_out = hold(t0, spatial, vectors, w_in, w_out)
    x = lay.exchange(t0, *GATHER_T[0])
    b0 = part_of(large + [pack_small(lay, spatial[0], vectors[0], me)], "b")
    y = lay.exchange(b0, *GATHER_B[0])
    x, y, w_in, w_out, spatial, vectors = hold(x, y, w_in, w_out, spatial, vectors)
    large = pack_large(lay, w_in[1], w_out[1])
    t1 = gather_start(lay, {p: part_of(large, p) for p in "ad"}, me)
    b1 = part_of(large + [pack_small(lay, spatial[1], vectors[1], me)], "b")
    t0, b0, patches, cotangent, info = hold(stack(t0, x), stack(b0, y), patches, cotangent, info)
    for k in (1, 2):
        x, y = lay.exchange(t0, *GATHER_T[k]), lay.exchange(b0, *GATHER_B[k])
        u, v = lay.exchange(t1, *GATHER_T[k - 1]), lay.exchange(b1, *GATHER_B[k - 1])
        if k == 1:
            info, patches, cotangent = describe(me, info), spread(patches), spread(cotangent)
        x, y, u, v, patches, cotangent, info = hold(x, y, u, v, patches, cotangent, info)
        t0, b0, t1, b1 = hold(stack(t0, x), stack(b0, y), stack(t1, u), stack(b1, v))
    t0c, b0c = lay.exchange(t0, CORE), lay.exchange(b0, CORE)
    x, y, u, v = [lay.exchange(g, *f) for g, f in ((t0, SECOND), (b0, (NEAR,)), (t1, FIRST), (b1, SECOND))]
    x, y, u, v = hold(x, y, u, v)
    weights0 = [t0, x, t0c, lay.exchange(x, CORE), b0, y, b0c, lay.exchange(y, CORE)]
    t1, b1 = stack(t1, u), stack(b1, v)
    x, y, t1c, b1c = [lay.exchange(v, *f) for v, f in ((t1, SECOND), (b1, (NEAR,)), (t1, (CORE,)), (b1, (CORE,)))]
    hidden, *saved = run_kernel(lay, "fore", info, weights0, patches)
    x, y, t1c, b1c, hidden = hold(x, y, t1c, b1c, hidden)
    weights1 = [t1, x, t1c, lay.exchange(x, CORE), b1, y, b1c, lay.exchange(y, CORE)]
    outputs, grad, *grads1 = run_kernel(lay, "both", info, weights1, hidden, dn=cotangent)

    far1, bfar1, near1, bnear1 = scatter_core(lay, grads1)
    far1, bfar1, grad = hold(far1, bfar1, grad)
    x, y = lay.exchange(far1, *SECOND), lay.exchange(bfar1, NEAR)
    patch_grad, *grads0 = run_kernel(lay, "back", info, weights0, patches, saved=saved, dn=grad)
    x, y, patch_grad, outputs, *grads0 = hold(x, y, patch_grad, outputs, *grads0)
    top1, b1 = add(add(*near1), x), add(add(*bnear1), y)
    u, v = lay.exchange(low(top1[1]), *SCATTER_T[1]), lay.exchange(low(b1[1]), *SCATTER_B[1])
    far0, bfar0, near0, bnear0 = scatter_core(lay, grads0)
    far0, bfar0, outputs, patch_grad = hold(far0, bfar0, outputs, patch_grad)
    x, y = lay.exchange(far0, *SECOND), lay.exchange(bfar0, NEAR)
    x, y, u, v, outputs, patch_grad = hold(x, y, u, v, tilt(outputs), tilt(patch_grad))
    top1, b1 = add(top1[0], u), add(b1[0], v)
    top0, b0 = add(add(*near0), x), add(add(*bnear0), y)
    for k in (1, 2):
        sends = [(low(v[1]), f) for v, f in ((top0, SCATTER_T[k]), (b0, SCATTER_B[k]), (top1, SCATTER_T[k + 1]), (b1, SCATTER_B[k + 1]))]
        x, y, u, v = move(lay, *sends)
        top0, b0, top1, b1 = add(top0[0], x), add(b0[0], y), add(top1[0], u), add(b1[0], v)
    send, send_b = hold(low(top0[1]), low(b0[1]))
    x, y = lay.exchange(send, *SCATTER_T[3]), lay.exchange(send_b, *SCATTER_B[3])
    last1 = lay.exchange(top1[1], CORE)
    b0 = add(b0[0], y)
    fields0, fields1 = part_fields(lay, "b", b0), part_fields(lay, "b", b1)
    small = [jnp.stack(v) for v in zip(*[unpack_small_grads(lay, f[9], me) for f in (fields0, fields1)])]
    fields1.update(end_fields(lay, me, top1, last1))
    x, *small = hold(x, *small)
    top0 = add(top0[0], x)
    fields0.update(end_fields(lay, me, top0, lay.exchange(top0[1], CORE)))
    outputs, patch_grad = outputs.transpose(1, 0, 2), patch_grad.transpose(1, 0, 2)
    return [outputs, patch_grad] + join_large(lay, fields0, fields1) + small


def tilt(v):
    return v[:, :P_SIZE].transpose(1, 0, 2)


def describe(me, size_class):
    return jnp.concatenate([size_class, jnp.stack([me[a] for a in ("core", "x", "z", "y")]).astype(jnp.int32)])


def spread(v):
    return jnp.pad(v, ((0, 0), (0, RMAX - P_SIZE), (0, 0)))


def plain_path(lay, me, size_class, params, patches, cotangent):
    packed = []
    for w_in, w_out, spatial, vectors in zip(*params):
        fields = pack_large(lay, w_in, w_out) + [pack_small(lay, spatial, vectors, me)]
        packed.append({p: part_of(fields, p) for p in PARTS})
    info, patches, cotangent = describe(me, size_class), spread(patches), spread(cotangent)
    weights0, weights1 = [gather_plain(lay, p, me) for p in packed]
    hidden, *saved = run_kernel(lay, "fore", info, weights0, patches)
    outputs, grad, *grads1 = run_kernel(lay, "both", info, weights1, hidden, dn=cotangent)
    patch_grad, *grads0 = run_kernel(lay, "back", info, weights0, patches, saved=saved, dn=grad)
    outputs, patch_grad = outputs[:, :P_SIZE], patch_grad[:, :P_SIZE]
    layers = []
    for grads in (grads0, grads1):
        sums = scatter_plain(lay, grads, me)
        layers.append({f: v for p in PARTS for f, v in part_fields(lay, p, sums[p]).items()})
    small = [jnp.stack(v) for v in zip(*[unpack_small_grads(lay, f[9], me) for f in layers])]
    return [outputs, patch_grad] + join_large(lay, *layers) + small


def scatter_plain(lay, grads, me):
    gwin, gwout, gframes = grads
    gwin = gwin.reshape(NH, lay.count, lay.rows, CW)
    gwout = gwout.reshape(lay.count, NG, lay.rows, D)
    gframes = gframes.reshape(lay.count, lay.small, CW)
    fields = [gwin[j] for j in range(NH)] + [gwout[:, k] for k in range(NG)] + [gframes]
    result = {}
    for p in PARTS:
        dims = ("core",) + PART_DIMS[p]
        value = jnp.concatenate([fields[f] for f in PART_FIELDS[p]], axis=1)
        value = value.reshape(lay.size["z"], 2, 2, lay.size["y"], lay.part_rows(p), CW)
        value = value.transpose([("z", "x", "core", "y").index(a) for a in dims] + [4, 5])
        for k, axis in enumerate(dims):
            n = lay.size[axis]
            value = jnp.take(value, lax.rem(me[axis] + jnp.arange(n), n), axis=k)
        for axis in dims:
            value = ring_scatter(lay, value, axis)
        result[p] = value
    return result


def unpack_small_grads(lay, rows, me):
    index = lay.index(me)
    sp = rows[0 : lay.sp_rows, 0:P_SIZE].reshape(-1)
    sp = lax.dynamic_slice(sp, (lax.rem(index * lay.sp_shard, P_SIZE),), (lay.sp_shard,))
    vec = rows[lay.sp_rows : lay.sp_rows + lay.vec_rows, 0:128].reshape(-1)
    return sp, lax.dynamic_slice(vec, (lax.rem(index * lay.vec_shard, 128),), (lay.vec_shard,))


def per_device(mesh_shape, patches, cotangent, size_class, w_in, w_out, spatial, vectors):
    lay = Layout(mesh_shape, spatial.shape[1], vectors.shape[1])
    wide, narrow = lax.axis_index("wide"), lax.axis_index("narrow")
    me = {"core": lax.rem(wide, 2), "x": lax.rem(wide // 2, 2), "z": wide // 4, "y": narrow}
    params = w_in, w_out, spatial, vectors
    path = native_path if lay.native else plain_path
    return tuple(path(lay, me, size_class, params, patches, cotangent))


def solution(mesh):
    shape = (mesh.shape["wide"], mesh.shape["narrow"])
    rows = P(AXES, None, None)
    flat = P(None, AXES)
    return jax.shard_map(
        functools.partial(per_device, shape),
        mesh=mesh,
        in_specs=(rows, rows, P(AXES), flat, flat, flat, flat),
        out_specs=(rows, rows, flat, flat, flat, flat),
        check_vma=False,
    )
```

```python
import functools
import jax
import jax.numpy as jnp
import numpy as np
from jax import lax
from jax.experimental import pallas as pl
from jax.experimental.pallas import tpu as pltpu
from jax.sharding import PartitionSpec as P

D = 512
H = 3072
P_SIZE = 324
LAYERS = 2
G = 1536
EPS = 1e-05
CW = 512
NG = G // CW
NH = H // CW
RMAX = 336
COUNTS = (100, 196, 324)
F32 = jnp.float32
BF16 = jnp.bfloat16
O_LN1G, O_LN1S, O_INB = 0, D, 2 * D
O_LN2G, O_LN2S, O_OUTB = 2 * D + H, 2 * D + H + G, 2 * D + H + 2 * G
VUSED = 3 * D + H + 2 * G
VROWS = VUSED // 128
VPAD = (VROWS + 15) // 16 * 16
GELU_C = 0.7978845608028654
GELU_A = 0.044715
AXES = ("wide", "narrow")
VLIM = {"plain": 60 * 2**20, "fore": 46 * 2**20, "both": 40 * 2**20, "back": 41 * 2**20}
PART_FIELDS = {"a": (0, 1, 6), "d": (2, 3, 7), "b": (4, 5, 8, 9)}
PART_DIMS = {"a": ("y", "x", "z"), "d": ("x", "y", "z"), "b": ("z", "y", "x")}
PARTS = ("a", "d", "b")
KEPT = ("fore", "both", "back")
PIECES = ("t00", "t01", "t10", "t11", "b00", "b01", "b10", "b11")


class Layout:
    def __init__(self, mesh_shape, sp_shard, vec_shard):
        wide, narrow = mesh_shape
        self.size = {"core": 2, "x": 2, "z": wide // 4, "y": narrow}
        self.count = wide * narrow
        self.rows = D // self.count
        self.sp_shard, self.vec_shard = sp_shard, vec_shard
        self.sp_rows = (sp_shard + 2 * P_SIZE - 2) // P_SIZE
        self.vec_rows = (vec_shard + 2 * 128 - 2) // 128
        self.native = self.rows == 16 and narrow == 2 and wide == 16
        self.small = (self.sp_rows + self.vec_rows + 7) // 8 * 8

    def part_rows(self, part):
        return sum(self.small if f == 9 else self.rows for f in PART_FIELDS[part])

    def offsets(self, part):
        spots, at = [], 0
        for f in PART_FIELDS[part]:
            spots.append((f, at))
            at += self.small if f == 9 else self.rows
        return spots

    def index(self, at):
        return ((at["z"] * 2 + at["x"]) * 2 + at["core"]) * self.size["y"] + at["y"]

    def coords(self, i):
        y, wide = i % self.size["y"], i // self.size["y"]
        return {"core": wide % 2, "x": wide // 2 % 2, "z": wide // 4, "y": y}

    def shift(self, value, axis, step=1):
        pairs = []
        for i in range(self.count):
            at = self.coords(i)
            at[axis] = (at[axis] + step) % self.size[axis]
            pairs.append((i, self.index(at)))
        return lax.ppermute(value, AXES, pairs)

    def exchange(self, value, *flips):
        pairs = []
        for i in range(self.count):
            at = self.coords(i)
            for axis, bit in flips[at["core"] % len(flips)].items():
                at[axis] ^= bit
            pairs.append((i, self.index(at)))
        return lax.ppermute(value, AXES, pairs)


CORE, NEAR, FAR = {"core": 1}, {"z": 1}, {"z": 2}
FIRST, SECOND = ({"x": 1}, {"y": 1}), ({"y": 1}, {"x": 1})


def dot(a, b):
    return lax.dot_general(a, b, (((1,), (0,)), ((), ())), preferred_element_type=F32)


def dot_nt(a, b):
    return lax.dot_general(a, b, (((1,), (1,)), ((), ())), preferred_element_type=F32)


def gelu_both(z):
    z2 = z * z
    t = jnp.tanh(z * (GELU_C + (GELU_C * GELU_A) * z2))
    w = 0.5 * t + 0.5
    h = z * w
    return h, w + (h - h * w) * (2.0 * GELU_C + (6.0 * GELU_C * GELU_A) * z2)


def rows_sum8(x):
    rows, cols = x.shape
    return jnp.sum(x.reshape(rows // 8, 8, cols), axis=0)


def picker(lay, rows, cols, first, per, length, width):
    r = lax.broadcasted_iota(jnp.int32, (rows, cols), 0)
    c = lax.broadcasted_iota(jnp.int32, (rows, cols), 1)
    i, t = c // lay.small, c % lay.small - first
    hit = (t >= 0) & (t < per) & (r == (i * length) // width + t)
    return jnp.where(hit, 1.0, 0.0).astype(BF16)


def unpack_small(lay, frames_ref, vec_ref, sc_ref, st_ref):
    count = lay.count * lay.small
    ms = picker(lay, RMAX, count, 0, lay.sp_rows, lay.sp_shard, P_SIZE)
    mv = picker(lay, VPAD, count, lay.sp_rows, lay.vec_rows, lay.vec_shard, 128)
    sp = dot(ms, frames_ref[:, 0:384])
    vec = dot(mv, frames_ref[:, 0:128])
    for r in range(VROWS):
        vec_ref[:, r * 128 : (r + 1) * 128] = vec[r : r + 1, :]
    row = lax.broadcasted_iota(jnp.int32, (RMAX, RMAX), 0)
    col = lax.broadcasted_iota(jnp.int32, (RMAX, RMAX), 1)
    inside = (row < P_SIZE) & (col < P_SIZE)
    sp = sp[:, 0:RMAX]
    sp_t = jnp.transpose(sp)
    sc_ref[...] = jnp.where(inside, sp, jnp.where((col == P_SIZE) & (row < P_SIZE), sp_t, 0.0)).astype(BF16)
    if st_ref is not None:
        st_ref[...] = jnp.where(inside, sp_t, 0.0).astype(BF16)


def role_blocks(lay, me, sign):
    for who in range(2):
        role = me["core"] ^ who
        for second in range(2):
            for first, k1, k2, core in np.ndindex(2, 2, 2, 2):
                swap = role * (first ^ second)
                at = {"z": me["z"] ^ (k1 + 2 * k2), "core": role ^ core, "x": me["x"] ^ first ^ swap, "y": me["y"] ^ second ^ swap}
                yield who, second, (first, k1, k2, core), role, lay.index(at)


def both_blocks(lay, me, sign):
    for who in range(2):
        role = me["core"] ^ who
        for k1 in range(2):
            for first, k2, second in np.ndindex(2, 2, 2):
                swap = role * (first ^ second)
                at = {"z": me["z"] ^ (k1 + 2 * k2), "core": role, "x": me["x"] ^ first ^ swap, "y": me["y"] ^ second ^ swap}
                yield who, k1, (first, k2, second), lay.index(at)


def sixteen(start):
    return pl.ds(pl.multiple_of(start, 16), 16)


def assemble(lay, me, given, win_ref, wout_ref, frames_ref):
    for who, second, place, role, i in role_blocks(lay, me, -1):
        src = given["t%d%d" % (who, second)]
        for t in range(2):
            win_ref[2 * role + t, sixteen(i * 16), :] = src[place + (slice(16 * t, 16 * t + 16),)]
        wout_ref[sixteen(i * 48 + 16 * role), :] = src[place + (slice(32, 48),)]
    for who, z, place, i in both_blocks(lay, me, -1):
        src = given["b%d%d" % (who, z)]
        for t in range(2):
            win_ref[4 + t, sixteen(i * 16), :] = src[place + (slice(16 * t, 16 * t + 16),)]
        wout_ref[sixteen(i * 48 + 32), :] = src[place + (slice(32, 48),)]
        frames_ref[sixteen(i * 16), :] = src[place + (slice(48, 64),)]


def forward_part(rows, valid, r_ref, vec_ref, win_ref, wout_ref, sc_ref, sv, save):
    h, hp = sv["h"], sv["hp"]
    r, k, xh, a = first_norm(rows, valid, r_ref, vec_ref)
    tot = jnp.zeros((rows, 1), F32)
    for j in list(range(NG, NH)) + list(range(NG)):
        z = dot(a, win_ref[j]) + vec_ref[:, O_INB + j * CW : O_INB + (j + 1) * CW]
        h[j], hpj = gelu_both(z)
        hp[j] = hpj
        if j >= NG:
            tot = tot + jnp.sum(h[j], axis=1, keepdims=True)
    mu2 = tot * (1.0 / G)
    ssq = jnp.zeros((rows, 1), F32)
    for j in range(NG):
        vc = h[NG + j] - mu2
        ssq = ssq + jnp.sum(vc * vc, axis=1, keepdims=True)
    k2 = lax.rsqrt(ssq * (1.0 / G) + EPS)
    one = jnp.where(lax.broadcasted_iota(jnp.int32, (rows, 1), 0) == P_SIZE, 1.0, 0.0)
    for j in range(NG):
        lo = j * CW
        xh2 = (h[NG + j] - mu2) * k2
        sv["v"][j] = xh2.astype(sv["v"].dtype)
        sv["hv"][j] = (hp[NG + j] * k2).astype(sv["hv"].dtype)
        q = xh2 * vec_ref[:, O_LN2G + lo : O_LN2G + lo + CW] + vec_ref[:, O_LN2S + lo : O_LN2S + lo + CW]
        sv["q"][j] = jnp.where(valid, q, one).astype(BF16)
    o = None
    for j in range(NG):
        s = dot(sc_ref[...], sv["q"][j])
        u = h[j]
        e = (u * s).astype(BF16)
        sv["sh"][j] = (hp[j] * s).astype(sv["sh"].dtype)
        sv["e"][j] = e
        if save:
            sv["u"][j] = u.astype(BF16)
        part = dot(e, wout_ref[j * CW : (j + 1) * CW, :])
        o = part if o is None else o + part
    o = jnp.where(valid, r + (o + vec_ref[:, O_OUTB : O_OUTB + D]), 0.0)
    return (k, xh, a), o


def first_norm(rows, valid, r_ref, vec_ref):
    r = jnp.where(valid, r_ref[0, 0:rows, :].astype(F32), 0.0)
    mu = jnp.mean(r, axis=1, keepdims=True)
    c = r - mu
    k = lax.rsqrt(jnp.mean(c * c, axis=1, keepdims=True) + EPS)
    xh = c * k
    a = (xh * vec_ref[:, O_LN1G : O_LN1G + D] + vec_ref[:, O_LN1S : O_LN1S + D]).astype(BF16)
    return r, k, xh, a


def backward_part(rows, valid, norm, dn_ref, vec_ref, win_ref, wout_ref, st_ref, sv, acc):
    k, xh, a = norm
    sv["xh1"][0:rows, :] = xh
    sv["at"][0:D, 0:rows] = jnp.transpose(a)
    dn = jnp.where(valid, dn_ref[0, 0:rows, :].astype(F32), 0.0)
    do = dn.astype(BF16)
    dot_t = jnp.transpose(do)
    gvec = acc["vec"]
    gvec[:, O_OUTB : O_OUTB + D] += rows_sum8(do.astype(F32))
    for j in range(NG):
        acc["wout"][j] += dot(dot_t, sv["e"][j, 0:rows, :])
        de = dot_nt(do, wout_ref[j * CW : (j + 1) * CW, :])
        sv["dz"][j, 0:rows, :] = (de * sv["sh"][j].astype(F32)).astype(BF16)
        sv["ds"][j, 0:rows, :] = (de * sv["u"][j].astype(F32)).astype(BF16)
    gs = None
    for j in range(NG):
        part = dot_nt(sv["ds"][j, 0:rows, :], sv["q"][j, 0:rows, :])
        gs = part if gs is None else gs + part
    acc["sp"][...] += gs
    m1 = jnp.zeros((rows, 1), F32)
    m2 = jnp.zeros((rows, 1), F32)
    for j in range(NG):
        lo = j * CW
        dq = jnp.where(valid, dot(st_ref[...], sv["ds"][j, 0:rows, :]), 0.0)
        sv["dq"][j, 0:rows, :] = dq
        gain = vec_ref[:, O_LN2G + lo : O_LN2G + lo + CW]
        w = dq * sv["v"][j].astype(F32)
        gvec[:, O_LN2G + lo : O_LN2G + lo + CW] += rows_sum8(w)
        gvec[:, O_LN2S + lo : O_LN2S + lo + CW] += rows_sum8(dq)
        m1 = m1 + jnp.sum(dq * gain, axis=1, keepdims=True)
        m2 = m2 + jnp.sum(w * gain, axis=1, keepdims=True)
    m1 = m1 * (1.0 / G)
    m2 = m2 * (1.0 / G)
    for j in range(NG):
        lo = j * CW
        gain = vec_ref[:, O_LN2G + lo : O_LN2G + lo + CW]
        dv = (sv["dq"][j, 0:rows, :] * gain - m1 - sv["v"][j].astype(F32) * m2)
        sv["dz"][NG + j, 0:rows, :] = (dv * sv["hv"][j].astype(F32)).astype(BF16)
    da = None
    for j in range(NH):
        dz = sv["dz"][j, 0:rows, :]
        acc["win"][j] += dot(sv["at"][0:D, 0:rows], dz)
        gvec[:, O_INB + j * CW : O_INB + (j + 1) * CW] += rows_sum8(dz.astype(F32))
        part = dot_nt(dz, win_ref[j])
        da = part if da is None else da + part
    xh = sv["xh1"][0:rows, :]
    gain = vec_ref[:, O_LN1G : O_LN1G + D]
    w = da * xh
    gvec[:, O_LN1G : O_LN1G + D] += rows_sum8(w)
    gvec[:, O_LN1S : O_LN1S + D] += rows_sum8(da)
    t = da * gain
    mt = jnp.mean(t, axis=1, keepdims=True)
    mx = jnp.mean(w * gain, axis=1, keepdims=True)
    return dn + k * (t - mt - xh * mx)


def gather_grads(lay, acc, wout_ref, frames_ref):
    for j in range(NG):
        wout_ref[j * CW : (j + 1) * CW, :] = jnp.transpose(acc["wout"][j]).astype(BF16)
    whole = acc["sp"][...]
    row = lax.broadcasted_iota(jnp.int32, (RMAX, RMAX), 0)
    col = lax.broadcasted_iota(jnp.int32, (RMAX, RMAX), 1)
    ext = jnp.where(row == P_SIZE, jnp.transpose(whole), jnp.where(row < P_SIZE, whole, 0.0))
    ext = jnp.where(col < P_SIZE, ext, 0.0).astype(BF16)
    sums = jnp.sum(acc["vec"][...], axis=0, keepdims=True)
    vec = jnp.concatenate([sums[:, r * 128 : (r + 1) * 128] for r in range(VROWS)] + [jnp.zeros((VPAD - VROWS, 128), F32)], axis=0)
    count = lay.count * lay.small
    ms = picker(lay, RMAX, count, 0, lay.sp_rows, lay.sp_shard, P_SIZE)
    mv = picker(lay, VPAD, count, lay.sp_rows, lay.vec_rows, lay.vec_shard, 128)
    tn = (((0,), (0,)), ((), ()))
    frames_ref[...] = jnp.zeros(frames_ref.shape, BF16)
    frames_ref[:, 0:RMAX] = lax.dot_general(ms, ext, tn, preferred_element_type=F32).astype(BF16)
    part = lax.dot_general(mv, vec.astype(BF16), tn, preferred_element_type=F32)
    frames_ref[:, 0:128] += part.astype(BF16)


def scatter_grads(lay, me, acc, wout_ref, frames_ref, out):
    for who, second, place, role, i in role_blocks(lay, me, 1):
        dst = out["t%d%d" % (who, second)]
        for t in range(2):
            dst[place + (slice(16 * t, 16 * t + 16),)] = acc["win"][2 * role + t, sixteen(i * 16), :].astype(BF16)
        dst[place + (slice(32, 48),)] = wout_ref[sixteen(i * 48 + 16 * role), :]
    for who, z, place, i in both_blocks(lay, me, 1):
        dst = out["b%d%d" % (who, z)]
        for t in range(2):
            dst[place + (slice(16 * t, 16 * t + 16),)] = acc["win"][4 + t, sixteen(i * 16), :].astype(BF16)
        dst[place + (slice(32, 48),)] = wout_ref[sixteen(i * 48 + 32), :]
        dst[place + (slice(48, 64),)] = frames_ref[sixteen(i * 16), :]


def read_me(info_ref, images):
    return {axis: info_ref[images + k] for k, axis in enumerate(("core", "x", "z", "y"))}


class Names:
    def __init__(self, refs):
        self.refs = list(refs)

    def take(self, names):
        got = dict(zip(names, self.refs))
        self.refs = self.refs[len(names) :]
        return got


WEIGHTS = ("win", "wout", "frames")
SAVED = ("u", "sh", "v", "hv", "q", "e")


def kernel_body(lay, images, mode, scratch_names, info_ref, *refs):
    names = Names(refs)
    given = names.take(weight_names(lay))
    r_ref = names.take(["r"])["r"]
    saved = names.take(SAVED) if mode == "back" else {}
    dn_ref = names.take(["dn"])["dn"] if mode != "fore" else None
    out_ref = names.take(["out"])["out"] if mode != "back" else None
    if mode == "fore":
        saved = names.take(SAVED)
    gr_ref = names.take(["gr"])["gr"] if mode != "fore" else None
    grad_refs = names.take(grad_names(lay)) if mode != "fore" else {}
    sv = names.take(scratch_names)
    w = sv if lay.native else given
    sv.update({k: saved[k].at[0] for k in saved})
    if mode == "both":
        sv.update(u=sv["h"], sh=sv["hp"], v=sv["h"].at[NG:NH], hv=sv["hp"].at[NG:NH])
    acc = {k: sv.get("a" + k) for k in ("win", "wout", "sp", "vec")}
    b = pl.program_id(0)

    @pl.when(b == 0)
    def _():
        if lay.native:
            assemble(lay, read_me(info_ref, images), given, w["win"], w["wout"], w["frames"])
        unpack_small(lay, w["frames"], sv["vec"], sv["sc"], sv.get("st"))
        if mode != "fore":
            for ref in acc.values():
                ref[...] = jnp.zeros(ref.shape, F32)

    cls = info_ref[b]
    n = jnp.where(cls == 0, COUNTS[0], jnp.where(cls == 1, COUNTS[1], COUNTS[2]))
    valid = lax.broadcasted_iota(jnp.int32, (RMAX, 1), 0) < n
    if mode == "back":
        _, k, xh, a = first_norm(RMAX, valid, r_ref, sv["vec"])
        norm = (k, xh, a)
    else:
        norm, o = forward_part(RMAX, valid, r_ref, sv["vec"], w["win"], w["wout"], sv["sc"], sv, mode == "fore")
        out_ref[0] = o
    if mode != "fore":
        gr_ref[0] = backward_part(RMAX, valid, norm, dn_ref, sv["vec"], w["win"], w["wout"], sv["st"], sv, acc)

        @pl.when(b == pl.num_programs(0) - 1)
        def _():
            if lay.native:
                gather_grads(lay, acc, w["wout"], w["frames"])
                scatter_grads(lay, read_me(info_ref, images), acc, w["wout"], w["frames"], grad_refs)
            else:
                gather_grads(lay, acc, grad_refs["gwout"], grad_refs["gframes"])
                grad_refs["gwin"][...] = acc["win"][...].astype(BF16)


def piece_shape(lay, piece):
    return ((2, 2, 2, 2) if piece[0] == "t" else (2, 2, 2)) + (lay.part_rows("a" if piece[0] == "t" else "b"), CW)


def scratch_for(lay, mode):
    big = lambda m, dt: pltpu.VMEM((m, RMAX, CW), dt)
    wide = lambda dt: pltpu.VMEM((RMAX, D), dt)
    made = {}
    if lay.native:
        made.update(win=pltpu.VMEM((NH, D, CW), BF16), wout=pltpu.VMEM((G, D), BF16), frames=pltpu.VMEM((lay.count * lay.small, CW), BF16))
    made.update(vec=pltpu.VMEM((1, VUSED), F32), sc=pltpu.VMEM((RMAX, RMAX), BF16))
    if mode != "back":
        made.update(h=big(NH, F32), hp=big(NH, F32))
    if mode == "both":
        made.update(q=big(NG, BF16), e=big(NG, BF16))
    if mode != "fore":
        made.update(st=pltpu.VMEM((RMAX, RMAX), BF16), ds=big(NG, BF16), dz=big(NH, BF16), dq=big(NG, F32), xh1=wide(F32))
        made.update(at=pltpu.VMEM((D, RMAX), BF16), awin=pltpu.VMEM((NH, D, CW), F32), awout=pltpu.VMEM((NG, D, CW), F32))
        made.update(asp=pltpu.VMEM((RMAX, RMAX), F32), avec=pltpu.VMEM((8, VUSED), F32))
    return made


def weight_names(lay):
    if not lay.native:
        return list(WEIGHTS)
    return list(PIECES)


def grad_names(lay):
    return list(PIECES) if lay.native else ["gwin", "gwout", "gframes"]


def image_spec():
    return pl.BlockSpec((1, RMAX, D), lambda b, c: (b, 0, 0))


def saved_shapes(images):
    return [jax.ShapeDtypeStruct((images, NG, RMAX, CW), BF16) for _ in SAVED]


def saved_specs():
    spec = pl.BlockSpec((1, NG, RMAX, CW), lambda b, c: (b, 0, 0, 0))
    return [spec] * len(SAVED)


def run_kernel(lay, mode, info, weights, r, saved=None, dn=None):
    images = r.shape[0]
    image = jax.ShapeDtypeStruct((images, RMAX, D), F32)
    whole = pl.BlockSpec(memory_space=pltpu.VMEM)
    operands = list(weights) + [r]
    if lay.native and mode in KEPT:
        operands = [pltpu.with_memory_space_constraint(w, pltpu.VMEM) for w in weights] + [r]
    in_specs = [whole] * len(weights) + [image_spec()]
    outs, out_specs = [], []
    if mode == "back":
        operands += list(saved)
        in_specs += saved_specs()
    if mode != "fore":
        operands.append(dn)
        in_specs.append(image_spec())
    if mode != "back":
        outs.append(image)
        out_specs.append(image_spec())
    if mode == "fore":
        outs += saved_shapes(images)
        out_specs += saved_specs()
    if mode != "fore":
        outs.append(image)
        out_specs.append(image_spec())
        if lay.native:
            grads = [piece_shape(lay, p) for p in PIECES]
        else:
            grads = [(NH, D, CW), (G, D), (lay.count * lay.small, CW)]
        outs += [pltpu.VMEM(s, BF16) if lay.native else jax.ShapeDtypeStruct(s, BF16) for s in grads]
        out_specs += [whole] * len(grads)
    scratch = scratch_for(lay, mode)
    return pl.pallas_call(
        functools.partial(kernel_body, lay, images, mode, list(scratch)),
        grid_spec=pltpu.PrefetchScalarGridSpec(
            num_scalar_prefetch=1, grid=(images,), in_specs=in_specs, out_specs=out_specs, scratch_shapes=list(scratch.values())
        ),
        out_shape=outs,
        compiler_params=pltpu.CompilerParams(vmem_limit_bytes=VLIM[mode if lay.native else "plain"]),
        name="layer_" + mode,
    )(info, *operands)


def pack_large(lay, w_in, w_out):
    win = w_in.reshape(lay.rows, NH, CW)
    wout = w_out.reshape(NG, lay.rows, D)
    return [win[:, j] for j in range(NH)] + [wout[k] for k in range(NG)]


def pack_small(lay, spatial, vectors, me):
    index = lay.index(me)
    sp_at = lax.rem(index * lay.sp_shard, P_SIZE)
    vec_at = lax.rem(index * lay.vec_shard, 128)
    sp = lax.dynamic_update_slice(jnp.zeros((lay.sp_rows * P_SIZE,), BF16), spatial, (sp_at,)).reshape(lay.sp_rows, P_SIZE)
    vec = lax.dynamic_update_slice(jnp.zeros((lay.vec_rows * 128,), BF16), vectors, (vec_at,)).reshape(lay.vec_rows, 128)
    sp = jnp.pad(sp, ((0, 0), (0, CW - P_SIZE)))
    vec = jnp.pad(vec, ((0, lay.small - lay.sp_rows - lay.vec_rows), (0, CW - 128)))
    return jnp.concatenate([sp, vec])


def part_of(fields, part):
    return jnp.concatenate([fields[f] for f in PART_FIELDS[part]])


def ring_gather(lay, value, axis):
    pieces = [value]
    for _ in range(lay.size[axis] - 1):
        pieces.append(lay.shift(pieces[-1], axis))
    return pieces


def hold(*values):
    return lax.optimization_barrier(values)


def move(lay, *items, join=False):
    values = hold(*[value for value, _ in items])
    items = [(value, flips) for value, (_, flips) in zip(values, items)]
    return hold(*(together(lay, *items) if join else [lay.exchange(value, *flips) for value, flips in items]))


def together(lay, *items):
    got = {}
    for k, (_, flips) in enumerate(items):
        same = [i for i, (_, f) in enumerate(items) if f == flips]
        if same[0] != k:
            continue
        if len(same) == 1:
            got[k] = lay.exchange(items[k][0], *flips)
            continue
        flat = [items[i][0].reshape(-1, CW) for i in same]
        joined, at = lay.exchange(jnp.concatenate(flat), *flips), 0
        for i, v in zip(same, flat):
            got[i] = joined[at : at + v.shape[0]].reshape(items[i][0].shape)
            at += v.shape[0]
    return [got[k] for k in range(len(items))]


def gather_start(lay, packed, me):
    even = me["core"] == 0
    keep = jnp.where(even, packed["a"], packed["d"])
    give = jnp.where(even, packed["d"], packed["a"])
    return jnp.stack([keep, lay.exchange(give, CORE)])


GATHER_T = ((FAR,), (NEAR,), FIRST, SECOND)
GATHER_B = (SECOND, (FAR,), FIRST, (NEAR,))


def gather_plain(lay, packed, me):
    win, wout, frames = [None] * NH, [None] * NG, None
    for p in PARTS:
        dims = ("core",) + PART_DIMS[p]
        value = packed[p]
        for axis in reversed(dims):
            value = jnp.stack(ring_gather(lay, value, axis))
        for k, axis in enumerate(dims):
            n = lay.size[axis]
            value = jnp.take(value, lax.rem(me[axis] - jnp.arange(n) + n, n), axis=k)
        order = [dims.index(a) for a in ("z", "x", "core", "y")]
        value = value.transpose(order + [4, 5]).reshape(lay.count, lay.part_rows(p), CW)
        for f, at in lay.offsets(p):
            if f < 6:
                win[f] = value[:, at : at + lay.rows].reshape(D, CW)
            elif f < 9:
                wout[f - 6] = value[:, at : at + lay.rows]
            else:
                frames = value[:, at : at + lay.small].reshape(lay.count * lay.small, CW)
    return [jnp.stack(win), jnp.stack(wout, axis=1).reshape(G, D), frames]


def ring_scatter(lay, value, axis):
    n = lay.size[axis]
    total = value[n - 1].astype(F32)
    for k in range(n - 2, -1, -1):
        total = lay.shift(total.astype(BF16), axis).astype(F32) + value[k].astype(F32)
    return total


def low(v):
    return v.astype(BF16)


def add(mine, got):
    return mine.astype(F32) + got.astype(F32)


def scatter_core(lay, grads):
    t00, t01, t10, t11, b00, b01, b10, b11 = grads
    t11, b11 = move(lay, (t11, (CORE,)), (b11, (CORE,)))
    far, bfar = hold(low(add(t01, t11)), low(add(b01, b11)))
    t10, b10, far, bfar = hold(t10, b10, far, bfar)
    return far, bfar, (t00, lay.exchange(t10, CORE)), (b00, lay.exchange(b10, CORE))


SCATTER_T = (SECOND, FIRST, (NEAR,), (FAR,))
SCATTER_B = ((NEAR,), FIRST, (FAR,), SECOND)


def part_fields(lay, part, rows):
    return {f: rows[at : at + (lay.small if f == 9 else lay.rows)] for f, at in lay.offsets(part)}


def end_fields(lay, me, top, other):
    even = me["core"] == 0
    a, d = jnp.where(even, top[0], other), jnp.where(even, other, top[0])
    return {**part_fields(lay, "a", a), **part_fields(lay, "d", d)}


def join_large(lay, *layers):
    gwin = [jnp.stack([fields[j] for j in range(NH)], axis=1).reshape(-1) for fields in layers]
    gwout = [jnp.concatenate([fields[6 + k] for k in range(NG)]).reshape(-1) for fields in layers]
    return [jnp.stack(gwin), jnp.stack(gwout)]


def native_path(lay, me, size_class, params, patches, cotangent):
    stack = lambda v, got: jnp.stack([v, got])
    info = size_class
    w_in, w_out, spatial, vectors = params
    large = pack_large(lay, w_in[0], w_out[0])
    t0 = gather_start(lay, {p: part_of(large, p) for p in "ad"}, me)
    t0, spatial, vectors, w_in, w_out = hold(t0, spatial, vectors, w_in, w_out)
    x = lay.exchange(t0, *GATHER_T[0])
    b0 = part_of(large + [pack_small(lay, spatial[0], vectors[0], me)], "b")
    y = lay.exchange(b0, *GATHER_B[0])
    x, y, w_in, w_out, spatial, vectors = hold(x, y, w_in, w_out, spatial, vectors)
    large = pack_large(lay, w_in[1], w_out[1])
    t1 = gather_start(lay, {p: part_of(large, p) for p in "ad"}, me)
    b1 = part_of(large + [pack_small(lay, spatial[1], vectors[1], me)], "b")
    t0, b0, patches, cotangent, info = hold(stack(t0, x), stack(b0, y), patches, cotangent, info)
    for k in (1, 2):
        x, y = lay.exchange(t0, *GATHER_T[k]), lay.exchange(b0, *GATHER_B[k])
        u, v = lay.exchange(t1, *GATHER_T[k - 1]), lay.exchange(b1, *GATHER_B[k - 1])
        if k == 1:
            info, patches, cotangent = describe(me, info), spread(patches), spread(cotangent)
        x, y, u, v, patches, cotangent, info = hold(x, y, u, v, patches, cotangent, info)
        t0, b0, t1, b1 = hold(stack(t0, x), stack(b0, y), stack(t1, u), stack(b1, v))
    t0c, b0c = lay.exchange(t0, CORE), lay.exchange(b0, CORE)
    x, y, u, v = [lay.exchange(g, *f) for g, f in ((t0, GATHER_T[3]), (b0, GATHER_B[3]), (t1, GATHER_T[2]), (b1, GATHER_B[2]))]
    x, y, u, v = hold(x, y, u, v)
    weights0 = [t0, x, t0c, lay.exchange(x, CORE), b0, y, b0c, lay.exchange(y, CORE)]
    t1, b1 = stack(t1, u), stack(b1, v)
    x, y, t1c, b1c = [lay.exchange(v, *f) for v, f in ((t1, SECOND), (b1, (NEAR,)), (t1, (CORE,)), (b1, (CORE,)))]
    hidden, *saved = run_kernel(lay, "fore", info, weights0, patches)
    x, y, t1c, b1c, hidden = hold(x, y, t1c, b1c, hidden)
    weights1 = [t1, x, t1c, lay.exchange(x, CORE), b1, y, b1c, lay.exchange(y, CORE)]
    outputs, grad, *grads1 = run_kernel(lay, "both", info, weights1, hidden, dn=cotangent)

    far1, bfar1, near1, bnear1 = scatter_core(lay, grads1)
    far1, bfar1, grad = hold(far1, bfar1, grad)
    x, y = lay.exchange(far1, *SECOND), lay.exchange(bfar1, NEAR)
    patch_grad, *grads0 = run_kernel(lay, "back", info, weights0, patches, saved=saved, dn=grad)
    x, y, patch_grad, outputs, *grads0 = hold(x, y, patch_grad, outputs, *grads0)
    top1, b1 = add(add(*near1), x), add(add(*bnear1), y)
    u, v = lay.exchange(low(top1[1]), *SCATTER_T[1]), lay.exchange(low(b1[1]), *SCATTER_B[1])
    far0, bfar0, near0, bnear0 = scatter_core(lay, grads0)
    far0, bfar0, outputs, patch_grad = hold(far0, bfar0, outputs, patch_grad)
    x, y = lay.exchange(far0, *SECOND), lay.exchange(bfar0, NEAR)
    x, y, u, v, outputs, patch_grad = hold(x, y, u, v, tilt(outputs), tilt(patch_grad))
    top1, b1 = add(top1[0], u), add(b1[0], v)
    top0, b0 = add(add(*near0), x), add(add(*bnear0), y)
    for k in (1, 2):
        sends = [(low(v[1]), f) for v, f in ((top0, SCATTER_T[k]), (b0, SCATTER_B[k]), (top1, SCATTER_T[k + 1]), (b1, SCATTER_B[k + 1]))]
        x, y, u, v = move(lay, *sends, join=True)
        top0, b0, top1, b1 = add(top0[0], x), add(b0[0], y), add(top1[0], u), add(b1[0], v)
    send, send_b = hold(low(top0[1]), low(b0[1]))
    x, y = lay.exchange(send, *SCATTER_T[3]), lay.exchange(send_b, *SCATTER_B[3])
    last1 = lay.exchange(top1[1], CORE)
    b0 = add(b0[0], y)
    fields0, fields1 = part_fields(lay, "b", b0), part_fields(lay, "b", b1)
    small = [jnp.stack(v) for v in zip(*[unpack_small_grads(lay, f[9], me) for f in (fields0, fields1)])]
    fields1.update(end_fields(lay, me, top1, last1))
    x, *small = hold(x, *small)
    top0 = add(top0[0], x)
    fields0.update(end_fields(lay, me, top0, lay.exchange(top0[1], CORE)))
    outputs, patch_grad = outputs.transpose(1, 0, 2), patch_grad.transpose(1, 0, 2)
    return [outputs, patch_grad] + join_large(lay, fields0, fields1) + small


def tilt(v):
    return v[:, :P_SIZE].transpose(1, 0, 2)


def describe(me, size_class):
    return jnp.concatenate([size_class, jnp.stack([me[a] for a in ("core", "x", "z", "y")]).astype(jnp.int32)])


def spread(v):
    return jnp.pad(v, ((0, 0), (0, RMAX - P_SIZE), (0, 0)))


def plain_path(lay, me, size_class, params, patches, cotangent):
    packed = []
    for w_in, w_out, spatial, vectors in zip(*params):
        fields = pack_large(lay, w_in, w_out) + [pack_small(lay, spatial, vectors, me)]
        packed.append({p: part_of(fields, p) for p in PARTS})
    info, patches, cotangent = describe(me, size_class), spread(patches), spread(cotangent)
    weights0, weights1 = [gather_plain(lay, p, me) for p in packed]
    hidden, *saved = run_kernel(lay, "fore", info, weights0, patches)
    outputs, grad, *grads1 = run_kernel(lay, "both", info, weights1, hidden, dn=cotangent)
    patch_grad, *grads0 = run_kernel(lay, "back", info, weights0, patches, saved=saved, dn=grad)
    outputs, patch_grad = outputs[:, :P_SIZE], patch_grad[:, :P_SIZE]
    layers = []
    for grads in (grads0, grads1):
        sums = scatter_plain(lay, grads, me)
        layers.append({f: v for p in PARTS for f, v in part_fields(lay, p, sums[p]).items()})
    small = [jnp.stack(v) for v in zip(*[unpack_small_grads(lay, f[9], me) for f in layers])]
    return [outputs, patch_grad] + join_large(lay, *layers) + small


def scatter_plain(lay, grads, me):
    gwin, gwout, gframes = grads
    gwin = gwin.reshape(NH, lay.count, lay.rows, CW)
    gwout = gwout.reshape(lay.count, NG, lay.rows, D)
    gframes = gframes.reshape(lay.count, lay.small, CW)
    fields = [gwin[j] for j in range(NH)] + [gwout[:, k] for k in range(NG)] + [gframes]
    result = {}
    for p in PARTS:
        dims = ("core",) + PART_DIMS[p]
        value = jnp.concatenate([fields[f] for f in PART_FIELDS[p]], axis=1)
        value = value.reshape(lay.size["z"], 2, 2, lay.size["y"], lay.part_rows(p), CW)
        value = value.transpose([("z", "x", "core", "y").index(a) for a in dims] + [4, 5])
        for k, axis in enumerate(dims):
            n = lay.size[axis]
            value = jnp.take(value, lax.rem(me[axis] + jnp.arange(n), n), axis=k)
        for axis in dims:
            value = ring_scatter(lay, value, axis)
        result[p] = value
    return result


def unpack_small_grads(lay, rows, me):
    index = lay.index(me)
    sp = rows[0 : lay.sp_rows, 0:P_SIZE].reshape(-1)
    sp = lax.dynamic_slice(sp, (lax.rem(index * lay.sp_shard, P_SIZE),), (lay.sp_shard,))
    vec = rows[lay.sp_rows : lay.sp_rows + lay.vec_rows, 0:128].reshape(-1)
    return sp, lax.dynamic_slice(vec, (lax.rem(index * lay.vec_shard, 128),), (lay.vec_shard,))


def per_device(mesh_shape, patches, cotangent, size_class, w_in, w_out, spatial, vectors):
    lay = Layout(mesh_shape, spatial.shape[1], vectors.shape[1])
    wide, narrow = lax.axis_index("wide"), lax.axis_index("narrow")
    me = {"core": lax.rem(wide, 2), "x": lax.rem(wide // 2, 2), "z": wide // 4, "y": narrow}
    params = w_in, w_out, spatial, vectors
    path = native_path if lay.native else plain_path
    return tuple(path(lay, me, size_class, params, patches, cotangent))


def solution(mesh):
    shape = (mesh.shape["wide"], mesh.shape["narrow"])
    rows = P(AXES, None, None)
    flat = P(None, AXES)
    return jax.shard_map(
        functools.partial(per_device, shape),
        mesh=mesh,
        in_specs=(rows, rows, P(AXES), flat, flat, flat, flat),
        out_specs=(rows, rows, flat, flat, flat, flat),
        check_vma=False,
    )
```

```python
import functools
import jax
import jax.numpy as jnp
import numpy as np
from jax import lax
from jax.experimental import pallas as pl
from jax.experimental.pallas import tpu as pltpu
from jax.sharding import PartitionSpec as P

D = 512
H = 3072
P_SIZE = 324
LAYERS = 2
G = 1536
EPS = 1e-05
CW = 512
NG = G // CW
NH = H // CW
RMAX = 336
COUNTS = (100, 196, 324)
F32 = jnp.float32
BF16 = jnp.bfloat16
O_LN1G, O_LN1S, O_INB = 0, D, 2 * D
O_LN2G, O_LN2S, O_OUTB = 2 * D + H, 2 * D + H + G, 2 * D + H + 2 * G
VUSED = 3 * D + H + 2 * G
VROWS = VUSED // 128
VPAD = (VROWS + 15) // 16 * 16
GELU_C = 0.7978845608028654
GELU_A = 0.044715
AXES = ("wide", "narrow")
VLIM = {"plain": 60 * 2**20, "fore": 46 * 2**20, "both": 40 * 2**20, "back": 41 * 2**20}
PART_FIELDS = {"a": (0, 1, 6), "d": (2, 3, 7), "b": (4, 5, 8, 9)}
PART_DIMS = {"a": ("y", "x", "z"), "d": ("x", "y", "z"), "b": ("z", "y", "x")}
PARTS = ("a", "d", "b")
KEPT = ("fore", "both", "back")
PIECES = ("t00", "t01", "t10", "t11", "b00", "b01", "b10", "b11")


class Layout:
    def __init__(self, mesh_shape, sp_shard, vec_shard):
        wide, narrow = mesh_shape
        self.size = {"core": 2, "x": 2, "z": wide // 4, "y": narrow}
        self.count = wide * narrow
        self.rows = D // self.count
        self.sp_shard, self.vec_shard = sp_shard, vec_shard
        self.sp_rows = (sp_shard + 2 * P_SIZE - 2) // P_SIZE
        self.vec_rows = (vec_shard + 2 * 128 - 2) // 128
        self.native = self.rows == 16 and narrow == 2 and wide == 16
        self.small = (self.sp_rows + self.vec_rows + 7) // 8 * 8

    def part_rows(self, part):
        return sum(self.small if f == 9 else self.rows for f in PART_FIELDS[part])

    def offsets(self, part):
        spots, at = [], 0
        for f in PART_FIELDS[part]:
            spots.append((f, at))
            at += self.small if f == 9 else self.rows
        return spots

    def index(self, at):
        return ((at["z"] * 2 + at["x"]) * 2 + at["core"]) * self.size["y"] + at["y"]

    def coords(self, i):
        y, wide = i % self.size["y"], i // self.size["y"]
        return {"core": wide % 2, "x": wide // 2 % 2, "z": wide // 4, "y": y}

    def shift(self, value, axis, step=1):
        pairs = []
        for i in range(self.count):
            at = self.coords(i)
            at[axis] = (at[axis] + step) % self.size[axis]
            pairs.append((i, self.index(at)))
        return lax.ppermute(value, AXES, pairs)

    def exchange(self, value, *flips):
        pairs = []
        for i in range(self.count):
            at = self.coords(i)
            for axis, bit in flips[at["core"] % len(flips)].items():
                at[axis] ^= bit
            pairs.append((i, self.index(at)))
        return lax.ppermute(value, AXES, pairs)


CORE, NEAR, FAR = {"core": 1}, {"z": 1}, {"z": 2}
FIRST, SECOND = ({"x": 1}, {"y": 1}), ({"y": 1}, {"x": 1})


def dot(a, b):
    return lax.dot_general(a, b, (((1,), (0,)), ((), ())), preferred_element_type=F32)


def dot_nt(a, b):
    return lax.dot_general(a, b, (((1,), (1,)), ((), ())), preferred_element_type=F32)


def gelu_both(z):
    z2 = z * z
    t = jnp.tanh(z * (GELU_C + (GELU_C * GELU_A) * z2))
    w = 0.5 * t + 0.5
    h = z * w
    return h, w + (h - h * w) * (2.0 * GELU_C + (6.0 * GELU_C * GELU_A) * z2)


def rows_sum8(x):
    rows, cols = x.shape
    return jnp.sum(x.reshape(rows // 8, 8, cols), axis=0)


def picker(lay, rows, cols, first, per, length, width):
    r = lax.broadcasted_iota(jnp.int32, (rows, cols), 0)
    c = lax.broadcasted_iota(jnp.int32, (rows, cols), 1)
    i, t = c // lay.small, c % lay.small - first
    hit = (t >= 0) & (t < per) & (r == (i * length) // width + t)
    return jnp.where(hit, 1.0, 0.0).astype(BF16)


def unpack_small(lay, frames_ref, vec_ref, sc_ref, st_ref):
    count = lay.count * lay.small
    ms = picker(lay, RMAX, count, 0, lay.sp_rows, lay.sp_shard, P_SIZE)
    mv = picker(lay, VPAD, count, lay.sp_rows, lay.vec_rows, lay.vec_shard, 128)
    sp = dot(ms, frames_ref[:, 0:384])
    vec = dot(mv, frames_ref[:, 0:128])
    for r in range(VROWS):
        vec_ref[:, r * 128 : (r + 1) * 128] = vec[r : r + 1, :]
    row = lax.broadcasted_iota(jnp.int32, (RMAX, RMAX), 0)
    col = lax.broadcasted_iota(jnp.int32, (RMAX, RMAX), 1)
    inside = (row < P_SIZE) & (col < P_SIZE)
    sp = sp[:, 0:RMAX]
    sp_t = jnp.transpose(sp)
    sc_ref[...] = jnp.where(inside, sp, jnp.where((col == P_SIZE) & (row < P_SIZE), sp_t, 0.0)).astype(BF16)
    if st_ref is not None:
        st_ref[...] = jnp.where(inside, sp_t, 0.0).astype(BF16)


def role_blocks(lay, me, sign):
    for who in range(2):
        role = me["core"] ^ who
        for second in range(2):
            for first, k1, k2, core in np.ndindex(2, 2, 2, 2):
                swap = role * (first ^ second)
                at = {"z": me["z"] ^ (k1 + 2 * k2), "core": role ^ core, "x": me["x"] ^ first ^ swap, "y": me["y"] ^ second ^ swap}
                yield who, second, (first, k1, k2, core), role, lay.index(at)


def both_blocks(lay, me, sign):
    for who in range(2):
        role = me["core"] ^ who
        for k1 in range(2):
            for first, k2, second in np.ndindex(2, 2, 2):
                swap = role * (first ^ second)
                at = {"z": me["z"] ^ (k1 + 2 * k2), "core": role, "x": me["x"] ^ first ^ swap, "y": me["y"] ^ second ^ swap}
                yield who, k1, (first, k2, second), lay.index(at)


def sixteen(start):
    return pl.ds(pl.multiple_of(start, 16), 16)


def assemble(lay, me, given, win_ref, wout_ref, frames_ref):
    for who, second, place, role, i in role_blocks(lay, me, -1):
        src = given["t%d%d" % (who, second)]
        for t in range(2):
            win_ref[2 * role + t, sixteen(i * 16), :] = src[place + (slice(16 * t, 16 * t + 16),)]
        wout_ref[sixteen(i * 48 + 16 * role), :] = src[place + (slice(32, 48),)]
    for who, z, place, i in both_blocks(lay, me, -1):
        src = given["b%d%d" % (who, z)]
        for t in range(2):
            win_ref[4 + t, sixteen(i * 16), :] = src[place + (slice(16 * t, 16 * t + 16),)]
        wout_ref[sixteen(i * 48 + 32), :] = src[place + (slice(32, 48),)]
        frames_ref[sixteen(i * 16), :] = src[place + (slice(48, 64),)]


def forward_part(rows, valid, r_ref, vec_ref, win_ref, wout_ref, sc_ref, sv, save):
    h, hp = sv["h"], sv["hp"]
    r, k, xh, a = first_norm(rows, valid, r_ref, vec_ref)
    tot = jnp.zeros((rows, 1), F32)
    for j in list(range(NG, NH)) + list(range(NG)):
        z = dot(a, win_ref[j]) + vec_ref[:, O_INB + j * CW : O_INB + (j + 1) * CW]
        h[j], hpj = gelu_both(z)
        hp[j] = hpj
        if j >= NG:
            tot = tot + jnp.sum(h[j], axis=1, keepdims=True)
    mu2 = tot * (1.0 / G)
    ssq = jnp.zeros((rows, 1), F32)
    for j in range(NG):
        vc = h[NG + j] - mu2
        ssq = ssq + jnp.sum(vc * vc, axis=1, keepdims=True)
    k2 = lax.rsqrt(ssq * (1.0 / G) + EPS)
    one = jnp.where(lax.broadcasted_iota(jnp.int32, (rows, 1), 0) == P_SIZE, 1.0, 0.0)
    for j in range(NG):
        lo = j * CW
        xh2 = (h[NG + j] - mu2) * k2
        sv["v"][j] = xh2.astype(sv["v"].dtype)
        sv["hv"][j] = (hp[NG + j] * k2).astype(sv["hv"].dtype)
        q = xh2 * vec_ref[:, O_LN2G + lo : O_LN2G + lo + CW] + vec_ref[:, O_LN2S + lo : O_LN2S + lo + CW]
        sv["q"][j] = jnp.where(valid, q, one).astype(BF16)
    o = None
    for j in range(NG):
        s = dot(sc_ref[...], sv["q"][j])
        u = h[j]
        e = (u * s).astype(BF16)
        sv["sh"][j] = (hp[j] * s).astype(sv["sh"].dtype)
        sv["e"][j] = e
        if save:
            sv["u"][j] = u.astype(BF16)
        part = dot(e, wout_ref[j * CW : (j + 1) * CW, :])
        o = part if o is None else o + part
    o = jnp.where(valid, r + (o + vec_ref[:, O_OUTB : O_OUTB + D]), 0.0)
    return (k, xh, a), o


def first_norm(rows, valid, r_ref, vec_ref):
    r = jnp.where(valid, r_ref[0, 0:rows, :].astype(F32), 0.0)
    mu = jnp.mean(r, axis=1, keepdims=True)
    c = r - mu
    k = lax.rsqrt(jnp.mean(c * c, axis=1, keepdims=True) + EPS)
    xh = c * k
    a = (xh * vec_ref[:, O_LN1G : O_LN1G + D] + vec_ref[:, O_LN1S : O_LN1S + D]).astype(BF16)
    return r, k, xh, a


def backward_part(rows, valid, norm, dn_ref, vec_ref, win_ref, wout_ref, st_ref, sv, acc):
    k, xh, a = norm
    sv["xh1"][0:rows, :] = xh
    sv["at"][0:D, 0:rows] = jnp.transpose(a)
    dn = jnp.where(valid, dn_ref[0, 0:rows, :].astype(F32), 0.0)
    do = dn.astype(BF16)
    dot_t = jnp.transpose(do)
    gvec = acc["vec"]
    gvec[:, O_OUTB : O_OUTB + D] += rows_sum8(do.astype(F32))
    for j in range(NG):
        acc["wout"][j] += dot(dot_t, sv["e"][j, 0:rows, :])
        de = dot_nt(do, wout_ref[j * CW : (j + 1) * CW, :])
        sv["dz"][j, 0:rows, :] = (de * sv["sh"][j].astype(F32)).astype(BF16)
        sv["ds"][j, 0:rows, :] = (de * sv["u"][j].astype(F32)).astype(BF16)
    gs = None
    for j in range(NG):
        part = dot_nt(sv["ds"][j, 0:rows, :], sv["q"][j, 0:rows, :])
        gs = part if gs is None else gs + part
    acc["sp"][...] += gs
    m1 = jnp.zeros((rows, 1), F32)
    m2 = jnp.zeros((rows, 1), F32)
    for j in range(NG):
        lo = j * CW
        dq = jnp.where(valid, dot(st_ref[...], sv["ds"][j, 0:rows, :]), 0.0)
        sv["dq"][j, 0:rows, :] = dq
        gain = vec_ref[:, O_LN2G + lo : O_LN2G + lo + CW]
        w = dq * sv["v"][j].astype(F32)
        gvec[:, O_LN2G + lo : O_LN2G + lo + CW] += rows_sum8(w)
        gvec[:, O_LN2S + lo : O_LN2S + lo + CW] += rows_sum8(dq)
        m1 = m1 + jnp.sum(dq * gain, axis=1, keepdims=True)
        m2 = m2 + jnp.sum(w * gain, axis=1, keepdims=True)
    m1 = m1 * (1.0 / G)
    m2 = m2 * (1.0 / G)
    for j in range(NG):
        lo = j * CW
        gain = vec_ref[:, O_LN2G + lo : O_LN2G + lo + CW]
        dv = (sv["dq"][j, 0:rows, :] * gain - m1 - sv["v"][j].astype(F32) * m2)
        sv["dz"][NG + j, 0:rows, :] = (dv * sv["hv"][j].astype(F32)).astype(BF16)
    da = None
    for j in range(NH):
        dz = sv["dz"][j, 0:rows, :]
        acc["win"][j] += dot(sv["at"][0:D, 0:rows], dz)
        gvec[:, O_INB + j * CW : O_INB + (j + 1) * CW] += rows_sum8(dz.astype(F32))
        part = dot_nt(dz, win_ref[j])
        da = part if da is None else da + part
    xh = sv["xh1"][0:rows, :]
    gain = vec_ref[:, O_LN1G : O_LN1G + D]
    w = da * xh
    gvec[:, O_LN1G : O_LN1G + D] += rows_sum8(w)
    gvec[:, O_LN1S : O_LN1S + D] += rows_sum8(da)
    t = da * gain
    mt = jnp.mean(t, axis=1, keepdims=True)
    mx = jnp.mean(w * gain, axis=1, keepdims=True)
    return dn + k * (t - mt - xh * mx)


def gather_grads(lay, acc, wout_ref, frames_ref):
    for j in range(NG):
        wout_ref[j * CW : (j + 1) * CW, :] = jnp.transpose(acc["wout"][j]).astype(BF16)
    whole = acc["sp"][...]
    row = lax.broadcasted_iota(jnp.int32, (RMAX, RMAX), 0)
    col = lax.broadcasted_iota(jnp.int32, (RMAX, RMAX), 1)
    ext = jnp.where(row == P_SIZE, jnp.transpose(whole), jnp.where(row < P_SIZE, whole, 0.0))
    ext = jnp.where(col < P_SIZE, ext, 0.0).astype(BF16)
    sums = jnp.sum(acc["vec"][...], axis=0, keepdims=True)
    vec = jnp.concatenate([sums[:, r * 128 : (r + 1) * 128] for r in range(VROWS)] + [jnp.zeros((VPAD - VROWS, 128), F32)], axis=0)
    count = lay.count * lay.small
    ms = picker(lay, RMAX, count, 0, lay.sp_rows, lay.sp_shard, P_SIZE)
    mv = picker(lay, VPAD, count, lay.sp_rows, lay.vec_rows, lay.vec_shard, 128)
    tn = (((0,), (0,)), ((), ()))
    frames_ref[...] = jnp.zeros(frames_ref.shape, BF16)
    frames_ref[:, 0:RMAX] = lax.dot_general(ms, ext, tn, preferred_element_type=F32).astype(BF16)
    part = lax.dot_general(mv, vec.astype(BF16), tn, preferred_element_type=F32)
    frames_ref[:, 0:128] += part.astype(BF16)


def scatter_grads(lay, me, acc, wout_ref, frames_ref, out):
    for who, second, place, role, i in role_blocks(lay, me, 1):
        dst = out["t%d%d" % (who, second)]
        for t in range(2):
            dst[place + (slice(16 * t, 16 * t + 16),)] = acc["win"][2 * role + t, sixteen(i * 16), :].astype(BF16)
        dst[place + (slice(32, 48),)] = wout_ref[sixteen(i * 48 + 16 * role), :]
    for who, z, place, i in both_blocks(lay, me, 1):
        dst = out["b%d%d" % (who, z)]
        for t in range(2):
            dst[place + (slice(16 * t, 16 * t + 16),)] = acc["win"][4 + t, sixteen(i * 16), :].astype(BF16)
        dst[place + (slice(32, 48),)] = wout_ref[sixteen(i * 48 + 32), :]
        dst[place + (slice(48, 64),)] = frames_ref[sixteen(i * 16), :]


def read_me(info_ref, images):
    return {axis: info_ref[images + k] for k, axis in enumerate(("core", "x", "z", "y"))}


class Names:
    def __init__(self, refs):
        self.refs = list(refs)

    def take(self, names):
        got = dict(zip(names, self.refs))
        self.refs = self.refs[len(names) :]
        return got


WEIGHTS = ("win", "wout", "frames")
SAVED = ("u", "sh", "v", "hv", "q", "e")


def kernel_body(lay, images, mode, scratch_names, info_ref, *refs):
    names = Names(refs)
    given = names.take(weight_names(lay))
    r_ref = names.take(["r"])["r"]
    saved = names.take(SAVED) if mode == "back" else {}
    dn_ref = names.take(["dn"])["dn"] if mode != "fore" else None
    out_ref = names.take(["out"])["out"] if mode != "back" else None
    if mode == "fore":
        saved = names.take(SAVED)
    gr_ref = names.take(["gr"])["gr"] if mode != "fore" else None
    grad_refs = names.take(grad_names(lay)) if mode != "fore" else {}
    sv = names.take(scratch_names)
    w = sv if lay.native else given
    sv.update({k: saved[k].at[0] for k in saved})
    if mode == "both":
        sv.update(u=sv["h"], sh=sv["hp"], v=sv["h"].at[NG:NH], hv=sv["hp"].at[NG:NH])
    acc = {k: sv.get("a" + k) for k in ("win", "wout", "sp", "vec")}
    b = pl.program_id(0)

    @pl.when(b == 0)
    def _():
        if lay.native:
            assemble(lay, read_me(info_ref, images), given, w["win"], w["wout"], w["frames"])
        unpack_small(lay, w["frames"], sv["vec"], sv["sc"], sv.get("st"))
        if mode != "fore":
            for ref in acc.values():
                ref[...] = jnp.zeros(ref.shape, F32)

    cls = info_ref[b]
    n = jnp.where(cls == 0, COUNTS[0], jnp.where(cls == 1, COUNTS[1], COUNTS[2]))
    valid = lax.broadcasted_iota(jnp.int32, (RMAX, 1), 0) < n
    if mode == "back":
        _, k, xh, a = first_norm(RMAX, valid, r_ref, sv["vec"])
        norm = (k, xh, a)
    else:
        norm, o = forward_part(RMAX, valid, r_ref, sv["vec"], w["win"], w["wout"], sv["sc"], sv, mode == "fore")
        out_ref[0] = o
    if mode != "fore":
        gr_ref[0] = backward_part(RMAX, valid, norm, dn_ref, sv["vec"], w["win"], w["wout"], sv["st"], sv, acc)

        @pl.when(b == pl.num_programs(0) - 1)
        def _():
            if lay.native:
                gather_grads(lay, acc, w["wout"], w["frames"])
                scatter_grads(lay, read_me(info_ref, images), acc, w["wout"], w["frames"], grad_refs)
            else:
                gather_grads(lay, acc, grad_refs["gwout"], grad_refs["gframes"])
                grad_refs["gwin"][...] = acc["win"][...].astype(BF16)


def piece_shape(lay, piece):
    return ((2, 2, 2, 2) if piece[0] == "t" else (2, 2, 2)) + (lay.part_rows("a" if piece[0] == "t" else "b"), CW)


def scratch_for(lay, mode):
    big = lambda m, dt: pltpu.VMEM((m, RMAX, CW), dt)
    wide = lambda dt: pltpu.VMEM((RMAX, D), dt)
    made = {}
    if lay.native:
        made.update(win=pltpu.VMEM((NH, D, CW), BF16), wout=pltpu.VMEM((G, D), BF16), frames=pltpu.VMEM((lay.count * lay.small, CW), BF16))
    made.update(vec=pltpu.VMEM((1, VUSED), F32), sc=pltpu.VMEM((RMAX, RMAX), BF16))
    if mode != "back":
        made.update(h=big(NH, F32), hp=big(NH, F32))
    if mode == "both":
        made.update(q=big(NG, BF16), e=big(NG, BF16))
    if mode != "fore":
        made.update(st=pltpu.VMEM((RMAX, RMAX), BF16), ds=big(NG, BF16), dz=big(NH, BF16), dq=big(NG, F32), xh1=wide(F32))
        made.update(at=pltpu.VMEM((D, RMAX), BF16), awin=pltpu.VMEM((NH, D, CW), F32), awout=pltpu.VMEM((NG, D, CW), F32))
        made.update(asp=pltpu.VMEM((RMAX, RMAX), F32), avec=pltpu.VMEM((8, VUSED), F32))
    return made


def weight_names(lay):
    if not lay.native:
        return list(WEIGHTS)
    return list(PIECES)


def grad_names(lay):
    return list(PIECES) if lay.native else ["gwin", "gwout", "gframes"]


def image_spec():
    return pl.BlockSpec((1, RMAX, D), lambda b, c: (b, 0, 0))


def saved_shapes(images):
    return [jax.ShapeDtypeStruct((images, NG, RMAX, CW), BF16) for _ in SAVED]


def saved_specs():
    spec = pl.BlockSpec((1, NG, RMAX, CW), lambda b, c: (b, 0, 0, 0))
    return [spec] * len(SAVED)


def run_kernel(lay, mode, info, weights, r, saved=None, dn=None):
    images = r.shape[0]
    image = jax.ShapeDtypeStruct((images, RMAX, D), F32)
    whole = pl.BlockSpec(memory_space=pltpu.VMEM)
    operands = list(weights) + [r]
    if lay.native and mode in KEPT:
        operands = [pltpu.with_memory_space_constraint(w, pltpu.VMEM) for w in weights] + [r]
    in_specs = [whole] * len(weights) + [image_spec()]
    outs, out_specs = [], []
    if mode == "back":
        operands += list(saved)
        in_specs += saved_specs()
    if mode != "fore":
        operands.append(dn)
        in_specs.append(image_spec())
    if mode != "back":
        outs.append(image)
        out_specs.append(image_spec())
    if mode == "fore":
        outs += saved_shapes(images)
        out_specs += saved_specs()
    if mode != "fore":
        outs.append(image)
        out_specs.append(image_spec())
        if lay.native:
            grads = [piece_shape(lay, p) for p in PIECES]
        else:
            grads = [(NH, D, CW), (G, D), (lay.count * lay.small, CW)]
        outs += [pltpu.VMEM(s, BF16) if lay.native else jax.ShapeDtypeStruct(s, BF16) for s in grads]
        out_specs += [whole] * len(grads)
    scratch = scratch_for(lay, mode)
    return pl.pallas_call(
        functools.partial(kernel_body, lay, images, mode, list(scratch)),
        grid_spec=pltpu.PrefetchScalarGridSpec(
            num_scalar_prefetch=1, grid=(images,), in_specs=in_specs, out_specs=out_specs, scratch_shapes=list(scratch.values())
        ),
        out_shape=outs,
        compiler_params=pltpu.CompilerParams(vmem_limit_bytes=VLIM[mode if lay.native else "plain"]),
        name="layer_" + mode,
    )(info, *operands)


def pack_large(lay, w_in, w_out):
    win = w_in.reshape(lay.rows, NH, CW)
    wout = w_out.reshape(NG, lay.rows, D)
    return [win[:, j] for j in range(NH)] + [wout[k] for k in range(NG)]


def pack_small(lay, spatial, vectors, me):
    index = lay.index(me)
    sp_at = lax.rem(index * lay.sp_shard, P_SIZE)
    vec_at = lax.rem(index * lay.vec_shard, 128)
    sp = lax.dynamic_update_slice(jnp.zeros((lay.sp_rows * P_SIZE,), BF16), spatial, (sp_at,)).reshape(lay.sp_rows, P_SIZE)
    vec = lax.dynamic_update_slice(jnp.zeros((lay.vec_rows * 128,), BF16), vectors, (vec_at,)).reshape(lay.vec_rows, 128)
    sp = jnp.pad(sp, ((0, 0), (0, CW - P_SIZE)))
    vec = jnp.pad(vec, ((0, lay.small - lay.sp_rows - lay.vec_rows), (0, CW - 128)))
    return jnp.concatenate([sp, vec])


def part_of(fields, part):
    return jnp.concatenate([fields[f] for f in PART_FIELDS[part]])


def ring_gather(lay, value, axis):
    pieces = [value]
    for _ in range(lay.size[axis] - 1):
        pieces.append(lay.shift(pieces[-1], axis))
    return pieces


def hold(*values):
    return lax.optimization_barrier(values)


def move(lay, *items, join=False):
    values = hold(*[value for value, _ in items])
    items = [(value, flips) for value, (_, flips) in zip(values, items)]
    return hold(*(together(lay, *items) if join else [lay.exchange(value, *flips) for value, flips in items]))


def together(lay, *items):
    got = {}
    for k, (_, flips) in enumerate(items):
        same = [i for i, (_, f) in enumerate(items) if f == flips]
        if same[0] != k:
            continue
        if len(same) == 1:
            got[k] = lay.exchange(items[k][0], *flips)
            continue
        flat = [items[i][0].reshape(-1, CW) for i in same]
        joined, at = lay.exchange(jnp.concatenate(flat), *flips), 0
        for i, v in zip(same, flat):
            got[i] = joined[at : at + v.shape[0]].reshape(items[i][0].shape)
            at += v.shape[0]
    return [got[k] for k in range(len(items))]


def gather_start(lay, packed, me):
    even = me["core"] == 0
    keep = jnp.where(even, packed["a"], packed["d"])
    give = jnp.where(even, packed["d"], packed["a"])
    return jnp.stack([keep, lay.exchange(give, CORE)])


GATHER_T = ((FAR,), (NEAR,), FIRST, SECOND)
GATHER_B = (SECOND, (FAR,), FIRST, (NEAR,))


def gather_plain(lay, packed, me):
    win, wout, frames = [None] * NH, [None] * NG, None
    for p in PARTS:
        dims = ("core",) + PART_DIMS[p]
        value = packed[p]
        for axis in reversed(dims):
            value = jnp.stack(ring_gather(lay, value, axis))
        for k, axis in enumerate(dims):
            n = lay.size[axis]
            value = jnp.take(value, lax.rem(me[axis] - jnp.arange(n) + n, n), axis=k)
        order = [dims.index(a) for a in ("z", "x", "core", "y")]
        value = value.transpose(order + [4, 5]).reshape(lay.count, lay.part_rows(p), CW)
        for f, at in lay.offsets(p):
            if f < 6:
                win[f] = value[:, at : at + lay.rows].reshape(D, CW)
            elif f < 9:
                wout[f - 6] = value[:, at : at + lay.rows]
            else:
                frames = value[:, at : at + lay.small].reshape(lay.count * lay.small, CW)
    return [jnp.stack(win), jnp.stack(wout, axis=1).reshape(G, D), frames]


def ring_scatter(lay, value, axis):
    n = lay.size[axis]
    total = value[n - 1].astype(F32)
    for k in range(n - 2, -1, -1):
        total = lay.shift(total.astype(BF16), axis).astype(F32) + value[k].astype(F32)
    return total


def low(v):
    return v.astype(BF16)


def add(mine, got):
    return mine.astype(F32) + got.astype(F32)


def scatter_core(lay, grads):
    t00, t01, t10, t11, b00, b01, b10, b11 = grads
    t11, b11 = hold(t11, b11)
    far = low(add(t01, lay.exchange(t11, CORE)))
    bfar = low(add(b01, lay.exchange(b11, CORE)))
    t10, _ = hold(t10, far)
    b10, _ = hold(b10, bfar)
    return far, bfar, (t00, lay.exchange(t10, CORE)), (b00, lay.exchange(b10, CORE))


SCATTER_T = (SECOND, FIRST, (NEAR,), (FAR,))
SCATTER_B = ((NEAR,), FIRST, (FAR,), SECOND)


def part_fields(lay, part, rows):
    return {f: rows[at : at + (lay.small if f == 9 else lay.rows)] for f, at in lay.offsets(part)}


def end_fields(lay, me, top, other):
    even = me["core"] == 0
    a, d = jnp.where(even, top[0], other), jnp.where(even, other, top[0])
    return {**part_fields(lay, "a", a), **part_fields(lay, "d", d)}


def join_large(lay, *layers):
    gwin = [jnp.stack([fields[j] for j in range(NH)], axis=1).reshape(-1) for fields in layers]
    gwout = [jnp.concatenate([fields[6 + k] for k in range(NG)]).reshape(-1) for fields in layers]
    return [jnp.stack(gwin), jnp.stack(gwout)]


def native_path(lay, me, size_class, params, patches, cotangent):
    stack = lambda v, got: jnp.stack([v, got])
    info = size_class
    w_in, w_out, spatial, vectors = params
    large = pack_large(lay, w_in[0], w_out[0])
    t0 = gather_start(lay, {p: part_of(large, p) for p in "ad"}, me)
    t0, spatial, vectors, w_in, w_out = hold(t0, spatial, vectors, w_in, w_out)
    x = lay.exchange(t0, *GATHER_T[0])
    b0 = part_of(large + [pack_small(lay, spatial[0], vectors[0], me)], "b")
    y = lay.exchange(b0, *GATHER_B[0])
    x, y, w_in, w_out, spatial, vectors = hold(x, y, w_in, w_out, spatial, vectors)
    large = pack_large(lay, w_in[1], w_out[1])
    t1 = gather_start(lay, {p: part_of(large, p) for p in "ad"}, me)
    b1 = part_of(large + [pack_small(lay, spatial[1], vectors[1], me)], "b")
    t0, b0, patches, cotangent, info = hold(stack(t0, x), stack(b0, y), patches, cotangent, info)
    for k in (1, 2):
        x, y = lay.exchange(t0, *GATHER_T[k]), lay.exchange(b0, *GATHER_B[k])
        u, v = lay.exchange(t1, *GATHER_T[k - 1]), lay.exchange(b1, *GATHER_B[k - 1])
        if k == 1:
            info, patches, cotangent = describe(me, info), spread(patches), spread(cotangent)
        x, y, u, v, patches, cotangent, info = hold(x, y, u, v, patches, cotangent, info)
        t0, b0, t1, b1 = hold(stack(t0, x), stack(b0, y), stack(t1, u), stack(b1, v))
    t0c, b0c = lay.exchange(t0, CORE), lay.exchange(b0, CORE)
    x, y, u, v = [lay.exchange(g, *f) for g, f in ((t0, GATHER_T[3]), (b0, GATHER_B[3]), (t1, GATHER_T[2]), (b1, GATHER_B[2]))]
    x, y, u, v = hold(x, y, u, v)
    weights0 = [t0, x, t0c, lay.exchange(x, CORE), b0, y, b0c, lay.exchange(y, CORE)]
    t1, b1 = stack(t1, u), stack(b1, v)
    x, y, t1c, b1c = [lay.exchange(v, *f) for v, f in ((t1, SECOND), (b1, (NEAR,)), (t1, (CORE,)), (b1, (CORE,)))]
    hidden, *saved = run_kernel(lay, "fore", info, weights0, patches)
    x, y, t1c, b1c, hidden = hold(x, y, t1c, b1c, hidden)
    weights1 = [t1, x, t1c, lay.exchange(x, CORE), b1, y, b1c, lay.exchange(y, CORE)]
    outputs, grad, *grads1 = run_kernel(lay, "both", info, weights1, hidden, dn=cotangent)

    far1, bfar1, near1, bnear1 = scatter_core(lay, grads1)
    x, y = lay.exchange(far1, *SECOND), lay.exchange(bfar1, NEAR)
    _, _, grad = hold(far1, bfar1, grad)
    patch_grad, *grads0 = run_kernel(lay, "back", info, weights0, patches, saved=saved, dn=grad)
    x, y, patch_grad, outputs, *grads0 = hold(x, y, patch_grad, outputs, *grads0)
    top1, b1 = add(add(*near1), x), add(add(*bnear1), y)
    u, v = lay.exchange(low(top1[1]), *SCATTER_T[1]), lay.exchange(low(b1[1]), *SCATTER_B[1])
    far0, bfar0, near0, bnear0 = scatter_core(lay, grads0)
    far0, bfar0, outputs, patch_grad = hold(far0, bfar0, outputs, patch_grad)
    x, y = lay.exchange(far0, *SECOND), lay.exchange(bfar0, NEAR)
    x, y, u, v, outputs, patch_grad = hold(x, y, u, v, tilt(outputs), tilt(patch_grad))
    top1, b1 = add(top1[0], u), add(b1[0], v)
    top0, b0 = add(add(*near0), x), add(add(*bnear0), y)
    for k in (1, 2):
        sends = [(low(v[1]), f) for v, f in ((top0, SCATTER_T[k]), (b0, SCATTER_B[k]), (top1, SCATTER_T[k + 1]), (b1, SCATTER_B[k + 1]))]
        x, y, u, v = move(lay, *sends, join=True)
        top0, b0, top1, b1 = add(top0[0], x), add(b0[0], y), add(top1[0], u), add(b1[0], v)
    send, send_b = hold(low(top0[1]), low(b0[1]))
    x, last1 = lay.exchange(send, *SCATTER_T[3]), lay.exchange(top1[1], CORE)
    send_b, last1 = hold(send_b, last1)
    y = lay.exchange(send_b, *SCATTER_B[3])
    b0 = add(b0[0], y)
    fields0, fields1 = part_fields(lay, "b", b0), part_fields(lay, "b", b1)
    small = [jnp.stack(v) for v in zip(*[unpack_small_grads(lay, f[9], me) for f in (fields0, fields1)])]
    fields1.update(end_fields(lay, me, top1, last1))
    x, *small = hold(x, *small)
    top0 = add(top0[0], x)
    fields0.update(end_fields(lay, me, top0, lay.exchange(top0[1], CORE)))
    outputs, patch_grad = outputs.transpose(1, 0, 2), patch_grad.transpose(1, 0, 2)
    return [outputs, patch_grad] + join_large(lay, fields0, fields1) + small


def tilt(v):
    return v[:, :P_SIZE].transpose(1, 0, 2)


def describe(me, size_class):
    return jnp.concatenate([size_class, jnp.stack([me[a] for a in ("core", "x", "z", "y")]).astype(jnp.int32)])


def spread(v):
    return jnp.pad(v, ((0, 0), (0, RMAX - P_SIZE), (0, 0)))


def plain_path(lay, me, size_class, params, patches, cotangent):
    packed = []
    for w_in, w_out, spatial, vectors in zip(*params):
        fields = pack_large(lay, w_in, w_out) + [pack_small(lay, spatial, vectors, me)]
        packed.append({p: part_of(fields, p) for p in PARTS})
    info, patches, cotangent = describe(me, size_class), spread(patches), spread(cotangent)
    weights0, weights1 = [gather_plain(lay, p, me) for p in packed]
    hidden, *saved = run_kernel(lay, "fore", info, weights0, patches)
    outputs, grad, *grads1 = run_kernel(lay, "both", info, weights1, hidden, dn=cotangent)
    patch_grad, *grads0 = run_kernel(lay, "back", info, weights0, patches, saved=saved, dn=grad)
    outputs, patch_grad = outputs[:, :P_SIZE], patch_grad[:, :P_SIZE]
    layers = []
    for grads in (grads0, grads1):
        sums = scatter_plain(lay, grads, me)
        layers.append({f: v for p in PARTS for f, v in part_fields(lay, p, sums[p]).items()})
    small = [jnp.stack(v) for v in zip(*[unpack_small_grads(lay, f[9], me) for f in layers])]
    return [outputs, patch_grad] + join_large(lay, *layers) + small


def scatter_plain(lay, grads, me):
    gwin, gwout, gframes = grads
    gwin = gwin.reshape(NH, lay.count, lay.rows, CW)
    gwout = gwout.reshape(lay.count, NG, lay.rows, D)
    gframes = gframes.reshape(lay.count, lay.small, CW)
    fields = [gwin[j] for j in range(NH)] + [gwout[:, k] for k in range(NG)] + [gframes]
    result = {}
    for p in PARTS:
        dims = ("core",) + PART_DIMS[p]
        value = jnp.concatenate([fields[f] for f in PART_FIELDS[p]], axis=1)
        value = value.reshape(lay.size["z"], 2, 2, lay.size["y"], lay.part_rows(p), CW)
        value = value.transpose([("z", "x", "core", "y").index(a) for a in dims] + [4, 5])
        for k, axis in enumerate(dims):
            n = lay.size[axis]
            value = jnp.take(value, lax.rem(me[axis] + jnp.arange(n), n), axis=k)
        for axis in dims:
            value = ring_scatter(lay, value, axis)
        result[p] = value
    return result


def unpack_small_grads(lay, rows, me):
    index = lay.index(me)
    sp = rows[0 : lay.sp_rows, 0:P_SIZE].reshape(-1)
    sp = lax.dynamic_slice(sp, (lax.rem(index * lay.sp_shard, P_SIZE),), (lay.sp_shard,))
    vec = rows[lay.sp_rows : lay.sp_rows + lay.vec_rows, 0:128].reshape(-1)
    return sp, lax.dynamic_slice(vec, (lax.rem(index * lay.vec_shard, 128),), (lay.vec_shard,))


def per_device(mesh_shape, patches, cotangent, size_class, w_in, w_out, spatial, vectors):
    lay = Layout(mesh_shape, spatial.shape[1], vectors.shape[1])
    wide, narrow = lax.axis_index("wide"), lax.axis_index("narrow")
    me = {"core": lax.rem(wide, 2), "x": lax.rem(wide // 2, 2), "z": wide // 4, "y": narrow}
    params = w_in, w_out, spatial, vectors
    path = native_path if lay.native else plain_path
    return tuple(path(lay, me, size_class, params, patches, cotangent))


def solution(mesh):
    shape = (mesh.shape["wide"], mesh.shape["narrow"])
    rows = P(AXES, None, None)
    flat = P(None, AXES)
    return jax.shard_map(
        functools.partial(per_device, shape),
        mesh=mesh,
        in_specs=(rows, rows, P(AXES), flat, flat, flat, flat),
        out_specs=(rows, rows, flat, flat, flat, flat),
        check_vma=False,
    )
```

```python
import functools
import jax
import jax.numpy as jnp
import numpy as np
from jax import lax
from jax.experimental import pallas as pl
from jax.experimental.pallas import tpu as pltpu
from jax.sharding import PartitionSpec as P

D = 512
H = 3072
P_SIZE = 324
LAYERS = 2
G = 1536
EPS = 1e-05
CW = 512
NG = G // CW
NH = H // CW
RMAX = 336
COUNTS = (100, 196, 324)
F32 = jnp.float32
BF16 = jnp.bfloat16
O_LN1G, O_LN1S, O_INB = 0, D, 2 * D
O_LN2G, O_LN2S, O_OUTB = 2 * D + H, 2 * D + H + G, 2 * D + H + 2 * G
VUSED = 3 * D + H + 2 * G
VROWS = VUSED // 128
VPAD = (VROWS + 15) // 16 * 16
GELU_C = 0.7978845608028654
GELU_A = 0.044715
AXES = ("wide", "narrow")
VLIM = {"plain": 60 * 2**20, "fore": 46 * 2**20, "both": 40 * 2**20, "back": 41 * 2**20}
PART_FIELDS = {"a": (0, 1, 6), "d": (2, 3, 7), "b": (4, 5, 8, 9)}
PART_DIMS = {"a": ("y", "x", "z"), "d": ("x", "y", "z"), "b": ("z", "y", "x")}
PARTS = ("a", "d", "b")
KEPT = ("fore", "both", "back")
PIECES = ("t00", "t01", "t10", "t11", "b00", "b01", "b10", "b11")


class Layout:
    def __init__(self, mesh_shape, sp_shard, vec_shard):
        wide, narrow = mesh_shape
        self.size = {"core": 2, "x": 2, "z": wide // 4, "y": narrow}
        self.count = wide * narrow
        self.rows = D // self.count
        self.sp_shard, self.vec_shard = sp_shard, vec_shard
        self.sp_rows = (sp_shard + 2 * P_SIZE - 2) // P_SIZE
        self.vec_rows = (vec_shard + 2 * 128 - 2) // 128
        self.native = self.rows == 16 and narrow == 2 and wide == 16
        self.small = (self.sp_rows + self.vec_rows + 7) // 8 * 8

    def part_rows(self, part):
        return sum(self.small if f == 9 else self.rows for f in PART_FIELDS[part])

    def offsets(self, part):
        spots, at = [], 0
        for f in PART_FIELDS[part]:
            spots.append((f, at))
            at += self.small if f == 9 else self.rows
        return spots

    def index(self, at):
        return ((at["z"] * 2 + at["x"]) * 2 + at["core"]) * self.size["y"] + at["y"]

    def coords(self, i):
        y, wide = i % self.size["y"], i // self.size["y"]
        return {"core": wide % 2, "x": wide // 2 % 2, "z": wide // 4, "y": y}

    def shift(self, value, axis, step=1):
        pairs = []
        for i in range(self.count):
            at = self.coords(i)
            at[axis] = (at[axis] + step) % self.size[axis]
            pairs.append((i, self.index(at)))
        return lax.ppermute(value, AXES, pairs)

    def exchange(self, value, *flips):
        pairs = []
        for i in range(self.count):
            at = self.coords(i)
            for axis, bit in flips[at["core"] % len(flips)].items():
                at[axis] ^= bit
            pairs.append((i, self.index(at)))
        return lax.ppermute(value, AXES, pairs)


CORE, NEAR, FAR = {"core": 1}, {"z": 1}, {"z": 2}
FIRST, SECOND = ({"x": 1}, {"y": 1}), ({"y": 1}, {"x": 1})


def dot(a, b):
    return lax.dot_general(a, b, (((1,), (0,)), ((), ())), preferred_element_type=F32)


def dot_nt(a, b):
    return lax.dot_general(a, b, (((1,), (1,)), ((), ())), preferred_element_type=F32)


def gelu_both(z):
    z2 = z * z
    t = jnp.tanh(z * (GELU_C + (GELU_C * GELU_A) * z2))
    w = 0.5 * t + 0.5
    h = z * w
    return h, w + (h - h * w) * (2.0 * GELU_C + (6.0 * GELU_C * GELU_A) * z2)


def rows_sum8(x):
    rows, cols = x.shape
    return jnp.sum(x.reshape(rows // 8, 8, cols), axis=0)


def picker(lay, rows, cols, first, per, length, width):
    r = lax.broadcasted_iota(jnp.int32, (rows, cols), 0)
    c = lax.broadcasted_iota(jnp.int32, (rows, cols), 1)
    i, t = c // lay.small, c % lay.small - first
    hit = (t >= 0) & (t < per) & (r == (i * length) // width + t)
    return jnp.where(hit, 1.0, 0.0).astype(BF16)


def unpack_small(lay, frames_ref, vec_ref, sc_ref, st_ref):
    count = lay.count * lay.small
    ms = picker(lay, RMAX, count, 0, lay.sp_rows, lay.sp_shard, P_SIZE)
    mv = picker(lay, VPAD, count, lay.sp_rows, lay.vec_rows, lay.vec_shard, 128)
    sp = dot(ms, frames_ref[:, 0:384])
    vec = dot(mv, frames_ref[:, 0:128])
    for r in range(VROWS):
        vec_ref[:, r * 128 : (r + 1) * 128] = vec[r : r + 1, :]
    row = lax.broadcasted_iota(jnp.int32, (RMAX, RMAX), 0)
    col = lax.broadcasted_iota(jnp.int32, (RMAX, RMAX), 1)
    inside = (row < P_SIZE) & (col < P_SIZE)
    sp = sp[:, 0:RMAX]
    sp_t = jnp.transpose(sp)
    sc_ref[...] = jnp.where(inside, sp, jnp.where((col == P_SIZE) & (row < P_SIZE), sp_t, 0.0)).astype(BF16)
    if st_ref is not None:
        st_ref[...] = jnp.where(inside, sp_t, 0.0).astype(BF16)


def role_blocks(lay, me, sign):
    for who in range(2):
        role = me["core"] ^ who
        for second in range(2):
            for first, k1, k2, core in np.ndindex(2, 2, 2, 2):
                swap = role * (first ^ second)
                at = {"z": me["z"] ^ (k1 + 2 * k2), "core": role ^ core, "x": me["x"] ^ first ^ swap, "y": me["y"] ^ second ^ swap}
                yield who, second, (first, k1, k2, core), role, lay.index(at)


def both_blocks(lay, me, sign):
    for who in range(2):
        role = me["core"] ^ who
        for k1 in range(2):
            for first, k2, second in np.ndindex(2, 2, 2):
                swap = role * (first ^ second)
                at = {"z": me["z"] ^ (k1 + 2 * k2), "core": role, "x": me["x"] ^ first ^ swap, "y": me["y"] ^ second ^ swap}
                yield who, k1, (first, k2, second), lay.index(at)


def sixteen(start):
    return pl.ds(pl.multiple_of(start, 16), 16)


def assemble(lay, me, given, win_ref, wout_ref, frames_ref):
    for who, second, place, role, i in role_blocks(lay, me, -1):
        src = given["t%d%d" % (who, second)]
        for t in range(2):
            win_ref[2 * role + t, sixteen(i * 16), :] = src[place + (slice(16 * t, 16 * t + 16),)]
        wout_ref[sixteen(i * 48 + 16 * role), :] = src[place + (slice(32, 48),)]
    for who, z, place, i in both_blocks(lay, me, -1):
        src = given["b%d%d" % (who, z)]
        for t in range(2):
            win_ref[4 + t, sixteen(i * 16), :] = src[place + (slice(16 * t, 16 * t + 16),)]
        wout_ref[sixteen(i * 48 + 32), :] = src[place + (slice(32, 48),)]
        frames_ref[sixteen(i * 16), :] = src[place + (slice(48, 64),)]


def forward_part(rows, valid, r_ref, vec_ref, win_ref, wout_ref, sc_ref, sv, save):
    h, hp = sv["h"], sv["hp"]
    r, k, xh, a = first_norm(rows, valid, r_ref, vec_ref)
    tot = jnp.zeros((rows, 1), F32)
    for j in list(range(NG, NH)) + list(range(NG)):
        z = dot(a, win_ref[j]) + vec_ref[:, O_INB + j * CW : O_INB + (j + 1) * CW]
        h[j], hpj = gelu_both(z)
        hp[j] = hpj
        if j >= NG:
            tot = tot + jnp.sum(h[j], axis=1, keepdims=True)
    mu2 = tot * (1.0 / G)
    ssq = jnp.zeros((rows, 1), F32)
    for j in range(NG):
        vc = h[NG + j] - mu2
        ssq = ssq + jnp.sum(vc * vc, axis=1, keepdims=True)
    k2 = lax.rsqrt(ssq * (1.0 / G) + EPS)
    one = jnp.where(lax.broadcasted_iota(jnp.int32, (rows, 1), 0) == P_SIZE, 1.0, 0.0)
    for j in range(NG):
        lo = j * CW
        xh2 = (h[NG + j] - mu2) * k2
        sv["v"][j] = xh2.astype(sv["v"].dtype)
        sv["hv"][j] = (hp[NG + j] * k2).astype(sv["hv"].dtype)
        q = xh2 * vec_ref[:, O_LN2G + lo : O_LN2G + lo + CW] + vec_ref[:, O_LN2S + lo : O_LN2S + lo + CW]
        sv["q"][j] = jnp.where(valid, q, one).astype(BF16)
    o = None
    for j in range(NG):
        s = dot(sc_ref[...], sv["q"][j])
        u = h[j]
        e = (u * s).astype(BF16)
        sv["sh"][j] = (hp[j] * s).astype(sv["sh"].dtype)
        sv["e"][j] = e
        if save:
            sv["u"][j] = u.astype(BF16)
        part = dot(e, wout_ref[j * CW : (j + 1) * CW, :])
        o = part if o is None else o + part
    o = jnp.where(valid, r + (o + vec_ref[:, O_OUTB : O_OUTB + D]), 0.0)
    return (k, xh, a), o


def first_norm(rows, valid, r_ref, vec_ref):
    r = jnp.where(valid, r_ref[0, 0:rows, :].astype(F32), 0.0)
    mu = jnp.mean(r, axis=1, keepdims=True)
    c = r - mu
    k = lax.rsqrt(jnp.mean(c * c, axis=1, keepdims=True) + EPS)
    xh = c * k
    a = (xh * vec_ref[:, O_LN1G : O_LN1G + D] + vec_ref[:, O_LN1S : O_LN1S + D]).astype(BF16)
    return r, k, xh, a


def backward_part(rows, valid, norm, dn_ref, vec_ref, win_ref, wout_ref, st_ref, sv, acc):
    k, xh, a = norm
    sv["xh1"][0:rows, :] = xh
    sv["at"][0:D, 0:rows] = jnp.transpose(a)
    dn = jnp.where(valid, dn_ref[0, 0:rows, :].astype(F32), 0.0)
    do = dn.astype(BF16)
    dot_t = jnp.transpose(do)
    gvec = acc["vec"]
    gvec[:, O_OUTB : O_OUTB + D] += rows_sum8(do.astype(F32))
    for j in range(NG):
        acc["wout"][j] += dot(dot_t, sv["e"][j, 0:rows, :])
        de = dot_nt(do, wout_ref[j * CW : (j + 1) * CW, :])
        sv["dz"][j, 0:rows, :] = (de * sv["sh"][j].astype(F32)).astype(BF16)
        sv["ds"][j, 0:rows, :] = (de * sv["u"][j].astype(F32)).astype(BF16)
    gs = None
    for j in range(NG):
        part = dot_nt(sv["ds"][j, 0:rows, :], sv["q"][j, 0:rows, :])
        gs = part if gs is None else gs + part
    acc["sp"][...] += gs
    m1 = jnp.zeros((rows, 1), F32)
    m2 = jnp.zeros((rows, 1), F32)
    for j in range(NG):
        lo = j * CW
        dq = jnp.where(valid, dot(st_ref[...], sv["ds"][j, 0:rows, :]), 0.0)
        sv["dq"][j, 0:rows, :] = dq
        gain = vec_ref[:, O_LN2G + lo : O_LN2G + lo + CW]
        w = dq * sv["v"][j].astype(F32)
        gvec[:, O_LN2G + lo : O_LN2G + lo + CW] += rows_sum8(w)
        gvec[:, O_LN2S + lo : O_LN2S + lo + CW] += rows_sum8(dq)
        m1 = m1 + jnp.sum(dq * gain, axis=1, keepdims=True)
        m2 = m2 + jnp.sum(w * gain, axis=1, keepdims=True)
    m1 = m1 * (1.0 / G)
    m2 = m2 * (1.0 / G)
    for j in range(NG):
        lo = j * CW
        gain = vec_ref[:, O_LN2G + lo : O_LN2G + lo + CW]
        dv = (sv["dq"][j, 0:rows, :] * gain - m1 - sv["v"][j].astype(F32) * m2)
        sv["dz"][NG + j, 0:rows, :] = (dv * sv["hv"][j].astype(F32)).astype(BF16)
    da = None
    for j in range(NH):
        dz = sv["dz"][j, 0:rows, :]
        acc["win"][j] += dot(sv["at"][0:D, 0:rows], dz)
        gvec[:, O_INB + j * CW : O_INB + (j + 1) * CW] += rows_sum8(dz.astype(F32))
        part = dot_nt(dz, win_ref[j])
        da = part if da is None else da + part
    xh = sv["xh1"][0:rows, :]
    gain = vec_ref[:, O_LN1G : O_LN1G + D]
    w = da * xh
    gvec[:, O_LN1G : O_LN1G + D] += rows_sum8(w)
    gvec[:, O_LN1S : O_LN1S + D] += rows_sum8(da)
    t = da * gain
    mt = jnp.mean(t, axis=1, keepdims=True)
    mx = jnp.mean(w * gain, axis=1, keepdims=True)
    return dn + k * (t - mt - xh * mx)


def gather_grads(lay, acc, wout_ref, frames_ref):
    for j in range(NG):
        wout_ref[j * CW : (j + 1) * CW, :] = jnp.transpose(acc["wout"][j]).astype(BF16)
    whole = acc["sp"][...]
    row = lax.broadcasted_iota(jnp.int32, (RMAX, RMAX), 0)
    col = lax.broadcasted_iota(jnp.int32, (RMAX, RMAX), 1)
    ext = jnp.where(row == P_SIZE, jnp.transpose(whole), jnp.where(row < P_SIZE, whole, 0.0))
    ext = jnp.where(col < P_SIZE, ext, 0.0).astype(BF16)
    sums = jnp.sum(acc["vec"][...], axis=0, keepdims=True)
    vec = jnp.concatenate([sums[:, r * 128 : (r + 1) * 128] for r in range(VROWS)] + [jnp.zeros((VPAD - VROWS, 128), F32)], axis=0)
    count = lay.count * lay.small
    ms = picker(lay, RMAX, count, 0, lay.sp_rows, lay.sp_shard, P_SIZE)
    mv = picker(lay, VPAD, count, lay.sp_rows, lay.vec_rows, lay.vec_shard, 128)
    tn = (((0,), (0,)), ((), ()))
    frames_ref[...] = jnp.zeros(frames_ref.shape, BF16)
    frames_ref[:, 0:RMAX] = lax.dot_general(ms, ext, tn, preferred_element_type=F32).astype(BF16)
    part = lax.dot_general(mv, vec.astype(BF16), tn, preferred_element_type=F32)
    frames_ref[:, 0:128] += part.astype(BF16)


def scatter_grads(lay, me, acc, wout_ref, frames_ref, out):
    for who, second, place, role, i in role_blocks(lay, me, 1):
        dst = out["t%d%d" % (who, second)]
        for t in range(2):
            dst[place + (slice(16 * t, 16 * t + 16),)] = acc["win"][2 * role + t, sixteen(i * 16), :].astype(BF16)
        dst[place + (slice(32, 48),)] = wout_ref[sixteen(i * 48 + 16 * role), :]
    for who, z, place, i in both_blocks(lay, me, 1):
        dst = out["b%d%d" % (who, z)]
        for t in range(2):
            dst[place + (slice(16 * t, 16 * t + 16),)] = acc["win"][4 + t, sixteen(i * 16), :].astype(BF16)
        dst[place + (slice(32, 48),)] = wout_ref[sixteen(i * 48 + 32), :]
        dst[place + (slice(48, 64),)] = frames_ref[sixteen(i * 16), :]


def read_me(info_ref, images):
    return {axis: info_ref[images + k] for k, axis in enumerate(("core", "x", "z", "y"))}


class Names:
    def __init__(self, refs):
        self.refs = list(refs)

    def take(self, names):
        got = dict(zip(names, self.refs))
        self.refs = self.refs[len(names) :]
        return got


WEIGHTS = ("win", "wout", "frames")
SAVED = ("u", "sh", "v", "hv", "q", "e")


def kernel_body(lay, images, mode, scratch_names, info_ref, *refs):
    names = Names(refs)
    given = names.take(weight_names(lay))
    r_ref = names.take(["r"])["r"]
    saved = names.take(SAVED) if mode == "back" else {}
    dn_ref = names.take(["dn"])["dn"] if mode != "fore" else None
    out_ref = names.take(["out"])["out"] if mode != "back" else None
    if mode == "fore":
        saved = names.take(SAVED)
    gr_ref = names.take(["gr"])["gr"] if mode != "fore" else None
    grad_refs = names.take(grad_names(lay)) if mode != "fore" else {}
    sv = names.take(scratch_names)
    w = sv if lay.native else given
    sv.update({k: saved[k].at[0] for k in saved})
    if mode == "both":
        sv.update(u=sv["h"], sh=sv["hp"], v=sv["h"].at[NG:NH], hv=sv["hp"].at[NG:NH])
    acc = {k: sv.get("a" + k) for k in ("win", "wout", "sp", "vec")}
    b = pl.program_id(0)

    @pl.when(b == 0)
    def _():
        if lay.native:
            assemble(lay, read_me(info_ref, images), given, w["win"], w["wout"], w["frames"])
        unpack_small(lay, w["frames"], sv["vec"], sv["sc"], sv.get("st"))
        if mode != "fore":
            for ref in acc.values():
                ref[...] = jnp.zeros(ref.shape, F32)

    cls = info_ref[b]
    n = jnp.where(cls == 0, COUNTS[0], jnp.where(cls == 1, COUNTS[1], COUNTS[2]))
    valid = lax.broadcasted_iota(jnp.int32, (RMAX, 1), 0) < n
    if mode == "back":
        _, k, xh, a = first_norm(RMAX, valid, r_ref, sv["vec"])
        norm = (k, xh, a)
    else:
        norm, o = forward_part(RMAX, valid, r_ref, sv["vec"], w["win"], w["wout"], sv["sc"], sv, mode == "fore")
        out_ref[0] = o
    if mode != "fore":
        gr_ref[0] = backward_part(RMAX, valid, norm, dn_ref, sv["vec"], w["win"], w["wout"], sv["st"], sv, acc)

        @pl.when(b == pl.num_programs(0) - 1)
        def _():
            if lay.native:
                gather_grads(lay, acc, w["wout"], w["frames"])
                scatter_grads(lay, read_me(info_ref, images), acc, w["wout"], w["frames"], grad_refs)
            else:
                gather_grads(lay, acc, grad_refs["gwout"], grad_refs["gframes"])
                grad_refs["gwin"][...] = acc["win"][...].astype(BF16)


def piece_shape(lay, piece):
    return ((2, 2, 2, 2) if piece[0] == "t" else (2, 2, 2)) + (lay.part_rows("a" if piece[0] == "t" else "b"), CW)


def scratch_for(lay, mode):
    big = lambda m, dt: pltpu.VMEM((m, RMAX, CW), dt)
    wide = lambda dt: pltpu.VMEM((RMAX, D), dt)
    made = {}
    if lay.native:
        made.update(win=pltpu.VMEM((NH, D, CW), BF16), wout=pltpu.VMEM((G, D), BF16), frames=pltpu.VMEM((lay.count * lay.small, CW), BF16))
    made.update(vec=pltpu.VMEM((1, VUSED), F32), sc=pltpu.VMEM((RMAX, RMAX), BF16))
    if mode != "back":
        made.update(h=big(NH, F32), hp=big(NH, F32))
    if mode == "both":
        made.update(q=big(NG, BF16), e=big(NG, BF16))
    if mode != "fore":
        made.update(st=pltpu.VMEM((RMAX, RMAX), BF16), ds=big(NG, BF16), dz=big(NH, BF16), dq=big(NG, F32), xh1=wide(F32))
        made.update(at=pltpu.VMEM((D, RMAX), BF16), awin=pltpu.VMEM((NH, D, CW), F32), awout=pltpu.VMEM((NG, D, CW), F32))
        made.update(asp=pltpu.VMEM((RMAX, RMAX), F32), avec=pltpu.VMEM((8, VUSED), F32))
    return made


def weight_names(lay):
    if not lay.native:
        return list(WEIGHTS)
    return list(PIECES)


def grad_names(lay):
    return list(PIECES) if lay.native else ["gwin", "gwout", "gframes"]


def image_spec():
    return pl.BlockSpec((1, RMAX, D), lambda b, c: (b, 0, 0))


def saved_shapes(images):
    return [jax.ShapeDtypeStruct((images, NG, RMAX, CW), BF16) for _ in SAVED]


def saved_specs():
    spec = pl.BlockSpec((1, NG, RMAX, CW), lambda b, c: (b, 0, 0, 0))
    return [spec] * len(SAVED)


def run_kernel(lay, mode, info, weights, r, saved=None, dn=None):
    images = r.shape[0]
    image = jax.ShapeDtypeStruct((images, RMAX, D), F32)
    whole = pl.BlockSpec(memory_space=pltpu.VMEM)
    operands = list(weights) + [r]
    if lay.native and mode in KEPT:
        operands = [pltpu.with_memory_space_constraint(w, pltpu.VMEM) for w in weights] + [r]
    in_specs = [whole] * len(weights) + [image_spec()]
    outs, out_specs = [], []
    if mode == "back":
        operands += list(saved)
        in_specs += saved_specs()
    if mode != "fore":
        operands.append(dn)
        in_specs.append(image_spec())
    if mode != "back":
        outs.append(image)
        out_specs.append(image_spec())
    if mode == "fore":
        outs += saved_shapes(images)
        out_specs += saved_specs()
    if mode != "fore":
        outs.append(image)
        out_specs.append(image_spec())
        if lay.native:
            grads = [piece_shape(lay, p) for p in PIECES]
        else:
            grads = [(NH, D, CW), (G, D), (lay.count * lay.small, CW)]
        outs += [pltpu.VMEM(s, BF16) if lay.native else jax.ShapeDtypeStruct(s, BF16) for s in grads]
        out_specs += [whole] * len(grads)
    scratch = scratch_for(lay, mode)
    return pl.pallas_call(
        functools.partial(kernel_body, lay, images, mode, list(scratch)),
        grid_spec=pltpu.PrefetchScalarGridSpec(
            num_scalar_prefetch=1, grid=(images,), in_specs=in_specs, out_specs=out_specs, scratch_shapes=list(scratch.values())
        ),
        out_shape=outs,
        compiler_params=pltpu.CompilerParams(vmem_limit_bytes=VLIM[mode if lay.native else "plain"]),
        name="layer_" + mode,
    )(info, *operands)


def pack_large(lay, w_in, w_out):
    win = w_in.reshape(lay.rows, NH, CW)
    wout = w_out.reshape(NG, lay.rows, D)
    return [win[:, j] for j in range(NH)] + [wout[k] for k in range(NG)]


def pack_small(lay, spatial, vectors, me):
    index = lay.index(me)
    sp_at = lax.rem(index * lay.sp_shard, P_SIZE)
    vec_at = lax.rem(index * lay.vec_shard, 128)
    sp = lax.dynamic_update_slice(jnp.zeros((lay.sp_rows * P_SIZE,), BF16), spatial, (sp_at,)).reshape(lay.sp_rows, P_SIZE)
    vec = lax.dynamic_update_slice(jnp.zeros((lay.vec_rows * 128,), BF16), vectors, (vec_at,)).reshape(lay.vec_rows, 128)
    sp = jnp.pad(sp, ((0, 0), (0, CW - P_SIZE)))
    vec = jnp.pad(vec, ((0, lay.small - lay.sp_rows - lay.vec_rows), (0, CW - 128)))
    return jnp.concatenate([sp, vec])


def part_of(fields, part):
    return jnp.concatenate([fields[f] for f in PART_FIELDS[part]])


def ring_gather(lay, value, axis):
    pieces = [value]
    for _ in range(lay.size[axis] - 1):
        pieces.append(lay.shift(pieces[-1], axis))
    return pieces


def hold(*values):
    return lax.optimization_barrier(values)


def move(lay, *items, join=False):
    values = hold(*[value for value, _ in items])
    items = [(value, flips) for value, (_, flips) in zip(values, items)]
    return hold(*(together(lay, *items) if join else [lay.exchange(value, *flips) for value, flips in items]))


def together(lay, *items):
    got = {}
    for k, (_, flips) in enumerate(items):
        same = [i for i, (_, f) in enumerate(items) if f == flips]
        if same[0] != k:
            continue
        if len(same) == 1:
            got[k] = lay.exchange(items[k][0], *flips)
            continue
        flat = [items[i][0].reshape(-1, CW) for i in same]
        joined, at = lay.exchange(jnp.concatenate(flat), *flips), 0
        for i, v in zip(same, flat):
            got[i] = joined[at : at + v.shape[0]].reshape(items[i][0].shape)
            at += v.shape[0]
    return [got[k] for k in range(len(items))]


def gather_start(lay, packed, me):
    even = me["core"] == 0
    keep = jnp.where(even, packed["a"], packed["d"])
    give = jnp.where(even, packed["d"], packed["a"])
    return jnp.stack([keep, lay.exchange(give, CORE)])


GATHER_T = ((FAR,), (NEAR,), FIRST, SECOND)
GATHER_B = (SECOND, (FAR,), FIRST, (NEAR,))


def gather_plain(lay, packed, me):
    win, wout, frames = [None] * NH, [None] * NG, None
    for p in PARTS:
        dims = ("core",) + PART_DIMS[p]
        value = packed[p]
        for axis in reversed(dims):
            value = jnp.stack(ring_gather(lay, value, axis))
        for k, axis in enumerate(dims):
            n = lay.size[axis]
            value = jnp.take(value, lax.rem(me[axis] - jnp.arange(n) + n, n), axis=k)
        order = [dims.index(a) for a in ("z", "x", "core", "y")]
        value = value.transpose(order + [4, 5]).reshape(lay.count, lay.part_rows(p), CW)
        for f, at in lay.offsets(p):
            if f < 6:
                win[f] = value[:, at : at + lay.rows].reshape(D, CW)
            elif f < 9:
                wout[f - 6] = value[:, at : at + lay.rows]
            else:
                frames = value[:, at : at + lay.small].reshape(lay.count * lay.small, CW)
    return [jnp.stack(win), jnp.stack(wout, axis=1).reshape(G, D), frames]


def ring_scatter(lay, value, axis):
    n = lay.size[axis]
    total = value[n - 1].astype(F32)
    for k in range(n - 2, -1, -1):
        total = lay.shift(total.astype(BF16), axis).astype(F32) + value[k].astype(F32)
    return total


def low(v):
    return v.astype(BF16)


def add(mine, got):
    return mine.astype(F32) + got.astype(F32)


def scatter_core(lay, grads):
    t00, t01, t10, t11, b00, b01, b10, b11 = grads
    t11, b11 = hold(t11, b11)
    far = low(add(t01, lay.exchange(t11, CORE)))
    bfar = low(add(b01, lay.exchange(b11, CORE)))
    t10, _ = hold(t10, far)
    b10, _ = hold(b10, bfar)
    return far, bfar, (t00, lay.exchange(t10, CORE)), (b00, lay.exchange(b10, CORE))


SCATTER_T = (SECOND, FIRST, (NEAR,), (FAR,))
SCATTER_B = ((NEAR,), FIRST, (FAR,), SECOND)


def part_fields(lay, part, rows):
    return {f: rows[at : at + (lay.small if f == 9 else lay.rows)] for f, at in lay.offsets(part)}


def end_fields(lay, me, top, other):
    even = me["core"] == 0
    a, d = jnp.where(even, top[0], other), jnp.where(even, other, top[0])
    return {**part_fields(lay, "a", a), **part_fields(lay, "d", d)}


def join_large(lay, *layers):
    gwin = [jnp.stack([fields[j] for j in range(NH)], axis=1).reshape(-1) for fields in layers]
    gwout = [jnp.concatenate([fields[6 + k] for k in range(NG)]).reshape(-1) for fields in layers]
    return [jnp.stack(gwin), jnp.stack(gwout)]


def native_path(lay, me, size_class, params, patches, cotangent):
    stack = lambda v, got: jnp.stack([v, got])
    info = size_class
    w_in, w_out, spatial, vectors = params
    large = pack_large(lay, w_in[0], w_out[0])
    t0 = gather_start(lay, {p: part_of(large, p) for p in "ad"}, me)
    t0, spatial, vectors, w_in, w_out = hold(t0, spatial, vectors, w_in, w_out)
    x = lay.exchange(t0, *GATHER_T[0])
    b0 = part_of(large + [pack_small(lay, spatial[0], vectors[0], me)], "b")
    y = lay.exchange(b0, *GATHER_B[0])
    x, y, w_in, w_out, spatial, vectors = hold(x, y, w_in, w_out, spatial, vectors)
    large = pack_large(lay, w_in[1], w_out[1])
    t1 = gather_start(lay, {p: part_of(large, p) for p in "ad"}, me)
    b1 = part_of(large + [pack_small(lay, spatial[1], vectors[1], me)], "b")
    t0, b0, patches, cotangent, info = hold(stack(t0, x), stack(b0, y), patches, cotangent, info)
    for k in (1, 2):
        x, y = lay.exchange(t0, *GATHER_T[k]), lay.exchange(b0, *GATHER_B[k])
        u, v = lay.exchange(t1, *GATHER_T[k - 1]), lay.exchange(b1, *GATHER_B[k - 1])
        if k == 1:
            info, patches, cotangent = describe(me, info), spread(patches), spread(cotangent)
        x, y, u, v, patches, cotangent, info = hold(x, y, u, v, patches, cotangent, info)
        t0, b0, t1, b1 = hold(stack(t0, x), stack(b0, y), stack(t1, u), stack(b1, v))
    t0c, b0c = lay.exchange(t0, CORE), lay.exchange(b0, CORE)
    x, y, u, v = [lay.exchange(g, *f) for g, f in ((t0, GATHER_T[3]), (b0, GATHER_B[3]), (t1, GATHER_T[2]), (b1, GATHER_B[2]))]
    x, u, v = hold(x, u, v)
    weights0 = [t0, x, t0c, lay.exchange(x, CORE), b0, y, b0c, lay.exchange(y, CORE)]
    t1, b1 = stack(t1, u), stack(b1, v)
    x, y, t1c, b1c = [lay.exchange(v, *f) for v, f in ((t1, SECOND), (b1, (NEAR,)), (t1, (CORE,)), (b1, (CORE,)))]
    hidden, *saved = run_kernel(lay, "fore", info, weights0, patches)
    x, y, t1c, b1c, hidden = hold(x, y, t1c, b1c, hidden)
    weights1 = [t1, x, t1c, lay.exchange(x, CORE), b1, y, b1c, lay.exchange(y, CORE)]
    outputs, grad, *grads1 = run_kernel(lay, "both", info, weights1, hidden, dn=cotangent)

    far1, bfar1, near1, bnear1 = scatter_core(lay, grads1)
    x, y = lay.exchange(far1, *SECOND), lay.exchange(bfar1, NEAR)
    _, _, grad = hold(far1, bfar1, grad)
    patch_grad, *grads0 = run_kernel(lay, "back", info, weights0, patches, saved=saved, dn=grad)
    x, y, patch_grad, outputs, *grads0 = hold(x, y, patch_grad, outputs, *grads0)
    top1, b1 = add(add(*near1), x), add(add(*bnear1), y)
    u, v = lay.exchange(low(top1[1]), *SCATTER_T[1]), lay.exchange(low(b1[1]), *SCATTER_B[1])
    far0, bfar0, near0, bnear0 = scatter_core(lay, grads0)
    far0, bfar0, outputs, patch_grad = hold(far0, bfar0, outputs, patch_grad)
    x, y = lay.exchange(far0, *SECOND), lay.exchange(bfar0, NEAR)
    x, y, u, v, outputs, patch_grad = hold(x, y, u, v, tilt(outputs), tilt(patch_grad))
    top1, b1 = add(top1[0], u), add(b1[0], v)
    top0, b0 = add(add(*near0), x), add(add(*bnear0), y)
    for k in (1, 2):
        sends = [(low(v[1]), f) for v, f in ((top0, SCATTER_T[k]), (b0, SCATTER_B[k]), (top1, SCATTER_T[k + 1]), (b1, SCATTER_B[k + 1]))]
        x, y, u, v = move(lay, *sends, join=True)
        top0, b0, top1, b1 = add(top0[0], x), add(b0[0], y), add(top1[0], u), add(b1[0], v)
    send, send_b = hold(low(top0[1]), low(b0[1]))
    x, last1 = lay.exchange(send, *SCATTER_T[3]), lay.exchange(top1[1], CORE)
    send_b, last1 = hold(send_b, last1)
    y = lay.exchange(send_b, *SCATTER_B[3])
    b0 = add(b0[0], y)
    fields0, fields1 = part_fields(lay, "b", b0), part_fields(lay, "b", b1)
    small = [jnp.stack(v) for v in zip(*[unpack_small_grads(lay, f[9], me) for f in (fields0, fields1)])]
    fields1.update(end_fields(lay, me, top1, last1))
    x, *small = hold(x, *small)
    top0 = add(top0[0], x)
    fields0.update(end_fields(lay, me, top0, lay.exchange(top0[1], CORE)))
    outputs, patch_grad = outputs.transpose(1, 0, 2), patch_grad.transpose(1, 0, 2)
    return [outputs, patch_grad] + join_large(lay, fields0, fields1) + small


def tilt(v):
    return v[:, :P_SIZE].transpose(1, 0, 2)


def describe(me, size_class):
    return jnp.concatenate([size_class, jnp.stack([me[a] for a in ("core", "x", "z", "y")]).astype(jnp.int32)])


def spread(v):
    return jnp.pad(v, ((0, 0), (0, RMAX - P_SIZE), (0, 0)))


def plain_path(lay, me, size_class, params, patches, cotangent):
    packed = []
    for w_in, w_out, spatial, vectors in zip(*params):
        fields = pack_large(lay, w_in, w_out) + [pack_small(lay, spatial, vectors, me)]
        packed.append({p: part_of(fields, p) for p in PARTS})
    info, patches, cotangent = describe(me, size_class), spread(patches), spread(cotangent)
    weights0, weights1 = [gather_plain(lay, p, me) for p in packed]
    hidden, *saved = run_kernel(lay, "fore", info, weights0, patches)
    outputs, grad, *grads1 = run_kernel(lay, "both", info, weights1, hidden, dn=cotangent)
    patch_grad, *grads0 = run_kernel(lay, "back", info, weights0, patches, saved=saved, dn=grad)
    outputs, patch_grad = outputs[:, :P_SIZE], patch_grad[:, :P_SIZE]
    layers = []
    for grads in (grads0, grads1):
        sums = scatter_plain(lay, grads, me)
        layers.append({f: v for p in PARTS for f, v in part_fields(lay, p, sums[p]).items()})
    small = [jnp.stack(v) for v in zip(*[unpack_small_grads(lay, f[9], me) for f in layers])]
    return [outputs, patch_grad] + join_large(lay, *layers) + small


def scatter_plain(lay, grads, me):
    gwin, gwout, gframes = grads
    gwin = gwin.reshape(NH, lay.count, lay.rows, CW)
    gwout = gwout.reshape(lay.count, NG, lay.rows, D)
    gframes = gframes.reshape(lay.count, lay.small, CW)
    fields = [gwin[j] for j in range(NH)] + [gwout[:, k] for k in range(NG)] + [gframes]
    result = {}
    for p in PARTS:
        dims = ("core",) + PART_DIMS[p]
        value = jnp.concatenate([fields[f] for f in PART_FIELDS[p]], axis=1)
        value = value.reshape(lay.size["z"], 2, 2, lay.size["y"], lay.part_rows(p), CW)
        value = value.transpose([("z", "x", "core", "y").index(a) for a in dims] + [4, 5])
        for k, axis in enumerate(dims):
            n = lay.size[axis]
            value = jnp.take(value, lax.rem(me[axis] + jnp.arange(n), n), axis=k)
        for axis in dims:
            value = ring_scatter(lay, value, axis)
        result[p] = value
    return result


def unpack_small_grads(lay, rows, me):
    index = lay.index(me)
    sp = rows[0 : lay.sp_rows, 0:P_SIZE].reshape(-1)
    sp = lax.dynamic_slice(sp, (lax.rem(index * lay.sp_shard, P_SIZE),), (lay.sp_shard,))
    vec = rows[lay.sp_rows : lay.sp_rows + lay.vec_rows, 0:128].reshape(-1)
    return sp, lax.dynamic_slice(vec, (lax.rem(index * lay.vec_shard, 128),), (lay.vec_shard,))


def per_device(mesh_shape, patches, cotangent, size_class, w_in, w_out, spatial, vectors):
    lay = Layout(mesh_shape, spatial.shape[1], vectors.shape[1])
    wide, narrow = lax.axis_index("wide"), lax.axis_index("narrow")
    me = {"core": lax.rem(wide, 2), "x": lax.rem(wide // 2, 2), "z": wide // 4, "y": narrow}
    params = w_in, w_out, spatial, vectors
    path = native_path if lay.native else plain_path
    return tuple(path(lay, me, size_class, params, patches, cotangent))


def solution(mesh):
    shape = (mesh.shape["wide"], mesh.shape["narrow"])
    rows = P(AXES, None, None)
    flat = P(None, AXES)
    return jax.shard_map(
        functools.partial(per_device, shape),
        mesh=mesh,
        in_specs=(rows, rows, P(AXES), flat, flat, flat, flat),
        out_specs=(rows, rows, flat, flat, flat, flat),
        check_vma=False,
    )
```
